32 devices in a mesh: dp: 8 (over y, x, core), tensor: 4 (over z).
Axes of the slice: x: 2, y: 2, z: 4, core: 2. Of those that a mesh axis runs over, the one named last changes fastest.
Arguments:
- tokens: bfloat16 [8, 1024, 1024], P('dp', 'tensor'), may hold values from -6 to 6
- segment_ids: int32 [8, 1024], P('dp'), may hold values from 0 to 7, as said below
- norm1_gain: float32 [1024], replicated, may hold values from 0.25 to 1.75
- norm1_bias: float32 [1024], replicated, may hold values from -1.75 to 1.75
- proj_weight: bfloat16 [1024, 3, 1024], P(None, None, 'tensor'), may hold values from -0.1875 to 0.1875
- proj_bias: float32 [3, 1024], P(None, 'tensor'), may hold values from -1.75 to 1.75
- short_weight: float32 [3, 3, 1024], P(None, None, 'tensor'), may hold values from -3.5 to 3.5
- short_bias: float32 [3, 1024], P(None, 'tensor'), may hold values from -1.75 to 1.75
- embed_weight: float32 [33, 64], replicated, may hold values from -1 to 1
- embed_bias: float32 [64], replicated, may hold values from -3 to 3
- sine_freq: float32 [3, 64], replicated, may hold values from 0.5 to 2
- inner_weight: float32 [2, 64, 64], replicated, may hold values from -0.75 to 0.75
- inner_bias: float32 [2, 64], replicated, may hold values from -3 to 3
- filter_weight: float32 [64, 1024], P(None, 'tensor'), may hold values from -0.09375 to 0.09375
- decay_rate: float32 [1024], P('tensor'), may hold values from 0.5 to 64
- skip_gain: float32 [1024], P('tensor'), may hold values from -6 to 6
- out_weight: bfloat16 [1024, 1024], P('tensor'), may hold values from -0.1875 to 0.1875
- out_bias: float32 [1024], replicated, may hold values from -1.75 to 1.75
- norm2_gain: float32 [1024], replicated, may hold values from 0.25 to 1.75
- norm2_bias: float32 [1024], replicated, may hold values from -1.75 to 1.75
- up_weight: bfloat16 [1024, 4096], P(None, 'tensor'), may hold values from -0.1875 to 0.1875
- up_bias: float32 [4096], P('tensor'), may hold values from -1.75 to 1.75
- down_weight: bfloat16 [4096, 1024], P('tensor'), may hold values from -0.1875 to 0.1875
- down_bias: float32 [1024], replicated, may hold values from -1.75 to 1.75
- cotangent: bfloat16 [8, 1024, 1024], P('dp', 'tensor'), may hold values from -6 to 6
Outputs:
- layer_out: bfloat16 [8, 1024, 1024], P('dp', 'tensor')
- grad_tokens: float32 [8, 1024, 1024], P('dp', 'tensor')
- grad_norm1_gain: float32 [1024], replicated
- grad_norm1_bias: float32 [1024], replicated
- grad_proj_weight: float32 [1024, 3, 1024], P(None, None, 'tensor')
- grad_proj_bias: float32 [3, 1024], P(None, 'tensor')
- grad_short_weight: float32 [3, 3, 1024], P(None, None, 'tensor')
- grad_short_bias: float32 [3, 1024], P(None, 'tensor')
- grad_embed_weight: float32 [33, 64], replicated
- grad_embed_bias: float32 [64], replicated
- grad_sine_freq: float32 [3, 64], replicated
- grad_inner_weight: float32 [2, 64, 64], replicated
- grad_inner_bias: float32 [2, 64], replicated
- grad_filter_weight: float32 [64, 1024], P(None, 'tensor')
- grad_skip_gain: float32 [1024], P('tensor')
- grad_out_weight: float32 [1024, 1024], P('tensor')
- grad_out_bias: float32 [1024], replicated
- grad_norm2_gain: float32 [1024], replicated
- grad_norm2_bias: float32 [1024], replicated
- grad_up_weight: float32 [1024, 4096], P(None, 'tensor')
- grad_up_bias: float32 [4096], P('tensor')
- grad_down_weight: float32 [4096, 1024], P('tensor')
- grad_down_bias: float32 [1024], replicated
The draws below stay inside these ranges and needn't reach their ends.
Inputs may be any that keep to these rules, and one draw needn't show every extreme that they name: Within a row segment_ids never fall, start at 0 and rise by one at each of 7 document boundaries, so every document is non-empty. Every boundary lies within the first 256 or the last 256 positions of its row, so the document at position 255 covers all positions from 255 to 768, and every other document lies within the first or the last 256 positions.
All inputs are finite; a program needn't handle non-finite values.
Results may differ from the reference program's by a relative error of at most 0.015.
Values may be sent and summed in bfloat16 or wider, within the bound.
A program may use at most 384 MiB of HBM per device.

```python
import math
import jax
import jax.numpy as jnp
from jax import lax

D = 1024
FF = 4096
FWIDTH = 64
FEAT = 33
SEQ = 1024
NDOC = 8
ROWS = 8
SHARD = 256


def draw_segment_ids(key, part):
    key = jax.random.fold_in(key, 7)

    def one_row(row_key):
        key_early, key_late, key_split = jax.random.split(row_key, 3)
        early = jnp.sort(jax.random.permutation(key_early, SHARD - 1)[:NDOC - 1]) + 1
        late = jnp.sort(jax.random.permutation(key_late, SHARD - 1)[:NDOC - 1]) + SEQ - SHARD + 1
        split_at = jax.random.randint(key_split, (), 0, NDOC)
        bounds = jnp.where(jnp.arange(NDOC - 1) < split_at, early, late)
        places = jnp.arange(SEQ)
        return jnp.sum((places[:, None] >= bounds[None, :]).astype(jnp.int32), axis=1, dtype=jnp.int32)
    return jax.vmap(one_row)(jax.random.split(key, ROWS)).astype(jnp.int32)


def block_levels(own_key, shape, shards, smallest, top_value):
    def one(dim, shards_of):
        steps = jax.random.uniform(jax.random.fold_in(jax.random.fold_in(own_key, 6), dim), (shards_of,), jnp.float32, smallest / len(shards), top_value / len(shards))
        return jnp.repeat(jnp.exp(steps), shape[dim] // shards_of).reshape((-1,) + (1,) * (len(shape) - dim - 1))

    gain = one(*shards[0])
    for cut in shards[1:]:
        gain = gain * one(*cut)
    return gain


def scatter_about(stream_key, shape, deviation, most, pieces=(), kind=jnp.bfloat16):
    loudness = block_levels(stream_key, shape, pieces, -0.22, 0.18) if pieces else 1.0
    entries = jax.random.normal(stream_key, shape, jnp.float32) * deviation * loudness
    return jnp.minimum(jnp.maximum(entries, -most), most).astype(kind)


def setup_inputs(seed: int = 0) -> dict:
    seeds = jax.random.split(jax.random.key(seed), 26)
    tokens = scatter_about(seeds[0], (ROWS, SEQ, D), 1.0, 6.0, ((0, 8), (1, 4)))
    segment_ids = draw_segment_ids(jax.random.fold_in(seeds[25], 71), 0)
    norm1_gain = jnp.clip(1.0 + 0.15 * jax.random.normal(seeds[2], (D,), jnp.float32), 0.25, 1.75)
    norm1_bias = scatter_about(seeds[3], (D,), 0.3, 1.75, (), jnp.float32)
    proj_weight = scatter_about(seeds[4], (D, 3, D), D ** -0.5, 0.1875, ((2, 4),))
    proj_bias = scatter_about(seeds[5], (3, D), 0.3, 1.75, ((1, 4),), jnp.float32)
    short_weight = scatter_about(seeds[6], (3, 3, D), 3 ** -0.5, 3.5, ((2, 4),), jnp.float32)
    short_bias = scatter_about(seeds[7], (3, D), 0.3, 1.75, ((1, 4),), jnp.float32)
    embed_weight = scatter_about(seeds[8], (FEAT, FWIDTH), FEAT ** -0.5, 1.0, (), jnp.float32)
    embed_bias = scatter_about(seeds[9], (FWIDTH,), 0.5, 3.0, (), jnp.float32)
    sine_freq = jnp.clip(jnp.exp(jax.random.uniform(seeds[10], (3, FWIDTH), jnp.float32, math.log(0.5), math.log(2.0))), 0.5, 2.0)
    inner_weight = scatter_about(seeds[11], (2, FWIDTH, FWIDTH), FWIDTH ** -0.5, 0.75, (), jnp.float32)
    inner_bias = scatter_about(seeds[12], (2, FWIDTH), 0.5, 3.0, (), jnp.float32)
    filter_weight = scatter_about(seeds[13], (FWIDTH, D), (64 * FWIDTH) ** -0.5, 0.09375, ((1, 4),), jnp.float32)
    decay_rate = jnp.clip(jnp.exp(math.log(64.0) - 4.8520303 * jax.random.uniform(seeds[14], (D,), jnp.float32) ** block_levels(seeds[14], (D,), ((0, 4),), -0.2, 0.2)), 0.5, 64.0)
    skip_gain = scatter_about(seeds[15], (D,), 1.0, 6.0, ((0, 4),), jnp.float32)
    out_weight = scatter_about(seeds[16], (D, D), D ** -0.5, 0.1875, ((0, 4),))
    out_bias = scatter_about(seeds[17], (D,), 0.3, 1.75, (), jnp.float32)
    norm2_gain = jnp.clip(1.0 + 0.15 * jax.random.normal(seeds[18], (D,), jnp.float32), 0.25, 1.75)
    norm2_bias = scatter_about(seeds[19], (D,), 0.3, 1.75, (), jnp.float32)
    up_weight = scatter_about(seeds[20], (D, FF), D ** -0.5, 0.1875, ((1, 4),))
    up_bias = scatter_about(seeds[21], (FF,), 0.3, 1.75, ((0, 4),), jnp.float32)
    down_weight = scatter_about(seeds[22], (FF, D), (FF // 4) ** -0.5, 0.1875, ((0, 4),))
    down_bias = scatter_about(seeds[23], (D,), 0.3, 1.75, (), jnp.float32)
    cotangent = scatter_about(seeds[24], (ROWS, SEQ, D), 1.0, 6.0, ((0, 8), (1, 4)))
    return dict(tokens=tokens, segment_ids=segment_ids, norm1_gain=norm1_gain, norm1_bias=norm1_bias, proj_weight=proj_weight, proj_bias=proj_bias, short_weight=short_weight, short_bias=short_bias, embed_weight=embed_weight, embed_bias=embed_bias, sine_freq=sine_freq, inner_weight=inner_weight, inner_bias=inner_bias, filter_weight=filter_weight, decay_rate=decay_rate, skip_gain=skip_gain, out_weight=out_weight, out_bias=out_bias, norm2_gain=norm2_gain, norm2_bias=norm2_bias, up_weight=up_weight, up_bias=up_bias, down_weight=down_weight, down_bias=down_bias, cotangent=cotangent)


EPS = 1e-05
HIGH = lax.Precision.HIGHEST
SHIFT = 0.1

@jax.custom_vjp
def low(v):
    return lax.optimization_barrier(v.astype(jnp.bfloat16)).astype(jnp.float32)

@jax.custom_vjp
def low_back(v):
    return v

def low_keep(v):
    return (low(v), None)

def low_pass(kept, grad):
    return (grad,)

def back_keep(v):
    return (v, None)

def back_low(kept, grad):
    return (low(grad),)
low.defvjp(low_keep, low_pass)
low_back.defvjp(back_keep, back_low)

def layer_norm(values, norm_gain, norm_bias):
    average = lax.optimization_barrier(jnp.mean(values, axis=-1, keepdims=True))
    centered = values - average
    variance = lax.optimization_barrier(jnp.mean(centered * centered, axis=-1, keepdims=True))
    return centered * lax.rsqrt(variance + EPS) * norm_gain + norm_bias

def position_features():
    places = jnp.arange(SEQ, dtype=jnp.float32)
    band_index = jnp.arange(1, (FEAT - 1) // 2 + 1, dtype=jnp.float32)
    angles = 2.0 * jnp.pi * places[:, None] * band_index[None, :] / SEQ
    return jnp.concatenate([(places / (SEQ - 1))[:, None], jnp.cos(angles), jnp.sin(angles)], axis=1)

def make_filter(embed_weight, embed_bias, sine_freq, inner_weight, inner_bias, filter_weight, decay_rate):
    places = jnp.arange(SEQ, dtype=jnp.float32)
    hidden = jnp.sin(sine_freq[0] * (jnp.dot(position_features(), embed_weight, precision=HIGH) + embed_bias))
    for layer_index in range(2):
        hidden = jnp.sin(sine_freq[layer_index + 1] * (jnp.dot(hidden, inner_weight[layer_index], precision=HIGH) + inner_bias[layer_index]))
    filter_taps = jnp.dot(hidden, filter_weight, precision=HIGH)
    return filter_taps * (jnp.exp(-decay_rate[None, :] * places[:, None] / SEQ) + SHIFT)

def short_conv(values, segment, short_weight, short_bias):
    running = short_bias[None] + short_weight[0][None] * values
    for lag_index in range(1, 3):
        shifted = jnp.concatenate([jnp.zeros((lag_index,) + values.shape[1:], values.dtype), values[:SEQ - lag_index]], axis=0)
        same_doc = jnp.concatenate([jnp.zeros((lag_index,), values.dtype), (segment[lag_index:] == segment[:SEQ - lag_index]).astype(values.dtype)])
        running = running + short_weight[lag_index][None] * shifted * same_doc[:, None, None]
    return running

def long_conv(values, segment, filter_taps):
    documents = (segment[None, :] == jnp.arange(NDOC, dtype=jnp.int32)[:, None]).astype(values.dtype)
    masked = documents[:, :, None] * values[None]
    spectra = jnp.fft.rfft(masked, n=2 * SEQ, axis=1) * jnp.fft.rfft(filter_taps, n=2 * SEQ, axis=0)[None]
    result = jnp.fft.irfft(spectra, n=2 * SEQ, axis=1)[:, :SEQ]
    return lax.optimization_barrier(jnp.sum(documents[:, :, None] * result, axis=0))

def reference(tokens, segment_ids, norm1_gain, norm1_bias, proj_weight, proj_bias, short_weight, short_bias, embed_weight, embed_bias, sine_freq, inner_weight, inner_bias, filter_weight, decay_rate, skip_gain, out_weight, out_bias, norm2_gain, norm2_bias, up_weight, up_bias, down_weight, down_bias, cotangent):

    def forward(tokens_f, norm1_gain, norm1_bias, proj_weight, proj_bias, short_weight, short_bias, embed_weight, embed_bias, sine_freq, inner_weight, inner_bias, filter_weight, skip_gain, out_weight, out_bias, norm2_gain, norm2_bias, up_weight, up_bias, down_weight, down_bias):
        filter_taps = low(make_filter(embed_weight, embed_bias, sine_freq, inner_weight, inner_bias, filter_weight, decay_rate))

        def row_step(row_pair):
            row_tokens, segment = row_pair
            normed = low(layer_norm(row_tokens, norm1_gain, norm1_bias))
            projected = low_back(jnp.einsum('td,dkc->tkc', normed, proj_weight, precision=HIGH)) + proj_bias[None]
            mixed = short_conv(projected, segment, short_weight, short_bias)
            gate_out = mixed[:, 0]
            product = mixed[:, 2] * mixed[:, 1]
            convolved = low_back(long_conv(low(product), segment, filter_taps))
            gated = low((convolved + skip_gain[None] * product) * gate_out)
            residual = row_tokens + low_back(jnp.dot(gated, out_weight, precision=HIGH)) + out_bias[None]
            second = low(layer_norm(residual, norm2_gain, norm2_bias))
            hidden = low_back(jnp.dot(second, up_weight, precision=HIGH)) + up_bias[None]
            active = low(jax.nn.gelu(hidden, approximate=True))
            return residual + low_back(jnp.dot(active, down_weight, precision=HIGH)) + down_bias[None]
        return lax.map(jax.checkpoint(row_step), (tokens_f, segment_ids))
    params = (norm1_gain, norm1_bias, proj_weight.astype(jnp.float32), proj_bias, short_weight, short_bias, embed_weight, embed_bias, sine_freq, inner_weight, inner_bias, filter_weight, skip_gain, out_weight.astype(jnp.float32), out_bias, norm2_gain, norm2_bias, up_weight.astype(jnp.float32), up_bias, down_weight.astype(jnp.float32), down_bias)
    outputs, pullback = jax.vjp(forward, tokens.astype(jnp.float32), *params)
    grads = pullback(cotangent.astype(jnp.float32))
    return (outputs.astype(jnp.bfloat16), grads[0], grads[1], grads[2], grads[3], grads[4], grads[5], grads[6], grads[7], grads[8], grads[9], grads[10], grads[11], grads[12], grads[13], grads[14], grads[15], grads[16], grads[17], grads[18], grads[19], grads[20], grads[21])
```

```python
import jax
import jax.numpy as jnp
import ml_dtypes
import numpy as np
from jax import lax
from jax.sharding import PartitionSpec as P

FEAT = 33
SEQ = 1024
NDOC = 8


EPS = 1e-05
HIGH = lax.Precision.HIGHEST
SHIFT = 0.1


def layer_norm(values, norm_gain, norm_bias):
    average = jnp.mean(values, axis=-1, keepdims=True)
    centered = values - average
    variance = jnp.mean(centered * centered, axis=-1, keepdims=True)
    return centered * lax.rsqrt(variance + EPS) * norm_gain + norm_bias


def gelu_tanh(values):
    return jax.nn.gelu(values, approximate=True)


def position_features():
    places = jnp.arange(SEQ, dtype=jnp.float32)
    band_index = jnp.arange(1, (FEAT - 1) // 2 + 1, dtype=jnp.float32)
    angles = 2.0 * jnp.pi * places[:, None] * band_index[None, :] / SEQ
    return jnp.concatenate(
        [(places / (SEQ - 1))[:, None], jnp.cos(angles), jnp.sin(angles)], axis=1
    )


def make_filter(
    embed_weight, embed_bias, sine_freq, inner_weight, inner_bias, filter_weight, decay_rate
):
    places = jnp.arange(SEQ, dtype=jnp.float32)
    hidden = jnp.sin(
        sine_freq[0] * (jnp.dot(position_features(), embed_weight, precision=HIGH) + embed_bias)
    )
    for layer_index in range(2):
        hidden = jnp.sin(
            sine_freq[layer_index + 1]
            * (jnp.dot(hidden, inner_weight[layer_index], precision=HIGH) + inner_bias[layer_index])
        )
    filter_taps = jnp.dot(hidden, filter_weight, precision=HIGH)
    return filter_taps * (jnp.exp(-decay_rate[None, :] * places[:, None] / SEQ) + SHIFT)


def short_conv(values, segment, short_weight, short_bias):
    length = values.shape[1]
    running = short_bias[None, None] + short_weight[0][None, None] * values
    for lag_index in range(1, 3):
        shifted = jnp.concatenate(
            [jnp.zeros_like(values[:, :lag_index]), values[:, : length - lag_index]], axis=1
        )
        same_doc = jnp.concatenate(
            [
                jnp.zeros(segment[:, :lag_index].shape, jnp.float32),
                (segment[:, lag_index:] == segment[:, : length - lag_index]).astype(jnp.float32),
            ],
            axis=1,
        )
        running = (
            running + short_weight[lag_index][None, None] * shifted * same_doc[:, :, None, None]
        )
    return running


def dft_rows(length):
    span = 2 * length
    places = np.arange(length)
    turns = (np.arange(length)[:, None] * places[None, :]) % span
    angles = turns * (2.0 * np.pi / span)
    sines = -np.sin(angles)
    sines[0] = 1.0 - 2.0 * (places % 2)
    rows = np.concatenate([np.cos(angles), sines], axis=0).astype(np.float32)
    high = rows.astype(ml_dtypes.bfloat16)
    low = (rows - high.astype(np.float32)).astype(ml_dtypes.bfloat16)
    return jnp.asarray(high), jnp.asarray(low)


def to_spectrum(matrix, values_b):
    high, low = matrix
    return jnp.dot(high, values_b, preferred_element_type=jnp.float32) + jnp.dot(
        low, values_b, preferred_element_type=jnp.float32
    )


def from_spectrum(matrix, spectrum):
    high, low = matrix
    top = spectrum.astype(jnp.bfloat16)
    rest = (spectrum - top.astype(jnp.float32)).astype(jnp.bfloat16)

    def back(rows, values):
        return lax.dot_general(
            rows, values, (((0,), (0,)), ((), ())), preferred_element_type=jnp.float32
        )

    return back(high, top) + back(low, top) + back(high, rest)


def spectral_scale(length):
    weights = np.full((length, 1), 1.0 / length, np.float32)
    weights[0] = 0.5 / length
    return jnp.asarray(weights)


def halves(spectrum):
    length = spectrum.shape[0] // 2
    return spectrum[:length], spectrum[length:]


def spectral_product(left, right, conjugate):
    left_re, left_im = halves(left)
    right_re, right_im = halves(right)
    first = lax.broadcasted_iota(jnp.int32, (left_re.shape[0],) + (1,) * (left.ndim - 1), 0) == 0
    cross = left_im * right_im
    if conjugate:
        real = left_re * right_re + jnp.where(first, 0.0, cross)
        imag = jnp.where(first, cross, left_re * right_im - left_im * right_re)
    else:
        real = left_re * right_re - jnp.where(first, 0.0, cross)
        imag = jnp.where(first, cross, left_re * right_im + left_im * right_re)
    return real, imag


def scaled(parts, length):
    scale = spectral_scale(length)
    scale = scale.reshape((length,) + (1,) * (parts[0].ndim - 1))
    return jnp.concatenate([parts[0] * scale, parts[1] * scale], axis=0)


def document_masks(segment, main_doc):
    docs = jnp.arange(NDOC, dtype=jnp.int32)
    same = (segment[:, None] == docs[None, :]) & (docs[None, :] != main_doc)
    return same.astype(jnp.bfloat16)


def split_documents(values_b, masks):
    main_mask, head_masks, tail_masks = masks
    region = head_masks.shape[0]
    length = values_b.shape[0]
    main = values_b * main_mask[:, None]
    small = (
        head_masks[:, :, None] * values_b[:region, None, :]
        + tail_masks[:, :, None] * values_b[length - region :, None, :]
    )
    return main, small.reshape(region, -1)


def join_documents(main, small, masks):
    main_mask, head_masks, tail_masks = masks
    region = head_masks.shape[0]
    length, channels = main.shape
    small = small.reshape(region, NDOC, channels)
    head = jnp.sum(small * head_masks[:, :, None].astype(jnp.float32), axis=1)
    tail = jnp.sum(small * tail_masks[:, :, None].astype(jnp.float32), axis=1)
    middle = jnp.zeros((length - 2 * region, channels), main.dtype)
    return main * main_mask[:, None].astype(jnp.float32) + jnp.concatenate(
        [head, middle, tail], axis=0
    )


def row_masks(segment, shard_len):
    length = segment.shape[0]
    main_doc = segment[shard_len - 1]
    return (
        (segment == main_doc).astype(jnp.bfloat16),
        document_masks(segment[:shard_len], main_doc),
        document_masks(segment[length - shard_len :], main_doc),
    )


def spectra_of(values_b, masks, matrices):
    main, small = split_documents(values_b, masks)
    region = masks[1].shape[0]
    return (
        to_spectrum(matrices[0], main),
        to_spectrum(matrices[1], small).reshape(2 * region, NDOC, -1),
    )


def filter_row(spectra, taps_spectra, masks, matrices, conjugate):
    length = spectra[0].shape[0] // 2
    region = spectra[1].shape[0] // 2
    main = from_spectrum(
        matrices[0], scaled(spectral_product(taps_spectra[0], spectra[0], conjugate), length)
    )
    mixed = scaled(
        spectral_product(taps_spectra[1][:, None, :], spectra[1], conjugate), region
    )
    small = from_spectrum(matrices[1], mixed.reshape(2 * region, -1))
    return join_documents(main, small, masks)


def taps_gradient(value_spectra, grad_spectra, matrices):
    length = value_spectra[0].shape[0] // 2
    region = value_spectra[1].shape[0] // 2
    main = from_spectrum(
        matrices[0], scaled(spectral_product(value_spectra[0], grad_spectra[0], True), length)
    )
    real, imag = spectral_product(value_spectra[1], grad_spectra[1], True)
    small = from_spectrum(
        matrices[1], scaled((jnp.sum(real, axis=1), jnp.sum(imag, axis=1)), region)
    )
    return main.at[:region].add(small)


def body(
    tokens,
    segment_ids,
    norm1_gain,
    norm1_bias,
    proj_weight,
    proj_bias,
    short_weight,
    short_bias,
    embed_weight,
    embed_bias,
    sine_freq,
    inner_weight,
    inner_bias,
    filter_weight,
    decay_rate,
    skip_gain,
    out_weight,
    out_bias,
    norm2_gain,
    norm2_bias,
    up_weight,
    up_bias,
    down_weight,
    down_bias,
    cotangent,
):
    row_count, shard_len, model_width = tokens.shape
    groups = lax.axis_size("tensor")
    length = shard_len * groups
    channels = proj_weight.shape[2]
    flat_rows = row_count * length
    tokens_f = tokens.astype(jnp.float32)
    normed1, norm1_back = jax.vjp(layer_norm, tokens_f, norm1_gain, norm1_bias)
    first_rows = lax.all_gather(normed1.astype(jnp.bfloat16), "tensor", axis=1, tiled=True)
    flat_first = first_rows.reshape(flat_rows, model_width)
    proj_flat = proj_weight.reshape(model_width, 3 * channels)
    projected = (
        jnp.dot(flat_first, proj_flat, preferred_element_type=jnp.float32).reshape(
            row_count, length, 3, channels
        )
        + proj_bias[None, None]
    )

    def local_short(values_in, weights_in, biases_in):
        return short_conv(values_in, segment_ids, weights_in, biases_in)

    mixed, short_back = jax.vjp(local_short, projected, short_weight, short_bias)
    gate_out = mixed[:, :, 0]
    gate_in = mixed[:, :, 1]
    values = mixed[:, :, 2]
    product = values * gate_in
    product_b = product.astype(jnp.bfloat16)

    def local_filter(embed_w, embed_b, freq_vals, inner_w, inner_b, filter_w):
        return make_filter(embed_w, embed_b, freq_vals, inner_w, inner_b, filter_w, decay_rate)

    filter_taps, filter_back = jax.vjp(
        local_filter, embed_weight, embed_bias, sine_freq, inner_weight, inner_bias, filter_weight
    )
    taps_b = filter_taps.astype(jnp.bfloat16)
    matrices = (dft_rows(length), dft_rows(shard_len))
    masks = row_masks(segment_ids[0], shard_len)
    taps_spectra = (
        to_spectrum(matrices[0], taps_b),
        to_spectrum(matrices[1], taps_b[:shard_len]),
    )
    value_spectra = spectra_of(product_b[0], masks, matrices)
    convolved = filter_row(value_spectra, taps_spectra, masks, matrices, False)[None]
    summed = convolved + skip_gain * product
    gated_b = (summed * gate_out).astype(jnp.bfloat16)
    flat_gated = gated_b.reshape(flat_rows, channels)
    partial_mix = jnp.dot(flat_gated, out_weight, preferred_element_type=jnp.float32).reshape(
        row_count, length, model_width
    )
    residual = (
        tokens_f
        + lax.psum_scatter(partial_mix, "tensor", scatter_dimension=1, tiled=True)
        + out_bias
    )
    normed2, norm2_back = jax.vjp(layer_norm, residual, norm2_gain, norm2_bias)
    second_rows = lax.all_gather(normed2.astype(jnp.bfloat16), "tensor", axis=1, tiled=True)
    flat_second = second_rows.reshape(flat_rows, model_width)
    hidden_pre = jnp.dot(flat_second, up_weight, preferred_element_type=jnp.float32) + up_bias
    active, gelu_back = jax.vjp(gelu_tanh, hidden_pre)
    active_b = active.astype(jnp.bfloat16)
    partial_mlp = jnp.dot(active_b, down_weight, preferred_element_type=jnp.float32).reshape(
        row_count, length, model_width
    )
    mlp_out = lax.psum_scatter(
        partial_mlp.astype(jnp.bfloat16), "tensor", scatter_dimension=1, tiled=True
    ).astype(jnp.float32)
    layer_out = (residual + mlp_out + down_bias).astype(jnp.bfloat16)
    grad_out = cotangent.astype(jnp.float32)
    grad_down_bias = jnp.sum(grad_out, axis=(0, 1))
    grad_rows = lax.all_gather(cotangent, "tensor", axis=1, tiled=True)
    flat_grad = grad_rows.reshape(flat_rows, model_width)
    grad_down_weight = jnp.einsum(
        "nf,nd->fd", active_b, flat_grad, preferred_element_type=jnp.float32
    )
    grad_active = jnp.einsum(
        "nd,fd->nf", flat_grad, down_weight, preferred_element_type=jnp.float32
    )
    grad_hidden = gelu_back(grad_active)[0]
    grad_up_bias = jnp.sum(grad_hidden, axis=0)
    hidden_b = grad_hidden.astype(jnp.bfloat16)
    grad_up_weight = jnp.einsum(
        "nd,nf->df", flat_second, hidden_b, preferred_element_type=jnp.float32
    )
    grad_second = jnp.einsum(
        "nf,df->nd", hidden_b, up_weight, preferred_element_type=jnp.float32
    ).reshape(row_count, length, model_width)
    grad_normed2 = lax.psum_scatter(grad_second, "tensor", scatter_dimension=1, tiled=True)
    grad_residual, grad_norm2_gain, grad_norm2_bias = norm2_back(grad_normed2)
    grad_residual = grad_residual + grad_out
    grad_resid_b = lax.all_gather(grad_residual.astype(jnp.bfloat16), "tensor", axis=1, tiled=True)
    grad_out_bias = jnp.sum(grad_residual, axis=(0, 1))
    flat_resid = grad_resid_b.reshape(flat_rows, model_width)
    grad_out_weight = jnp.einsum(
        "nc,nd->cd", flat_gated, flat_resid, preferred_element_type=jnp.float32
    )
    grad_gated = jnp.einsum(
        "nd,cd->nc", flat_resid, out_weight, preferred_element_type=jnp.float32
    ).reshape(row_count, length, channels)
    grad_summed = grad_gated * gate_out
    grad_gate_out = grad_gated * summed
    grad_skip_gain = jnp.sum(grad_summed * product, axis=(0, 1))
    grad_spectra = spectra_of(grad_summed[0].astype(jnp.bfloat16), masks, matrices)
    grad_conv = filter_row(grad_spectra, taps_spectra, masks, matrices, True)[None]
    grad_taps = taps_gradient(value_spectra, grad_spectra, matrices)
    grad_product = grad_conv + grad_summed * skip_gain
    grad_mixed = jnp.stack([grad_gate_out, grad_product * values, grad_product * gate_in], axis=2)
    grad_projected, grad_short_weight, grad_short_bias = short_back(grad_mixed)
    (
        grad_embed_weight,
        grad_embed_bias,
        grad_sine_freq,
        grad_inner_weight,
        grad_inner_bias,
        grad_filter_weight,
    ) = filter_back(grad_taps)
    grad_proj_bias = jnp.sum(grad_projected, axis=(0, 1))
    projected_b = grad_projected.astype(jnp.bfloat16).reshape(flat_rows, 3 * channels)
    grad_proj_weight = jnp.einsum(
        "nd,nk->dk", flat_first, projected_b, preferred_element_type=jnp.float32
    ).reshape(model_width, 3, channels)
    grad_first = jnp.einsum(
        "nk,dk->nd", projected_b, proj_flat, preferred_element_type=jnp.float32
    ).reshape(row_count, length, model_width)
    grad_normed1 = lax.psum_scatter(
        grad_first.astype(jnp.bfloat16), "tensor", scatter_dimension=1, tiled=True
    ).astype(jnp.float32)
    grad_tokens, grad_norm1_gain, grad_norm1_bias = norm1_back(grad_normed1)
    grad_tokens = grad_tokens + grad_residual
    (
        grad_proj_weight,
        grad_proj_bias,
        grad_short_weight,
        grad_short_bias,
        grad_filter_weight,
        grad_skip_gain,
        grad_out_weight,
        grad_up_weight,
        grad_up_bias,
        grad_down_weight,
    ) = (
        lax.psum(grad_proj_weight.astype(jnp.bfloat16), "dp").astype(jnp.float32),
        lax.psum(grad_proj_bias.astype(jnp.bfloat16), "dp").astype(jnp.float32),
        lax.psum(grad_short_weight.astype(jnp.bfloat16), "dp").astype(jnp.float32),
        lax.psum(grad_short_bias.astype(jnp.bfloat16), "dp").astype(jnp.float32),
        lax.psum(grad_filter_weight.astype(jnp.bfloat16), "dp").astype(jnp.float32),
        lax.psum(grad_skip_gain.astype(jnp.bfloat16), "dp").astype(jnp.float32),
        lax.psum(grad_out_weight.astype(jnp.bfloat16), "dp").astype(jnp.float32),
        lax.psum(grad_up_weight.astype(jnp.bfloat16), "dp").astype(jnp.float32),
        lax.psum(grad_up_bias.astype(jnp.bfloat16), "dp").astype(jnp.float32),
        lax.psum(grad_down_weight.astype(jnp.bfloat16), "dp").astype(jnp.float32),
    )
    (
        grad_norm1_gain,
        grad_norm1_bias,
        grad_out_bias,
        grad_norm2_gain,
        grad_norm2_bias,
        grad_down_bias,
        grad_embed_weight,
        grad_embed_bias,
        grad_sine_freq,
        grad_inner_weight,
        grad_inner_bias,
    ) = lax.psum(
        (
            grad_norm1_gain,
            grad_norm1_bias,
            grad_out_bias,
            grad_norm2_gain,
            grad_norm2_bias,
            grad_down_bias,
            grad_embed_weight,
            grad_embed_bias,
            grad_sine_freq,
            grad_inner_weight,
            grad_inner_bias,
        ),
        ("dp", "tensor"),
    )
    return (
        layer_out,
        grad_tokens,
        grad_norm1_gain,
        grad_norm1_bias,
        grad_proj_weight,
        grad_proj_bias,
        grad_short_weight,
        grad_short_bias,
        grad_embed_weight,
        grad_embed_bias,
        grad_sine_freq,
        grad_inner_weight,
        grad_inner_bias,
        grad_filter_weight,
        grad_skip_gain,
        grad_out_weight,
        grad_out_bias,
        grad_norm2_gain,
        grad_norm2_bias,
        grad_up_weight,
        grad_up_bias,
        grad_down_weight,
        grad_down_bias,
    )


def solution(mesh):
    return jax.shard_map(
        body,
        mesh=mesh,
        in_specs=(
            P("dp", "tensor", None),
            P("dp", None),
            P(),
            P(),
            P(None, None, "tensor"),
            P(None, "tensor"),
            P(None, None, "tensor"),
            P(None, "tensor"),
            P(),
            P(),
            P(),
            P(),
            P(),
            P(None, "tensor"),
            P("tensor"),
            P("tensor"),
            P("tensor", None),
            P(),
            P(),
            P(),
            P(None, "tensor"),
            P("tensor"),
            P("tensor", None),
            P(),
            P("dp", "tensor", None),
        ),
        out_specs=(
            P("dp", "tensor", None),
            P("dp", "tensor", None),
            P(),
            P(),
            P(None, None, "tensor"),
            P(None, "tensor"),
            P(None, None, "tensor"),
            P(None, "tensor"),
            P(),
            P(),
            P(),
            P(),
            P(),
            P(None, "tensor"),
            P("tensor"),
            P("tensor", None),
            P(),
            P(),
            P(),
            P(None, "tensor"),
            P("tensor"),
            P("tensor", None),
            P(),
        ),
        check_vma=False,
    )
```

```python
import functools
import math

import jax
import jax.numpy as jnp
import ml_dtypes
import numpy as np
from jax import lax
from jax.experimental import pallas as pl
from jax.experimental.pallas import tpu as pltpu
from jax.sharding import PartitionSpec as P

FEAT = 33
SEQ = 1024
NDOC = 8


EPS = 1e-05
HIGH = lax.Precision.HIGHEST
SHIFT = 0.1


def layer_norm(values, norm_gain, norm_bias):
    average = jnp.mean(values, axis=-1, keepdims=True)
    centered = values - average
    variance = jnp.mean(centered * centered, axis=-1, keepdims=True)
    return centered * lax.rsqrt(variance + EPS) * norm_gain + norm_bias


BY_INDEX = pl.DeviceIdType.MESH


def greet(devices):
    barrier = pltpu.get_barrier_semaphore()
    for device in devices:
        pl.semaphore_signal(barrier, inc=1, device_id=device, device_id_type=BY_INDEX)
    pl.semaphore_wait(barrier, len(devices))


def remote(source, target, send_sem, recv_sem, device):
    return pltpu.make_async_remote_copy(
        src_ref=source,
        dst_ref=target,
        send_sem=send_sem,
        recv_sem=recv_sem,
        device_id=device,
        device_id_type=BY_INDEX,
    )


def tensor_peers():
    count = lax.axis_size("tensor")
    me = lax.axis_index("tensor")
    return [lax.rem(me + k, count) for k in range(1, count)]


def sibling():
    me = lax.axis_index("dp")
    return me + 1 - 2 * lax.rem(me, 2)


def chip_peers():
    chips = lax.axis_size("dp") // 2
    me = lax.axis_index("dp")
    core = lax.rem(me, 2)
    result = []
    for k in range(1, chips):
        chip = lax.rem(me // 2 + k, chips)
        result.append((chip, 2 * chip + core))
    return result


def exchange_kernel(kinds, *refs):
    count = len(kinds)
    sources, targets = refs[:count], refs[count : 2 * count]
    local_sem, send_sem, recv_sem = refs[2 * count :]
    me = lax.axis_index("tensor")
    peers = tensor_peers()
    greet([{"tensor": peer} for peer in peers])
    copies = []
    for i, kind in enumerate(kinds):
        for k, peer in enumerate(peers):
            copies.append(
                remote(
                    sources[i] if kind == "gather" else sources[i].at[peer],
                    targets[i].at[me],
                    send_sem.at[i, k],
                    recv_sem.at[i, k],
                    {"tensor": peer},
                )
            )
            copies[-1].start()
    for i, kind in enumerate(kinds):
        own = sources[i] if kind == "gather" else sources[i].at[me]
        copies.append(pltpu.make_async_copy(own, targets[i].at[me], local_sem.at[i]))
        copies[-1].start()
    for copy in copies:
        copy.wait()


def exchange(arrays, kinds, channel):
    groups = lax.axis_size("tensor")
    count = len(arrays)
    shapes = []
    for array, kind in zip(arrays, kinds):
        shape = (groups,) + array.shape if kind == "gather" else array.shape
        shapes.append(jax.ShapeDtypeStruct(shape, array.dtype))
    anywhere = pl.BlockSpec(memory_space=pl.ANY)
    return pl.pallas_call(
        functools.partial(exchange_kernel, kinds),
        out_shape=shapes,
        in_specs=[anywhere] * count,
        out_specs=[anywhere] * count,
        scratch_shapes=[
            pltpu.SemaphoreType.DMA((count,)),
            pltpu.SemaphoreType.DMA((count, groups - 1)),
            pltpu.SemaphoreType.DMA((count, groups - 1)),
        ],
        compiler_params=pltpu.CompilerParams(collective_id=channel, has_side_effects=True),
        cost_estimate=pl.CostEstimate(
            flops=0,
            bytes_accessed=130_000_000 if "gather" in kinds else 45_000_000,
            transcendentals=0,
        ),
        name=f"exchange_{channel}",
    )(*arrays)


def start_kernel(
    first, part, first_all, part_all, local_sems, first_sems, part_sems, chip_sems, core_sems
):
    me = lax.axis_index("tensor")
    place = lax.axis_index("dp")
    core = lax.rem(place, 2)
    chip = place // 2
    near = sibling()
    peers = tensor_peers()
    mates = chip_peers()
    greet(
        [{"tensor": peer} for peer in peers]
        + [{"dp": near}]
        + [{"dp": mate} for unused_chip, mate in mates]
    )

    def spread(source, target, sems, devices):
        copies = [
            remote(source, target, sems.at[0, k], sems.at[1, k], device)
            for k, device in enumerate(devices)
        ]
        for copy in copies:
            copy.start()
        return copies

    own = pltpu.make_async_copy(part, part_all.at[me, chip, core], local_sems.at[0])
    own.start()
    own_first = pltpu.make_async_copy(first, first_all.at[me], local_sems.at[1])
    own_first.start()
    tensor_devices = [{"tensor": peer} for peer in peers]
    parts = spread(part, part_all.at[me, chip, core], part_sems, tensor_devices)
    firsts = spread(first, first_all.at[me], first_sems, tensor_devices)
    own.wait()
    for copy in parts:
        copy.wait()
    held = part_all.at[:, chip, core]
    for copy in spread(held, held, chip_sems, [{"dp": mate} for unused_chip, mate in mates]):
        copy.wait()
    held = part_all.at[:, :, core]
    for copy in spread(held, held, core_sems, [{"dp": near}]):
        copy.wait()
    own_first.wait()
    for copy in firsts:
        copy.wait()


def start(first, part, channel):
    groups = lax.axis_size("tensor")
    chips = lax.axis_size("dp") // 2
    anywhere = pl.BlockSpec(memory_space=pl.ANY)
    return pl.pallas_call(
        start_kernel,
        out_shape=[
            jax.ShapeDtypeStruct((groups,) + first.shape, first.dtype),
            jax.ShapeDtypeStruct((groups, chips, 2) + part.shape, part.dtype),
        ],
        in_specs=[anywhere] * 2,
        out_specs=[anywhere] * 2,
        scratch_shapes=[
            pltpu.SemaphoreType.DMA((2,)),
            pltpu.SemaphoreType.DMA((2, groups - 1)),
            pltpu.SemaphoreType.DMA((2, groups - 1)),
            pltpu.SemaphoreType.DMA((2, chips - 1)),
            pltpu.SemaphoreType.DMA((2, 1)),
        ],
        compiler_params=pltpu.CompilerParams(collective_id=channel, has_side_effects=True),
        cost_estimate=pl.CostEstimate(flops=0, bytes_accessed=130_000_000, transcendentals=0),
        name="start",
    )(first, part)


def row_reduce_kernel(kinds, *refs):
    count = len(kinds)
    blocks, weights = refs[0], refs[1 : 1 + count]
    block_sum, weight_sums = refs[1 + count], refs[2 + count : 2 + 2 * count]
    block_recv, block_sems = refs[2 + 2 * count : 4 + 2 * count]
    scratch = refs[4 + 2 * count :]
    per_weight = []
    for kind in kinds:
        per_weight.append(scratch[:7])
        scratch = scratch[7:]
    tensor_scratch = scratch
    me = lax.axis_index("tensor")
    peers = tensor_peers()
    chips = lax.axis_size("dp") // 2
    place = lax.axis_index("dp")
    core = lax.rem(place, 2)
    chip = place // 2
    near = sibling()
    mates = chip_peers()
    barrier_devices = [{"tensor": peer} for peer in peers]
    if count:
        barrier_devices += [{"dp": near}] + [{"dp": mate} for unused_chip, mate in mates]
    greet(barrier_devices)

    def span(index, size):
        return pl.ds(pl.multiple_of(index * size, 16), size)

    def step(source, target, sems, devices, first=0):
        copies = [
            remote(
                source(k) if callable(source) else source,
                target(k) if callable(target) else target,
                sems.at[0, first + k],
                sems.at[1, first + k],
                device,
            )
            for k, device in enumerate(devices)
        ]
        for copy in copies:
            copy.start()
        return copies

    tensor_devices = [{"tensor": peer} for peer in peers]
    chip_devices = [{"dp": mate} for unused_chip, mate in mates]
    pairs = []
    for i, kind in enumerate(kinds):
        core_recv, half, chip_recv, whole, core_sems, chip_sems, gather_sems = per_weight[i]
        other_half = weights[i].at[..., span(1 - core, half.shape[-2]), :]
        pairs.append(step(other_half, core_recv, core_sems, [{"dp": near}]))
    arriving = step(
        lambda k: blocks.at[peers[k]], lambda k: block_recv.at[k], block_sems, tensor_devices
    )
    spread = []
    for i, kind in enumerate(kinds):
        core_recv, half, chip_recv, whole, core_sems, chip_sems, gather_sems = per_weight[i]
        part = half.shape[-2] // chips
        pairs[i][0].wait()
        half[...] = (
            weights[i][..., span(core, half.shape[-2]), :].astype(jnp.float32)
            + core_recv[...].astype(jnp.float32)
        ).astype(half.dtype)
        spread.append(
            step(
                lambda k, half=half, part=part: half.at[..., span(mates[k][0], part), :],
                lambda k, chip_recv=chip_recv: chip_recv.at[k],
                chip_sems,
                chip_devices,
            )
        )
    totals = []
    across = []
    for i, kind in enumerate(kinds):
        core_recv, half, chip_recv, whole, core_sems, chip_sems, gather_sems = per_weight[i]
        part = half.shape[-2] // chips
        total = half[..., span(chip, part), :].astype(jnp.float32)
        for k, copy in enumerate(spread[i]):
            copy.wait()
            total = total + chip_recv[k].astype(jnp.float32)
        totals.append(total)
        if kind == "tensor":
            held, held_recv, held_sems = tensor_scratch
            held[...] = total.astype(held.dtype)
            across = step(
                lambda k: held.at[peers[k]], lambda k: held_recv.at[k], held_sems, tensor_devices
            )
    back = []
    for i, kind in enumerate(kinds):
        core_recv, half, chip_recv, whole, core_sems, chip_sems, gather_sems = per_weight[i]
        part = half.shape[-2] // chips
        total = totals[i]
        if kind == "tensor":
            held, held_recv, held_sems = tensor_scratch
            total = held[me].astype(jnp.float32)
            for k, copy in enumerate(across):
                copy.wait()
                total = total + held_recv[k].astype(jnp.float32)
        mine = span(core * chips + chip, part)
        whole[mine] = total.astype(whole.dtype)
        back.append(step(whole.at[mine], whole.at[mine], gather_sems, chip_devices))
    last = []
    for i, kind in enumerate(kinds):
        core_recv, half, chip_recv, whole, core_sems, chip_sems, gather_sems = per_weight[i]
        for copy in back[i]:
            copy.wait()
        own_half = whole.at[span(core, half.shape[-2])]
        last.append(step(own_half, own_half, core_sems, [{"dp": near}], 1))
    block_total = blocks[me].astype(jnp.float32)
    for k, copy in enumerate(arriving):
        copy.wait()
        block_total = block_total + block_recv[k].astype(jnp.float32)
    block_sum[...] = block_total
    for i in range(count):
        last[i][0].wait()
        weight_sums[i][...] = per_weight[i][3][...]


def row_reduce(blocks, weights, channel):
    groups, tokens, width = blocks.shape
    chips = lax.axis_size("dp") // 2
    low = jnp.bfloat16
    vmem = pl.BlockSpec(memory_space=pltpu.VMEM)
    scratch = [
        pltpu.VMEM((groups - 1, tokens, width), low),
        pltpu.SemaphoreType.DMA((2, groups - 1)),
    ]
    tensor_scratch = []
    kinds = []
    shapes = [jax.ShapeDtypeStruct((tokens, width), jnp.float32)]
    for weight in weights:
        rows, columns = weight.shape[-2:]
        lead = weight.shape[:-2]
        part = rows // 2 // chips
        kinds.append("tensor" if lead else "dp")
        shapes.append(jax.ShapeDtypeStruct((rows, columns), low))
        scratch += [
            pltpu.VMEM(lead + (rows // 2, columns), low),
            pltpu.VMEM(lead + (rows // 2, columns), low),
            pltpu.VMEM((chips - 1,) + lead + (part, columns), low),
            pltpu.VMEM((rows, columns), low),
            pltpu.SemaphoreType.DMA((2, 2)),
            pltpu.SemaphoreType.DMA((2, chips - 1)),
            pltpu.SemaphoreType.DMA((2, chips - 1)),
        ]
        if lead:
            tensor_scratch = [
                pltpu.VMEM(lead + (part, columns), low),
                pltpu.VMEM((groups - 1, part, columns), low),
                pltpu.SemaphoreType.DMA((2, groups - 1)),
            ]
    return pl.pallas_call(
        functools.partial(row_reduce_kernel, kinds),
        out_shape=shapes,
        in_specs=[vmem] * (1 + len(weights)),
        out_specs=[vmem] * len(shapes),
        scratch_shapes=scratch + tensor_scratch,
        compiler_params=pltpu.CompilerParams(
            collective_id=channel, has_side_effects=True, vmem_limit_bytes=48 * 1024 * 1024
        ),
        cost_estimate=pl.CostEstimate(flops=0, bytes_accessed=150_000_000, transcendentals=0),
        name=f"row_reduce_{channel}",
    )(blocks, *weights)


def small_sum_kernel(
    wide_rows, packed, result, core_recv, chip_slots, group_slots, core_sems, chip_sems, group_sems
):
    groups = lax.axis_size("tensor")
    me = lax.axis_index("tensor")
    peers = tensor_peers()
    chips = lax.axis_size("dp") // 2
    chip = lax.axis_index("dp") // 2
    near = sibling()
    mates = chip_peers()
    greet(
        [{"tensor": peer} for peer in peers]
        + [{"dp": near}]
        + [{"dp": mate} for unused_chip, mate in mates]
    )
    pair = remote(packed, core_recv, core_sems.at[0], core_sems.at[1], {"dp": near})
    pair.start()
    pair.wait()
    chip_slots[chip] = packed[...] + core_recv[...]
    copies = []
    for k, (other, mate) in enumerate(mates):
        copies.append(
            remote(
                chip_slots.at[chip],
                chip_slots.at[chip],
                chip_sems.at[0, k],
                chip_sems.at[1, k],
                {"dp": mate},
            )
        )
        copies[-1].start()
    for copy in copies:
        copy.wait()
    total = chip_slots[0]
    for i in range(1, chips):
        total = total + chip_slots[i]
    result[...] = total
    group_slots[me] = total[:wide_rows]
    copies = []
    for k, peer in enumerate(peers):
        copies.append(
            remote(
                group_slots.at[me],
                group_slots.at[me],
                group_sems.at[0, k],
                group_sems.at[1, k],
                {"tensor": peer},
            )
        )
        copies[-1].start()
    for copy in copies:
        copy.wait()
    total = group_slots[0]
    for i in range(1, groups):
        total = total + group_slots[i]
    result[:wide_rows] = total


def small_sum(packed, wide_rows, channel):
    groups = lax.axis_size("tensor")
    chips = lax.axis_size("dp") // 2
    vmem = pl.BlockSpec(memory_space=pltpu.VMEM)
    return pl.pallas_call(
        functools.partial(small_sum_kernel, wide_rows),
        out_shape=jax.ShapeDtypeStruct(packed.shape, packed.dtype),
        in_specs=[vmem],
        out_specs=vmem,
        scratch_shapes=[
            pltpu.VMEM(packed.shape, packed.dtype),
            pltpu.VMEM((chips,) + packed.shape, packed.dtype),
            pltpu.VMEM((groups, wide_rows) + packed.shape[1:], packed.dtype),
            pltpu.SemaphoreType.DMA((2,)),
            pltpu.SemaphoreType.DMA((2, chips - 1)),
            pltpu.SemaphoreType.DMA((2, groups - 1)),
        ],
        compiler_params=pltpu.CompilerParams(collective_id=channel, has_side_effects=True),
        cost_estimate=pl.CostEstimate(flops=0, bytes_accessed=60_000_000, transcendentals=0),
        name="small_sum",
    )(packed)


GELU_RATE = math.sqrt(2.0 / math.pi)
GELU_CUBE = 0.044715


def dot_nn(left, right):
    return jnp.dot(left, right, preferred_element_type=jnp.float32)


def dot_nt(left, right):
    return lax.dot_general(
        left, right, (((1,), (1,)), ((), ())), preferred_element_type=jnp.float32
    )


def dot_tn(left, right):
    return lax.dot_general(
        left, right, (((0,), (0,)), ((), ())), preferred_element_type=jnp.float32
    )


def feed_forward_kernel(
    second, cotangent, up, bias, down, mlp, grad_second, up_grad, down_grad, bias_grad, mlp_sum, grad_sum
):
    step = pl.program_id(0)
    hidden = dot_nn(second[...], up[...]) + bias[...]
    cube = GELU_CUBE * hidden * hidden
    slope = jnp.tanh(GELU_RATE * hidden * (1.0 + cube))
    gate = 0.5 * (1.0 + slope)
    active = (hidden * gate).astype(jnp.bfloat16)
    rate = gate + (0.5 * GELU_RATE) * hidden * (1.0 - slope * slope) * (1.0 + 3.0 * cube)
    grad_hidden = dot_nt(cotangent[...], down[...]) * rate
    bias_grad[...] = jnp.sum(grad_hidden, axis=0, keepdims=True)
    low = grad_hidden.astype(jnp.bfloat16)
    mlp_part = dot_nn(active, down[...])
    grad_part = dot_nt(low, up[...])
    up_grad[...] = dot_tn(second[...], low).astype(jnp.bfloat16)
    down_grad[...] = dot_tn(active, cotangent[...]).astype(jnp.bfloat16)

    @pl.when(step == 0)
    def _():
        mlp_sum[...] = mlp_part
        grad_sum[...] = grad_part

    @pl.when(step > 0)
    def _():
        mlp_sum[...] += mlp_part
        grad_sum[...] += grad_part

    @pl.when(step == pl.num_programs(0) - 1)
    def _():
        mlp[...] = mlp_sum[...].astype(jnp.bfloat16)
        grad_second[...] = grad_sum[...].astype(jnp.bfloat16)


def feed_forward(second, cotangent, up, bias, down):
    tokens, width = second.shape
    units = up.shape[1]
    chunk = min(256, units)

    def whole(step):
        return (0, 0)

    def column(step):
        return (0, step)

    def row(step):
        return (step, 0)

    low = jnp.bfloat16
    return pl.pallas_call(
        feed_forward_kernel,
        grid=(units // chunk,),
        in_specs=[
            pl.BlockSpec((tokens, width), whole),
            pl.BlockSpec((tokens, width), whole),
            pl.BlockSpec((width, chunk), column),
            pl.BlockSpec((1, chunk), column),
            pl.BlockSpec((chunk, width), row),
        ],
        out_specs=[
            pl.BlockSpec((tokens, width), whole),
            pl.BlockSpec((tokens, width), whole),
            pl.BlockSpec((width, chunk), column),
            pl.BlockSpec((chunk, width), row),
            pl.BlockSpec((1, chunk), column),
        ],
        out_shape=[
            jax.ShapeDtypeStruct((tokens, width), low),
            jax.ShapeDtypeStruct((tokens, width), low),
            jax.ShapeDtypeStruct((width, units), low),
            jax.ShapeDtypeStruct((units, width), low),
            jax.ShapeDtypeStruct((1, units), jnp.float32),
        ],
        scratch_shapes=[
            pltpu.VMEM((tokens, width), jnp.float32),
            pltpu.VMEM((tokens, width), jnp.float32),
        ],
        compiler_params=pltpu.CompilerParams(
            dimension_semantics=("arbitrary",), vmem_limit_bytes=56 * 1024 * 1024
        ),
        cost_estimate=pl.CostEstimate(
            flops=12 * tokens * width * units,
            bytes_accessed=8 * width * units + 8 * tokens * width,
            transcendentals=tokens * units,
        ),
        name="feed_forward",
    )(second, cotangent, up, bias, down)


def transform(length):
    places = np.arange(length)
    angles = ((places[:, None] * places[None, :]) % (2 * length)) * (np.pi / length)
    return (
        jnp.asarray(np.cos(angles).astype(ml_dtypes.bfloat16)),
        jnp.asarray((-np.sin(angles)).astype(ml_dtypes.bfloat16)),
    )


def features_by_row():
    places = np.arange(SEQ, dtype=np.float32)
    bands = np.arange(1, (FEAT - 1) // 2 + 1, dtype=np.float32)
    angles = 2.0 * np.pi * np.arange(SEQ)[None, :] * bands[:, None].astype(np.float64) / SEQ
    rows = np.concatenate([(places / (SEQ - 1))[None, :], np.cos(angles), np.sin(angles)], axis=0)
    rows = np.concatenate([rows, np.zeros((-FEAT % 8, SEQ))], axis=0)
    return jnp.asarray(rows.astype(np.float32))


def exact(left, right, contract):
    return lax.dot_general(
        left, right, (contract, ((), ())), precision=HIGH, preferred_element_type=jnp.float32
    )


def bin_scale(length):
    bins = lax.broadcasted_iota(jnp.int32, (length, 1), 0)
    return jnp.where(bins == 0, 0.5 / length, 1.0 / length)


def signs(length):
    places = lax.broadcasted_iota(jnp.int32, (length, 1), 0)
    return (1 - 2 * lax.rem(places, 2)).astype(jnp.float32)


def modulation(length, decay):
    places = lax.broadcasted_iota(jnp.int32, (length, 1), 0).astype(jnp.float32)
    return jnp.exp(-decay * (places / SEQ)) + SHIFT


def taps_kernel(
    features,
    embed,
    inner,
    columns,
    filter_weight,
    decay,
    cos_main,
    sin_main,
    cos_small,
    sin_small,
    pre,
    main_re,
    main_im,
    main_top,
    small_re,
    small_im,
    small_top,
):
    length = features.shape[1]
    region = cos_small.shape[0]
    hidden = None
    for i in range(3):
        if i == 0:
            value = exact(embed[...], features[...], ((0,), (0,)))
        else:
            value = exact(inner[i - 1], hidden, ((0,), (0,)))
        value = value + columns[:, 3 + i : 4 + i]
        pre[i] = value
        hidden = jnp.sin(columns[:, i : i + 1] * value)
    taps = exact(hidden, filter_weight[...], ((0,), (0,)))
    taps = (taps * modulation(length, decay[...])).astype(jnp.bfloat16)
    scale = bin_scale(length)
    main_re[...] = dot_nn(cos_main[...], taps) * scale
    main_im[...] = dot_nn(sin_main[...], taps) * scale
    top = jnp.sum(taps.astype(jnp.float32) * signs(length), axis=0, keepdims=True)
    main_top[...] = top * (0.5 / length)
    short = taps[:region]
    scale = bin_scale(region)
    small_re[...] = dot_nn(cos_small[...], short) * scale
    small_im[...] = dot_nn(sin_small[...], short) * scale
    top = jnp.sum(short.astype(jnp.float32) * signs(region), axis=0, keepdims=True)
    small_top[...] = top * (0.5 / region)


def spectra(values, marks, cos_main, sin_main, cos_small, sin_small):
    length = values.shape[0]
    region = cos_small.shape[0]
    main = jnp.where(marks[:, 0:1] > 0, values, 0.0)
    top = jnp.sum(main * signs(length), axis=0, keepdims=True)
    main = main.astype(jnp.bfloat16)
    main_bins = (dot_nn(cos_main[...], main), dot_nn(sin_main[...], main), top)
    head, tail = values[:region], values[length - region :]
    head_slot, tail_slot = marks[:region, 3:4], marks[length - region :, 4:5]
    pieces = [
        jnp.where(head_slot == d, head, 0.0) + jnp.where(tail_slot == d, tail, 0.0)
        for d in range(NDOC)
    ]
    small = jnp.concatenate(pieces, axis=1)
    top = jnp.sum(small * signs(region), axis=0, keepdims=True)
    small = small.astype(jnp.bfloat16)
    small_bins = (dot_nn(cos_small[...], small), dot_nn(sin_small[...], small), top)
    return main_bins, small_bins


def times(left, right, conjugate):
    left_re, left_im, left_top = left
    right_re, right_im, right_top = right
    if conjugate:
        return (
            left_re * right_re + left_im * right_im,
            left_re * right_im - left_im * right_re,
            left_top * right_top,
        )
    return (
        left_re * right_re - left_im * right_im,
        left_re * right_im + left_im * right_re,
        left_top * right_top,
    )


def from_bins(bins, cos_rows, sin_rows):
    real, imag, top = bins
    return (
        dot_nn(cos_rows[...], real.astype(jnp.bfloat16))
        + dot_nn(sin_rows[...], imag.astype(jnp.bfloat16))
        + signs(real.shape[0]) * top
    )


def beside(part):
    return jnp.concatenate([part] * NDOC, axis=1)


def filtered(main_bins, small_bins, taps_main, taps_small, marks, transforms, conjugate):
    cos_main, sin_main, cos_small, sin_small = transforms
    main = from_bins(times(taps_main, main_bins, conjugate), cos_main, sin_main)
    taps_wide = tuple(beside(part) for part in taps_small)
    small = from_bins(times(taps_wide, small_bins, conjugate), cos_small, sin_small)
    length, channels = main.shape
    region = small.shape[0]
    main = jnp.where(marks[:, 0:1] > 0, main, 0.0)
    head, tail = main[:region], main[length - region :]
    head_slot, tail_slot = marks[:region, 3:4], marks[length - region :, 4:5]
    for d in range(NDOC):
        piece = small[:, d * channels : (d + 1) * channels]
        head = head + jnp.where(head_slot == d, piece, 0.0)
        tail = tail + jnp.where(tail_slot == d, piece, 0.0)
    return jnp.concatenate([head, main[region : length - region], tail], axis=0)


def operator_kernel(
    first,
    proj,
    proj_bias,
    short,
    short_bias,
    skip,
    marks,
    cos_main,
    sin_main,
    cos_small,
    sin_small,
    main_re,
    main_im,
    main_top,
    small_re,
    small_im,
    small_top,
    gated,
    projected,
    mixed,
    summed,
):
    channels = skip.shape[1]
    transforms = (cos_main, sin_main, cos_small, sin_small)
    for k in range(3):
        lanes = slice(k * channels, (k + 1) * channels)
        part = dot_nn(first[...], proj[:, lanes]) + proj_bias[:, lanes]
        projected[:, lanes] = part
        running = short_bias[:, lanes] + short[0:1, lanes] * part
        for lag in (1, 2):
            moved = jnp.where(marks[:, lag : lag + 1] > 0, pltpu.roll(part, lag, 0), 0.0)
            running = running + short[lag : lag + 1, lanes] * moved
        mixed[:, lanes] = running
    product = mixed[:, 2 * channels :] * mixed[:, channels : 2 * channels]
    low = product.astype(jnp.bfloat16).astype(jnp.float32)
    main_bins, small_bins = spectra(low, marks, *transforms)
    result = filtered(
        main_bins,
        small_bins,
        (main_re[...], main_im[...], main_top[...]),
        (small_re[...], small_im[...], small_top[...]),
        marks,
        transforms,
        False,
    )
    total = result + skip[...] * product
    summed[...] = total
    gated[...] = (total * mixed[:, :channels]).astype(jnp.bfloat16)


def operator_back_kernel(
    grad_gated,
    first,
    proj,
    short,
    skip,
    marks,
    cos_main,
    sin_main,
    cos_small,
    sin_small,
    main_re,
    main_im,
    main_top,
    small_re,
    small_im,
    small_top,
    projected,
    mixed,
    summed,
    grad_first,
    proj_grad,
    grad_taps,
    sums,
    skip_sum,
    grad_low,
):
    channels = skip.shape[1]
    length = first.shape[0]
    region = cos_small.shape[0]
    transforms = (cos_main, sin_main, cos_small, sin_small)
    gate_out = mixed[:, :channels]
    gate_in = mixed[:, channels : 2 * channels]
    values = mixed[:, 2 * channels :]
    product = values * gate_in
    low = product.astype(jnp.bfloat16).astype(jnp.float32)
    value_main, value_small = spectra(low, marks, *transforms)
    grad = grad_gated[...].astype(jnp.float32)
    grad_summed = grad * gate_out
    skip_sum[...] = jnp.sum(grad_summed * product, axis=0, keepdims=True)
    low = grad_summed.astype(jnp.bfloat16).astype(jnp.float32)
    grad_main, grad_small = spectra(low, marks, *transforms)
    real, imag, top = times(value_main, grad_main, True)
    scale = bin_scale(length)
    taps = from_bins((real * scale, imag * scale, top * (0.5 / length)), cos_main, sin_main)
    scale = bin_scale(region)
    real, imag, top = (
        sum(part[:, d * channels : (d + 1) * channels] for d in range(NDOC))
        for part in times(value_small, grad_small, True)
    )
    taps_small = from_bins((real * scale, imag * scale, top * (0.5 / region)), cos_small, sin_small)
    grad_taps[:region] = taps[:region] + taps_small
    grad_taps[region:] = taps[region:]
    result = filtered(
        grad_main,
        grad_small,
        (main_re[...], main_im[...], main_top[...]),
        (small_re[...], small_im[...], small_top[...]),
        marks,
        transforms,
        True,
    )
    grad_product = result + grad_summed * skip[...]
    parts = (grad * summed[...], grad_product * values, grad_product * gate_in)
    for k, part in enumerate(parts):
        lanes = slice(k * channels, (k + 1) * channels)
        source = projected[:, lanes]
        sums[3:4, lanes] = jnp.sum(part, axis=0, keepdims=True)
        sums[0:1, lanes] = jnp.sum(part * source, axis=0, keepdims=True)
        running = short[0:1, lanes] * part
        for lag in (1, 2):
            kept = jnp.where(marks[:, lag : lag + 1] > 0, part, 0.0)
            sums[lag : lag + 1, lanes] = jnp.sum(
                kept * pltpu.roll(source, lag, 0), axis=0, keepdims=True
            )
            running = running + short[lag : lag + 1, lanes] * pltpu.roll(kept, length - lag, 0)
        sums[4:5, lanes] = jnp.sum(running, axis=0, keepdims=True)
        grad_low[:, lanes] = running.astype(jnp.bfloat16)
    sums[5:8] = jnp.zeros_like(sums[5:8])
    grad_first[...] = dot_nt(grad_low[...], proj[...]).astype(jnp.bfloat16)
    proj_grad[...] = dot_tn(first[...], grad_low[...]).astype(jnp.bfloat16)


def filter_back_kernel(
    grad_taps,
    features,
    embed,
    inner,
    columns,
    filter_weight,
    decay,
    pre,
    embed_grad,
    inner_grad,
    filter_grad,
    column_grad,
):
    length = features.shape[1]
    raw = grad_taps[...] * modulation(length, decay[...])
    back = exact(filter_weight[...], raw, ((1,), (1,)))
    column_grad[...] = jnp.zeros_like(column_grad)
    for i in (2, 1, 0):
        rate = columns[:, i : i + 1]
        angle = rate * pre[i]
        if i == 2:
            filter_grad[...] = exact(jnp.sin(angle), raw, ((1,), (0,)))
        act = back * jnp.cos(angle)
        column_grad[:, i : i + 1] = jnp.sum(act * pre[i], axis=1, keepdims=True)
        step = act * rate
        column_grad[:, 3 + i : 4 + i] = jnp.sum(step, axis=1, keepdims=True)
        if i == 0:
            embed_grad[...] = exact(features[...], step, ((1,), (1,)))
        else:
            below = jnp.sin(columns[:, i - 1 : i] * pre[i - 1])
            inner_grad[i - 1] = exact(below, step, ((1,), (1,)))
            back = exact(inner[i - 1], step, ((1,), (0,)))


def local_call(kernel, shapes, operands, name, cost, scratch=()):
    vmem = pl.BlockSpec(memory_space=pltpu.VMEM)
    return pl.pallas_call(
        kernel,
        out_shape=shapes,
        in_specs=[vmem] * len(operands),
        out_specs=[vmem] * len(shapes),
        scratch_shapes=list(scratch),
        compiler_params=pltpu.CompilerParams(vmem_limit_bytes=56 * 1024 * 1024),
        cost_estimate=pl.CostEstimate(flops=0, bytes_accessed=cost, transcendentals=0),
        name=name,
    )(*operands)


def shaped(shape, dtype=jnp.float32):
    return jax.ShapeDtypeStruct(shape, dtype)


def row_marks(segment, region):
    length = segment.shape[0]
    main = segment[region - 1]
    places = jnp.arange(length)

    def same(lag):
        return ((segment == jnp.roll(segment, lag)) & (places >= lag)).astype(jnp.int32)

    inside = segment == main
    head = jnp.where(inside | (places >= region), -1, segment)
    tail = jnp.where(inside | (places < length - region), -1, segment)
    none = jnp.zeros_like(segment)
    return jnp.stack(
        [inside.astype(jnp.int32), same(1), same(2), head, tail, none, none, none], axis=1
    )


def body(
    tokens,
    segment_ids,
    norm1_gain,
    norm1_bias,
    proj_weight,
    proj_bias,
    short_weight,
    short_bias,
    embed_weight,
    embed_bias,
    sine_freq,
    inner_weight,
    inner_bias,
    filter_weight,
    decay_rate,
    skip_gain,
    out_weight,
    out_bias,
    norm2_gain,
    norm2_bias,
    up_weight,
    up_bias,
    down_weight,
    down_bias,
    cotangent,
):
    row_count, shard_len, model_width = tokens.shape
    groups = lax.axis_size("tensor")
    rows = lax.axis_size("dp")
    place = lax.axis_index("tensor")
    row_place = lax.axis_index("dp")
    length = shard_len * groups
    channels = proj_weight.shape[2]
    units = up_weight.shape[1]
    channel_slice = channels // rows

    out_part = lax.dynamic_slice_in_dim(out_weight, row_place * channel_slice, channel_slice, 0)
    out_rows = -(-channel_slice // 16) * 16
    out_part = jnp.pad(out_part, ((0, out_rows - channel_slice), (0, 0)))

    tokens_f = tokens[0].astype(jnp.float32)
    normed1, norm1_back = jax.vjp(layer_norm, tokens_f, norm1_gain, norm1_bias)
    first_own = normed1.astype(jnp.bfloat16)
    first_all, out_all = start(first_own, out_part, 0)
    out_all = out_all[..., :channel_slice, :].reshape(groups, channels, model_width)
    flat_first = first_all.reshape(length, model_width)
    own_cotangent, flat_first = lax.optimization_barrier((cotangent[0], flat_first))
    all_cotangent = lax.all_gather(own_cotangent, "tensor", axis=0, tiled=True)

    region = shard_len
    main_transform = transform(length)
    small_transform = transform(region)
    transforms = main_transform + small_transform
    features = features_by_row()
    embed = jnp.pad(embed_weight, ((0, -FEAT % 8), (0, 0)))
    columns = jnp.stack(
        [*sine_freq, embed_bias, *inner_bias] + [jnp.zeros_like(embed_bias)] * 2, axis=1
    )
    decay = decay_rate[None]
    width = embed_weight.shape[1]
    pre, *taps_bins = local_call(
        taps_kernel,
        [
            shaped((3, width, length)),
            shaped((length, channels)),
            shaped((length, channels)),
            shaped((1, channels)),
            shaped((region, channels)),
            shaped((region, channels)),
            shaped((1, channels)),
        ],
        [features, embed, inner_weight, columns, filter_weight, decay, *transforms],
        "taps",
        20_000_000,
    )
    marks = row_marks(segment_ids[0], region)
    proj_flat = proj_weight.reshape(model_width, 3 * channels)
    short_flat = short_weight.reshape(3, 3 * channels)
    skip = skip_gain[None]
    gated_b, projected, mixed, summed = local_call(
        operator_kernel,
        [
            shaped((length, channels), jnp.bfloat16),
            shaped((length, 3 * channels)),
            shaped((length, 3 * channels)),
            shaped((length, channels)),
        ],
        [
            flat_first,
            proj_flat,
            proj_bias.reshape(1, 3 * channels),
            short_flat,
            short_bias.reshape(1, 3 * channels),
            skip,
            marks,
            *transforms,
            *taps_bins,
        ],
        "operator",
        50_000_000,
    )
    (gated_own,) = exchange([gated_b.reshape(groups, shard_len, channels)], ["swap"], 1)
    mixed_out = jnp.einsum("ztc,zcd->td", gated_own, out_all, preferred_element_type=jnp.float32)
    residual = tokens_f + mixed_out + out_bias
    normed2, norm2_back = jax.vjp(layer_norm, residual, norm2_gain, norm2_bias)
    second = normed2.astype(jnp.bfloat16)
    grad_out = own_cotangent.astype(jnp.float32)
    grad_down_bias = jnp.sum(grad_out, axis=0)
    (second_all,) = exchange([second], ["gather"], 2)
    mlp_partial, grad_partial, up_grad, down_grad, grad_up_bias = feed_forward(
        second_all.reshape(length, model_width), all_cotangent, up_weight, up_bias[None], down_weight
    )
    grad_up_bias = grad_up_bias[0]
    cut = units // 2
    grad_normed2, up_grad, down_first = row_reduce(
        grad_partial.reshape(groups, shard_len, model_width), [up_grad, down_grad[:cut]], 3
    )
    mlp_partial, grad_normed2 = lax.optimization_barrier((mlp_partial, grad_normed2))
    mlp_out = lax.psum_scatter(mlp_partial, "tensor", scatter_dimension=0, tiled=True)

    grad_residual, grad_norm2_gain, grad_norm2_bias = norm2_back(grad_normed2)
    grad_residual = grad_residual + grad_out
    grad_out_bias = jnp.sum(grad_residual, axis=0)
    grad_resid_b = grad_residual.astype(jnp.bfloat16)
    grad_gated_own = jnp.einsum(
        "td,zcd->ztc", grad_resid_b, out_all, preferred_element_type=jnp.float32
    ).astype(jnp.bfloat16)
    (grad_gated,) = exchange([grad_gated_own], ["swap"], 4)
    out_partial = jnp.einsum(
        "ztc,td->zcd", gated_own, grad_resid_b, preferred_element_type=jnp.float32
    ).astype(jnp.bfloat16)
    mlp_out = lax.psum_scatter(mlp_partial, "tensor", scatter_dimension=0, tiled=True)
    grad_first, proj_partial, grad_taps, sums, skip_sum = local_call(
        operator_back_kernel,
        [
            shaped((length, model_width), jnp.bfloat16),
            shaped((model_width, 3 * channels), jnp.bfloat16),
            shaped((length, channels)),
            shaped((8, 3 * channels)),
            shaped((1, channels)),
        ],
        [
            grad_gated.reshape(length, channels),
            flat_first,
            proj_flat,
            short_flat,
            skip,
            marks,
            *transforms,
            *taps_bins,
            projected,
            mixed,
            summed,
        ],
        "operator_back",
        90_000_000,
        [pltpu.VMEM((length, 3 * channels), jnp.bfloat16)],
    )
    grad_skip_gain = skip_sum[0]
    grad_short_weight = sums[:3].reshape(short_weight.shape)
    grad_short_bias = sums[3].reshape(short_bias.shape)
    grad_proj_bias = sums[4].reshape(proj_bias.shape)
    embed_grad, grad_inner_weight, grad_filter_weight, column_grad = local_call(
        filter_back_kernel,
        [
            shaped(embed.shape),
            shaped(inner_weight.shape),
            shaped(filter_weight.shape),
            shaped(columns.shape),
        ],
        [grad_taps, features, embed, inner_weight, columns, filter_weight, decay, pre],
        "filter_back",
        25_000_000,
    )
    grad_embed_weight = embed_grad[:FEAT]
    grad_sine_freq = column_grad[:, :3].T
    grad_embed_bias = column_grad[:, 3]
    grad_inner_bias = column_grad[:, 4:6].T
    mlp_out, grad_first = lax.optimization_barrier((mlp_out, grad_first))
    grad_normed1, proj_grad, down_last, out_grad = row_reduce(
        grad_first.reshape(groups, shard_len, model_width),
        [proj_partial, down_grad[cut:], out_partial],
        5,
    )
    grad_proj_weight = proj_grad.astype(jnp.float32).reshape(model_width, 3, channels)
    grad_out_weight = out_grad.astype(jnp.float32)
    grad_up_weight = up_grad.astype(jnp.float32)
    grad_down_weight = jnp.concatenate([down_first, down_last], axis=0).astype(jnp.float32)
    layer_out = (residual + mlp_out.astype(jnp.float32) + down_bias).astype(jnp.bfloat16)[None]
    grad_tokens, grad_norm1_gain, grad_norm1_bias = norm1_back(grad_normed1)
    grad_tokens = (grad_tokens + grad_residual)[None]

    everywhere = (
        grad_norm1_gain,
        grad_norm1_bias,
        grad_out_bias,
        grad_norm2_gain,
        grad_norm2_bias,
        grad_down_bias,
        grad_embed_weight,
        grad_embed_bias,
        grad_sine_freq,
        grad_inner_weight,
        grad_inner_bias,
    )
    rows_only = (
        grad_proj_bias,
        grad_short_weight,
        grad_short_bias,
        grad_filter_weight,
        grad_skip_gain,
        grad_up_bias,
    )

    def pack(parts):
        flat = jnp.concatenate([part.reshape(-1) for part in parts])
        return jnp.pad(flat, (0, -flat.size % 1024)).reshape(-1, 128)

    def unpack(packed, parts):
        flat = packed.reshape(-1)
        results = []
        start = 0
        for part in parts:
            results.append(flat[start : start + part.size].reshape(part.shape))
            start += part.size
        return results

    wide = pack(everywhere)
    narrow = pack(rows_only)
    packed = jnp.concatenate([wide, narrow], axis=0)
    packed = small_sum(packed, wide.shape[0], 6)
    wide, narrow = packed[: wide.shape[0]], packed[wide.shape[0] :]
    (
        grad_norm1_gain,
        grad_norm1_bias,
        grad_out_bias,
        grad_norm2_gain,
        grad_norm2_bias,
        grad_down_bias,
        grad_embed_weight,
        grad_embed_bias,
        grad_sine_freq,
        grad_inner_weight,
        grad_inner_bias,
    ) = unpack(wide, everywhere)
    (
        grad_proj_bias,
        grad_short_weight,
        grad_short_bias,
        grad_filter_weight,
        grad_skip_gain,
        grad_up_bias,
    ) = unpack(narrow, rows_only)
    return (
        layer_out,
        grad_tokens,
        grad_norm1_gain,
        grad_norm1_bias,
        grad_proj_weight,
        grad_proj_bias,
        grad_short_weight,
        grad_short_bias,
        grad_embed_weight,
        grad_embed_bias,
        grad_sine_freq,
        grad_inner_weight,
        grad_inner_bias,
        grad_filter_weight,
        grad_skip_gain,
        grad_out_weight,
        grad_out_bias,
        grad_norm2_gain,
        grad_norm2_bias,
        grad_up_weight,
        grad_up_bias,
        grad_down_weight,
        grad_down_bias,
    )


def solution(mesh):
    return jax.shard_map(
        body,
        mesh=mesh,
        in_specs=(
            P("dp", "tensor", None),
            P("dp", None),
            P(),
            P(),
            P(None, None, "tensor"),
            P(None, "tensor"),
            P(None, None, "tensor"),
            P(None, "tensor"),
            P(),
            P(),
            P(),
            P(),
            P(),
            P(None, "tensor"),
            P("tensor"),
            P("tensor"),
            P("tensor", None),
            P(),
            P(),
            P(),
            P(None, "tensor"),
            P("tensor"),
            P("tensor", None),
            P(),
            P("dp", "tensor", None),
        ),
        out_specs=(
            P("dp", "tensor", None),
            P("dp", "tensor", None),
            P(),
            P(),
            P(None, None, "tensor"),
            P(None, "tensor"),
            P(None, None, "tensor"),
            P(None, "tensor"),
            P(),
            P(),
            P(),
            P(),
            P(),
            P(None, "tensor"),
            P("tensor"),
            P("tensor", None),
            P(),
            P(),
            P(),
            P(None, "tensor"),
            P("tensor"),
            P("tensor", None),
            P(),
        ),
        check_vma=False,
    )
```

```python
import functools
import math

import jax
import jax.numpy as jnp
import ml_dtypes
import numpy as np
from jax import lax
from jax.experimental import pallas as pl
from jax.experimental.pallas import tpu as pltpu
from jax.sharding import PartitionSpec as P

FEAT = 33
SEQ = 1024
NDOC = 8


EPS = 1e-05
HIGH = lax.Precision.HIGHEST
SHIFT = 0.1
GELU_RATE = math.sqrt(2.0 / math.pi)
GELU_CUBE = 0.044715


def dot_nn(left, right):
    return jnp.dot(left, right, preferred_element_type=jnp.float32)


def dot_nt(left, right):
    return lax.dot_general(
        left, right, (((1,), (1,)), ((), ())), preferred_element_type=jnp.float32
    )


def dot_tn(left, right):
    return lax.dot_general(
        left, right, (((0,), (0,)), ((), ())), preferred_element_type=jnp.float32
    )


def transform(length):
    places = np.arange(length)
    angles = ((places[:, None] * places[None, :]) % (2 * length)) * (np.pi / length)
    return (
        jnp.asarray(np.cos(angles).astype(ml_dtypes.bfloat16)),
        jnp.asarray((-np.sin(angles)).astype(ml_dtypes.bfloat16)),
    )


def features_by_row():
    places = np.arange(SEQ, dtype=np.float32)
    bands = np.arange(1, (FEAT - 1) // 2 + 1, dtype=np.float32)
    angles = 2.0 * np.pi * np.arange(SEQ)[None, :] * bands[:, None].astype(np.float64) / SEQ
    rows = np.concatenate([(places / (SEQ - 1))[None, :], np.cos(angles), np.sin(angles)], axis=0)
    return jnp.asarray(rows.astype(np.float32))


def exact(left, right, contract):
    return lax.dot_general(
        left, right, (contract, ((), ())), precision=HIGH, preferred_element_type=jnp.float32
    )


def bin_scale(length):
    bins = lax.broadcasted_iota(jnp.int32, (length, 1), 0)
    return jnp.where(bins == 0, 0.5 / length, 1.0 / length)


def signs(length):
    places = lax.broadcasted_iota(jnp.int32, (length, 1), 0)
    return (1 - 2 * lax.rem(places, 2)).astype(jnp.float32)


def modulation(length, decay):
    places = lax.broadcasted_iota(jnp.int32, (length, 1), 0).astype(jnp.float32)
    return jnp.exp(-decay * (places / SEQ)) + SHIFT


def make_taps(
    features, embed, inner, columns, filter_weight, decay, transforms, pre, taps_bins
):
    cos_main, sin_main, cos_small, sin_small = transforms
    main_re, main_im, main_top, small_re, small_im, small_top = taps_bins
    length = features.shape[1]
    region = cos_small.shape[0]
    hidden = None
    for i in range(3):
        if i == 0:
            value = exact(embed[...], features[...], ((0,), (0,)))
        else:
            value = exact(inner[i - 1], hidden, ((0,), (0,)))
        value = value + columns[:, 3 + i : 4 + i]
        pre[i] = value
        hidden = jnp.sin(columns[:, i : i + 1] * value)
    taps = exact(hidden, filter_weight[...], ((0,), (0,)))
    taps = (taps * modulation(length, decay[...])).astype(jnp.bfloat16)
    scale = bin_scale(length)
    main_re[...] = dot_nn(cos_main[...], taps) * scale
    main_im[...] = dot_nn(sin_main[...], taps) * scale
    top = jnp.sum(taps.astype(jnp.float32) * signs(length), axis=0, keepdims=True)
    main_top[...] = top * (0.5 / length)
    short = taps[:region]
    scale = bin_scale(region)
    small_re[...] = dot_nn(cos_small[...], short) * scale
    small_im[...] = dot_nn(sin_small[...], short) * scale
    top = jnp.sum(short.astype(jnp.float32) * signs(region), axis=0, keepdims=True)
    small_top[...] = top * (0.5 / region)


def spectra(values, marks, cos_main, sin_main, cos_small, sin_small):
    length = values.shape[0]
    region = cos_small.shape[0]
    main = jnp.where(marks[:, 0:1] > 0, values, 0.0)
    top = jnp.sum(main * signs(length), axis=0, keepdims=True)
    main = main.astype(jnp.bfloat16)
    main_bins = (dot_nn(cos_main[...], main), dot_nn(sin_main[...], main), top)
    head, tail = values[:region], values[length - region :]
    head_slot, tail_slot = marks[:region, 3:4], marks[length - region :, 4:5]
    pieces = [
        jnp.where(head_slot == d, head, 0.0) + jnp.where(tail_slot == d, tail, 0.0)
        for d in range(NDOC)
    ]
    small = jnp.concatenate(pieces, axis=1)
    top = jnp.sum(small * signs(region), axis=0, keepdims=True)
    small = small.astype(jnp.bfloat16)
    small_bins = (dot_nn(cos_small[...], small), dot_nn(sin_small[...], small), top)
    return main_bins, small_bins


def times(left, right, conjugate):
    left_re, left_im, left_top = left
    right_re, right_im, right_top = right
    if conjugate:
        return (
            left_re * right_re + left_im * right_im,
            left_re * right_im - left_im * right_re,
            left_top * right_top,
        )
    return (
        left_re * right_re - left_im * right_im,
        left_re * right_im + left_im * right_re,
        left_top * right_top,
    )


def from_bins(bins, cos_rows, sin_rows):
    real, imag, top = bins
    return (
        dot_nn(cos_rows[...], real.astype(jnp.bfloat16))
        + dot_nn(sin_rows[...], imag.astype(jnp.bfloat16))
        + signs(real.shape[0]) * top
    )


def beside(part):
    return jnp.concatenate([part] * NDOC, axis=1)


def filtered(main_bins, small_bins, taps_main, taps_small, marks, transforms, conjugate):
    cos_main, sin_main, cos_small, sin_small = transforms
    main = from_bins(times(taps_main, main_bins, conjugate), cos_main, sin_main)
    taps_wide = tuple(beside(part) for part in taps_small)
    small = from_bins(times(taps_wide, small_bins, conjugate), cos_small, sin_small)
    length, channels = main.shape
    region = small.shape[0]
    main = jnp.where(marks[:, 0:1] > 0, main, 0.0)
    head, tail = main[:region], main[length - region :]
    head_slot, tail_slot = marks[:region, 3:4], marks[length - region :, 4:5]
    for d in range(NDOC):
        piece = small[:, d * channels : (d + 1) * channels]
        head = head + jnp.where(head_slot == d, piece, 0.0)
        tail = tail + jnp.where(tail_slot == d, piece, 0.0)
    return jnp.concatenate([head, main[region : length - region], tail], axis=0)


def filter_back_kernel(
    grad_taps,
    features,
    embed,
    inner,
    columns,
    filter_weight,
    decay,
    pre,
    embed_grad,
    inner_grad,
    filter_grad,
    column_grad,
):
    length = features.shape[1]
    raw = grad_taps[...] * modulation(length, decay[...])
    back = exact(filter_weight[...], raw, ((1,), (1,)))
    column_grad[...] = jnp.zeros_like(column_grad)
    for i in (2, 1, 0):
        rate = columns[:, i : i + 1]
        angle = rate * pre[i]
        if i == 2:
            filter_grad[...] = exact(jnp.sin(angle), raw, ((1,), (0,)))
        act = back * jnp.cos(angle)
        column_grad[:, i : i + 1] = jnp.sum(act * pre[i], axis=1, keepdims=True)
        step = act * rate
        column_grad[:, 3 + i : 4 + i] = jnp.sum(step, axis=1, keepdims=True)
        if i == 0:
            embed_grad[...] = exact(features[...], step, ((1,), (1,)))
        else:
            below = jnp.sin(columns[:, i - 1 : i] * pre[i - 1])
            inner_grad[i - 1] = exact(below, step, ((1,), (1,)))
            back = exact(inner[i - 1], step, ((1,), (0,)))


def shaped(shape, dtype=jnp.float32):
    return jax.ShapeDtypeStruct(shape, dtype)


def row_marks(segment, marks, region):
    ids = segment[...]
    length = ids.shape[0]
    places = lax.broadcasted_iota(jnp.int32, ids.shape, 0)
    inside = ids == ids[region - 1 : region]
    marks[:, 0:1] = inside.astype(jnp.int32)
    for lag in (1, 2):
        same = (ids == pltpu.roll(ids, lag, 0)) & (places >= lag)
        marks[:, lag : lag + 1] = same.astype(jnp.int32)
    marks[:, 3:4] = jnp.where(inside | (places >= region), -1, ids)
    marks[:, 4:5] = jnp.where(inside | (places < length - region), -1, ids)


BY_INDEX = pl.DeviceIdType.MESH


def greet(devices):
    barrier = pltpu.get_barrier_semaphore()
    for device in devices:
        pl.semaphore_signal(barrier, inc=1, device_id=device, device_id_type=BY_INDEX)
    pl.semaphore_wait(barrier, len(devices))


def remote(source, target, send_sem, recv_sem, device):
    return pltpu.make_async_remote_copy(
        src_ref=source,
        dst_ref=target,
        send_sem=send_sem,
        recv_sem=recv_sem,
        device_id=device,
        device_id_type=BY_INDEX,
    )


def tensor_peers():
    count = lax.axis_size("tensor")
    me = lax.axis_index("tensor")
    return [lax.rem(me + k, count) for k in range(1, count)]


def tensor_devices():
    return [{"tensor": peer} for peer in tensor_peers()]


def sibling():
    me = lax.axis_index("dp")
    return {"dp": me + 1 - 2 * lax.rem(me, 2)}


def chip_peers():
    chips = lax.axis_size("dp") // 2
    me = lax.axis_index("dp")
    core = lax.rem(me, 2)
    result = []
    for k in range(1, chips):
        chip = lax.rem(me // 2 + k, chips)
        result.append((chip, 2 * chip + core))
    return result


def chip_devices():
    return [{"dp": mate} for unused_chip, mate in chip_peers()]


def spread(source, target, sems, devices):
    copies = []
    for k, device in enumerate(devices):
        copies.append(
            remote(
                source(k) if callable(source) else source,
                target(k) if callable(target) else target,
                sems.at[0, k],
                sems.at[1, k],
                device,
            )
        )
        copies[-1].start()
    return copies


def wait_all(copies):
    for copy in copies:
        copy.wait()


def span(index, size):
    return pl.ds(pl.multiple_of(index * size, 16), size)


class Chain:
    def __init__(self, slots, send_sems, recv_sems):
        self.slots, self.send_sems, self.recv_sems = slots, send_sems, recv_sems
        self.count = lax.axis_size("tensor")
        self.me = lax.axis_index("tensor")

    def copy(self, block, side):
        step = 1 - 2 * side
        return remote(
            self.slots.at[block],
            self.slots.at[block],
            self.send_sems.at[side, block],
            self.recv_sems.at[block],
            {"tensor": lax.rem(self.me + step + self.count, self.count)},
        )

    def advance(self, step):
        lower, upper = self.me - step, self.me + step

        @pl.when(lower >= 0)
        def _():
            @pl.when(step > 0)
            def _():
                self.copy(lower, 0).wait_recv()

            @pl.when(self.me < self.count - 1)
            def _():
                self.copy(lower, 0).start()

        @pl.when(upper < self.count)
        def _():
            @pl.when(step > 0)
            def _():
                self.copy(upper, 1).wait_recv()

            @pl.when(self.me > 0)
            def _():
                self.copy(upper, 1).start()

    def finish(self):
        for block in range(self.count):

            @pl.when((self.me < self.count - 1) & (block <= self.me))
            def _():
                self.copy(block, 0).wait_send()

            @pl.when((self.me > 0) & (block >= self.me))
            def _():
                self.copy(block, 1).wait_send()


def normalised(values):
    average = jnp.mean(values, axis=-1, keepdims=True)
    centered = values - average
    variance = jnp.mean(centered * centered, axis=-1, keepdims=True)
    rate = lax.rsqrt(variance + EPS)
    return centered * rate, rate


def norm_back(grad, gain, hat, rate):
    e = grad * gain
    return rate * (
        e
        - jnp.mean(e, axis=-1, keepdims=True)
        - hat * jnp.mean(e * hat, axis=-1, keepdims=True)
    )


def column_sum(values):
    return jnp.sum(values, axis=0, keepdims=True)


def front_kernel(
    tokens,
    gain,
    shift,
    part,
    segment,
    features,
    embed,
    inner,
    columns,
    filter_weight,
    decay,
    proj,
    proj_bias,
    short,
    short_bias,
    skip,
    cos_main,
    sin_main,
    cos_small,
    sin_small,
    first_all,
    part_all,
    pre,
    main_re,
    main_im,
    main_top,
    small_re,
    small_im,
    small_top,
    gated_own,
    projected,
    mixed,
    summed,
    gated,
    marks,
    local_sems,
    first_send,
    first_recv,
    part_sems,
    chip_sems,
    core_sems,
    gated_sems,
):
    me = lax.axis_index("tensor")
    count = lax.axis_size("tensor")
    place = lax.axis_index("dp")
    core = lax.rem(place, 2)
    chip = place // 2
    peers = tensor_peers()
    shard = tokens.shape[0]
    channels = skip.shape[1]
    taps_bins = (main_re, main_im, main_top, small_re, small_im, small_top)
    transforms = (cos_main, sin_main, cos_small, sin_small)
    greet(tensor_devices() + [sibling()] + chip_devices())

    hat, unused_rate = normalised(tokens[...].astype(jnp.float32))
    first_all[me] = (hat * gain[...] + shift[...]).astype(jnp.bfloat16)
    chain = Chain(first_all, first_send, first_recv)
    chain.advance(0)
    own = pltpu.make_async_copy(part, part_all.at[me, chip, core], local_sems.at[0])
    own.start()
    parts = spread(part, part_all.at[me, chip, core], part_sems, tensor_devices())

    def project(block):
        rows = pl.ds(pl.multiple_of(block * shard, shard), shard)
        for k in range(3):
            lanes = slice(k * channels, (k + 1) * channels)
            projected[rows, lanes] = dot_nn(first_all[block], proj[k]) + proj_bias[:, lanes]

    project(me)
    make_taps(
        features, embed, inner, columns, filter_weight, decay, transforms, pre, taps_bins
    )
    row_marks(segment, marks, cos_small.shape[0])

    def turn(step, carry):
        chain.advance(step)

        def side(index, carry):
            block = me + step * (2 * index - 1)

            @pl.when((block >= 0) & (block < count))
            def _():
                project(block)

            return carry

        return lax.fori_loop(0, 2, side, carry)

    lax.fori_loop(1, 2, turn, 0)
    own.wait()
    wait_all(parts)
    held = part_all.at[:, chip, core]
    parts = spread(held, held, chip_sems, chip_devices())
    lax.fori_loop(2, count, turn, 0)
    wait_all(parts)
    held = part_all.at[:, :, core]
    parts = spread(held, held, core_sems, [sibling()])

    for k in range(3):
        lanes = slice(k * channels, (k + 1) * channels)
        value = projected[:, lanes]
        running = short_bias[:, lanes] + short[0:1, lanes] * value
        for lag in (1, 2):
            moved = jnp.where(marks[:, lag : lag + 1] > 0, pltpu.roll(value, lag, 0), 0.0)
            running = running + short[lag : lag + 1, lanes] * moved
        mixed[:, lanes] = running
    product = mixed[:, 2 * channels :] * mixed[:, channels : 2 * channels]
    low = product.astype(jnp.bfloat16).astype(jnp.float32)
    main_bins, small_bins = spectra(low, marks, *transforms)
    result = filtered(
        main_bins,
        small_bins,
        (main_re[...], main_im[...], main_top[...]),
        (small_re[...], small_im[...], small_top[...]),
        marks,
        transforms,
        False,
    )
    total = result + skip[...] * product
    summed[...] = total
    gated[...] = (total * mixed[:, :channels]).astype(jnp.bfloat16).reshape(gated.shape)
    swapped = spread(
        lambda k: gated.at[peers[k]], gated_own.at[me], gated_sems, tensor_devices()
    )
    gated_own[me] = gated[me]
    chain.finish()
    wait_all(parts + swapped)


def middle_kernel(
    gated,
    out,
    tokens,
    vectors,
    cotangent,
    up,
    bias,
    down,
    residual,
    grad_residual,
    mlp,
    up_grad,
    down_grad,
    bias_grad,
    grad_gated,
    out_grad,
    sums,
    second,
    active,
    low,
    parting,
    arriving,
    own_part,
    second_send,
    second_recv,
    part_send,
    part_recv,
):
    me = lax.axis_index("tensor")
    count = lax.axis_size("tensor")
    shard, width = tokens.shape
    units = up.shape[1]
    greet(tensor_devices())
    base = tokens[...].astype(jnp.float32) + vectors[0:1]
    for block in range(count):
        base = base + dot_nn(gated[block], out[block])
    residual[...] = base
    hat, unused_rate = normalised(base)
    second[me] = (hat * vectors[1:2] + vectors[2:3]).astype(jnp.bfloat16)
    chain = Chain(second, second_send, second_recv)
    bias_grad[...] = jnp.zeros_like(bias_grad)

    def sent(block):
        return remote(
            parting.at[block],
            arriving.at[me],
            part_send.at[block],
            part_recv.at[me],
            {"tensor": block},
        )

    def work(block):
        cut = units // 2
        mlp_part = None
        for lanes in (slice(0, cut), slice(cut, units)):
            hidden = dot_nn(second[block], up[:, lanes]) + bias[:, lanes]
            cube = GELU_CUBE * hidden * hidden
            slope = jnp.tanh(GELU_RATE * hidden * (1.0 + cube))
            gate = 0.5 * (1.0 + slope)
            active[block, :, lanes] = (hidden * gate).astype(jnp.bfloat16)
            rate = gate + (0.5 * GELU_RATE) * hidden * (1.0 - slope * slope) * (1.0 + 3.0 * cube)
            grad_hidden = dot_nt(cotangent[block], down[lanes]) * rate
            bias_grad[:, lanes] += column_sum(grad_hidden)
            low[block, :, lanes] = grad_hidden.astype(jnp.bfloat16)
        part = dot_nt(low[block], up[...])

        @pl.when(block == me)
        def _():
            own_part[...] = part

        @pl.when(block != me)
        def _():
            parting[block] = part.astype(jnp.bfloat16)
            sent(block).start()

        mlp[block] = dot_nn(active[block], down[...]).astype(jnp.bfloat16)

    def turn(step, carry):
        chain.advance(step)

        def side(index, carry):
            block = me + step * (2 * index - 1)

            @pl.when((block >= 0) & (block < count) & ((step > 0) | (index == 0)))
            def _():
                work(block)

            return carry

        return lax.fori_loop(0, 2, side, carry)

    lax.fori_loop(0, count, turn, 0)
    tokens_all = count * shard
    up_grad[...] = dot_tn(
        second[...].reshape(tokens_all, width), low[...].reshape(tokens_all, units)
    ).astype(jnp.bfloat16)
    down_grad[...] = dot_tn(
        active[...].reshape(tokens_all, units), cotangent[...].reshape(tokens_all, width)
    ).astype(jnp.bfloat16)
    for peer in tensor_peers():
        remote(
            parting.at[peer], arriving.at[peer], part_send.at[peer], part_recv.at[peer], {"tensor": peer}
        ).wait_recv()
        own_part[...] += arriving[peer].astype(jnp.float32)
    grad_normed = own_part[...]
    hat, rate = normalised(residual[...])
    grad_out = cotangent[me].astype(jnp.float32)
    grad = grad_out + norm_back(grad_normed, vectors[1:2], hat, rate)
    grad_residual[...] = grad
    sums[...] = jnp.zeros_like(sums)
    sums[0:1] = column_sum(grad_normed * hat)
    sums[1:2] = column_sum(grad_normed)
    sums[2:3] = column_sum(grad)
    sums[3:4] = column_sum(grad_out)
    grad_low = grad.astype(jnp.bfloat16)
    for block in range(count):
        grad_gated[block] = dot_nt(grad_low, out[block]).astype(jnp.bfloat16)
        out_grad[block] = dot_tn(gated[block], grad_low).astype(jnp.bfloat16)
    chain.finish()
    for peer in tensor_peers():
        sent(peer).wait_send()


class RowReduce:
    def __init__(self, source, part, refs):
        half, core_recv, chip_recv, load_sem, core_sems, chip_sems = refs[:6]
        self.source, self.part, self.half = source, part, half
        self.core_recv, self.chip_recv = core_recv, chip_recv
        self.load_sem, self.core_sems, self.chip_sems = load_sem, core_sems, chip_sems
        self.across = tuple(refs[6:])
        place = lax.axis_index("dp")
        self.core, self.chip = lax.rem(place, 2), place // 2
        self.chips = lax.axis_size("dp") // 2
        self.rows = half.shape[-2]
        self.size = self.rows // self.chips

    def pair(self):
        self.load = pltpu.make_async_copy(
            self.source.at[..., span(self.core, self.rows), :], self.half, self.load_sem.at[0]
        )
        self.load.start()
        self.copies = spread(
            self.source.at[..., span(1 - self.core, self.rows), :],
            self.core_recv,
            self.core_sems,
            [sibling()],
        )

    def plane(self):
        self.load.wait()
        wait_all(self.copies)
        self.half[...] = (
            self.half[...].astype(jnp.float32) + self.core_recv[...].astype(jnp.float32)
        ).astype(self.half.dtype)
        mates = chip_peers()
        self.copies = spread(
            lambda k: self.half.at[..., span(mates[k][0], self.size), :],
            lambda k: self.chip_recv.at[k],
            self.chip_sems,
            chip_devices(),
        )

    def gathered(self):
        value = self.half[..., span(self.chip, self.size), :].astype(jnp.float32)
        for k, copy in enumerate(self.copies):
            copy.wait()
            value = value + self.chip_recv[k].astype(jnp.float32)
        return value

    def cross(self):
        held, held_recv, sems = self.across
        held[...] = self.gathered().astype(held.dtype)
        peers = tensor_peers()
        self.copies = spread(
            lambda k: held.at[peers[k]], lambda k: held_recv.at[k], sems, tensor_devices()
        )

    def crossed(self):
        held, held_recv, sems = self.across
        value = held[lax.axis_index("tensor")].astype(jnp.float32)
        for k, copy in enumerate(self.copies):
            copy.wait()
            value = value + held_recv[k].astype(jnp.float32)
        return value

    def finish(self):
        value = self.crossed() if self.across else self.gathered()
        self.part[...] = value.astype(self.part.dtype)


def row_reduce_scratch(shape, chips):
    rows, columns = shape[-2:]
    lead = tuple(shape[:-2])
    size = rows // 2 // chips
    low = jnp.bfloat16
    scratch = [
        pltpu.VMEM(lead + (rows // 2, columns), low),
        pltpu.VMEM(lead + (rows // 2, columns), low),
        pltpu.VMEM((chips - 1,) + lead + (size, columns), low),
        pltpu.SemaphoreType.DMA((1,)),
        pltpu.SemaphoreType.DMA((2, 1)),
        pltpu.SemaphoreType.DMA((2, chips - 1)),
    ]
    if lead:
        scratch += [
            pltpu.VMEM(lead + (size, columns), low),
            pltpu.VMEM((lead[0] - 1, size, columns), low),
            pltpu.SemaphoreType.DMA((2, lead[0] - 1)),
        ]
    return scratch


class RowGather:
    def __init__(self, part, total, refs):
        self.part, self.total = part, total
        self.chip_sems, self.core_sems = refs
        place = lax.axis_index("dp")
        core, chip = lax.rem(place, 2), place // 2
        chips = lax.axis_size("dp") // 2
        self.mine = span(core * chips + chip, part.shape[0])
        self.half = span(core, part.shape[0] * chips)

    def plane(self):
        own = self.total.at[self.mine]
        own[...] = self.part[...]
        self.copies = spread(own, own, self.chip_sems, chip_devices())

    def pair(self):
        wait_all(self.copies)
        own = self.total.at[self.half]
        self.copies = spread(own, own, self.core_sems, [sibling()])

    def finish(self):
        wait_all(self.copies)


def row_gather_scratch(chips):
    return [pltpu.SemaphoreType.DMA((2, chips - 1)), pltpu.SemaphoreType.DMA((2, 1))]


def back_kernel(
    grad_blocks,
    mlp,
    up_grad,
    down_grad,
    out_grad,
    proj,
    short,
    skip,
    segment,
    features,
    embed,
    inner,
    columns,
    filter_weight,
    decay,
    pre,
    cos_main,
    sin_main,
    cos_small,
    sin_small,
    main_re,
    main_im,
    main_top,
    small_re,
    small_im,
    small_top,
    projected,
    mixed,
    summed,
    grad_first,
    grad_low,
    sums,
    skip_sum,
    mlp_sum,
    up_part,
    down_part,
    out_part,
    embed_grad,
    inner_grad,
    filter_grad,
    column_grad,
    grad_gated,
    grad_taps,
    marks,
    mlp_own,
    mlp_recv,
    local_sems,
    gated_sems,
    mlp_sems,
    *scratch,
):
    me = lax.axis_index("tensor")
    count = lax.axis_size("tensor")
    peers = tensor_peers()
    channels = skip.shape[1]
    length = projected.shape[0]
    region = cos_small.shape[0]
    shard = length // count
    transforms = (cos_main, sin_main, cos_small, sin_small)
    greet(tensor_devices() + [sibling()] + chip_devices())
    up_row = RowReduce(up_grad, up_part, scratch[:6])
    down_row = RowReduce(down_grad, down_part, scratch[6:12])
    out_row = RowReduce(out_grad, out_part, scratch[12:])
    weights = (out_row, up_row, down_row)

    own = pltpu.make_async_copy(grad_blocks.at[me], grad_gated.at[me], local_sems.at[0])
    own.start()
    arriving = spread(
        lambda k: grad_blocks.at[peers[k]], grad_gated.at[me], gated_sems, tensor_devices()
    )
    for weight in weights:
        weight.pair()
    own_mlp = pltpu.make_async_copy(mlp.at[me], mlp_own, local_sems.at[1])
    own_mlp.start()
    row_marks(segment, marks, region)
    gate_out = mixed[:, :channels]
    gate_in = mixed[:, channels : 2 * channels]
    values = mixed[:, 2 * channels :]
    product = values * gate_in
    low = product.astype(jnp.bfloat16).astype(jnp.float32)
    value_main, value_small = spectra(low, marks, *transforms)
    for weight in weights:
        weight.plane()
    own.wait()
    wait_all(arriving)
    mlps = spread(
        lambda k: mlp.at[peers[k]], lambda k: mlp_recv.at[k], mlp_sems, tensor_devices()
    )
    grad = grad_gated[...].reshape(length, channels).astype(jnp.float32)
    grad_summed = grad * gate_out
    skip_sum[...] = column_sum(grad_summed * product)
    low = grad_summed.astype(jnp.bfloat16).astype(jnp.float32)
    grad_main, grad_small = spectra(low, marks, *transforms)
    real, imag, top = times(value_main, grad_main, True)
    scale = bin_scale(length)
    taps = from_bins((real * scale, imag * scale, top * (0.5 / length)), cos_main, sin_main)
    scale = bin_scale(region)
    real, imag, top = (
        sum(part[:, d * channels : (d + 1) * channels] for d in range(NDOC))
        for part in times(value_small, grad_small, True)
    )
    taps_small = from_bins((real * scale, imag * scale, top * (0.5 / region)), cos_small, sin_small)
    grad_taps[:region] = taps[:region] + taps_small
    grad_taps[region:] = taps[region:]
    out_row.cross()
    result = filtered(
        grad_main,
        grad_small,
        (main_re[...], main_im[...], main_top[...]),
        (small_re[...], small_im[...], small_top[...]),
        marks,
        transforms,
        True,
    )
    grad_product = result + grad_summed * skip[...]
    parts = (grad * summed[...], grad_product * values, grad_product * gate_in)
    for k, part in enumerate(parts):
        lanes = slice(k * channels, (k + 1) * channels)
        source = projected[:, lanes]
        sums[3:4, lanes] = column_sum(part)
        sums[0:1, lanes] = column_sum(part * source)
        running = short[0:1, lanes] * part
        for lag in (1, 2):
            kept = jnp.where(marks[:, lag : lag + 1] > 0, part, 0.0)
            sums[lag : lag + 1, lanes] = column_sum(kept * pltpu.roll(source, lag, 0))
            running = running + short[lag : lag + 1, lanes] * pltpu.roll(kept, length - lag, 0)
        sums[4:5, lanes] = column_sum(running)
        grad_low[:, lanes] = running.astype(jnp.bfloat16)
    sums[5:8] = jnp.zeros_like(sums[5:8])
    for block in range(count):
        rows = slice(block * shard, (block + 1) * shard)
        total = dot_nt(grad_low[rows, :channels], proj[0])
        for k in (1, 2):
            total = total + dot_nt(grad_low[rows, k * channels : (k + 1) * channels], proj[k])
        grad_first[block] = total.astype(jnp.bfloat16)
    filter_back_kernel(
        grad_taps,
        features,
        embed,
        inner,
        columns,
        filter_weight,
        decay,
        pre,
        embed_grad,
        inner_grad,
        filter_grad,
        column_grad,
    )
    for weight in weights:
        weight.finish()
    own_mlp.wait()
    total = mlp_own[...].astype(jnp.float32)
    for k, copy in enumerate(mlps):
        copy.wait()
        total = total + mlp_recv[k].astype(jnp.float32)
    mlp_sum[...] = total


class SmallSum:
    def __init__(self, packed, result, refs):
        self.packed, self.result = packed, result
        (
            self.core_recv,
            self.chip_slots,
            self.group_slots,
            self.core_sems,
            self.chip_sems,
            self.group_sems,
        ) = refs
        self.me = lax.axis_index("tensor")
        self.chip = lax.axis_index("dp") // 2
        self.wide = self.group_slots.shape[1]

    def pair(self):
        self.copies = spread(self.packed, self.core_recv, self.core_sems, [sibling()])

    def plane(self):
        wait_all(self.copies)
        self.chip_slots[self.chip] = self.packed[...] + self.core_recv[...]
        own = self.chip_slots.at[self.chip]
        self.copies = spread(own, own, self.chip_sems, chip_devices())

    def tensor(self):
        wait_all(self.copies)
        total = self.chip_slots[0]
        for i in range(1, self.chip_slots.shape[0]):
            total = total + self.chip_slots[i]
        self.result[...] = total
        self.group_slots[self.me] = total[: self.wide]
        own = self.group_slots.at[self.me]
        self.copies = spread(own, own, self.group_sems, tensor_devices())

    def finish(self):
        wait_all(self.copies)
        total = self.group_slots[0]
        for i in range(1, self.group_slots.shape[0]):
            total = total + self.group_slots[i]
        self.result[: self.wide] = total


def small_sum_scratch(shape, wide, chips, groups):
    rows, columns = shape
    return [
        pltpu.VMEM((rows, columns), jnp.float32),
        pltpu.VMEM((chips, rows, columns), jnp.float32),
        pltpu.VMEM((groups, wide, columns), jnp.float32),
        pltpu.SemaphoreType.DMA((2, 1)),
        pltpu.SemaphoreType.DMA((2, chips - 1)),
        pltpu.SemaphoreType.DMA((2, groups - 1)),
    ]


def final_kernel(
    grad_first,
    first,
    grad_low,
    tokens,
    gain,
    grad_residual,
    packed,
    up_part,
    down_part,
    out_part,
    grad_tokens,
    proj_sum,
    norm_sums,
    packed_sum,
    up_sum,
    down_sum,
    out_sum,
    proj_grad,
    proj_part,
    norm_own,
    block_recv,
    block_sems,
    *scratch,
):
    me = lax.axis_index("tensor")
    peers = tensor_peers()
    greet(tensor_devices() + [sibling()] + chip_devices())
    blocks = spread(
        lambda k: grad_first.at[peers[k]], lambda k: block_recv.at[k], block_sems, tensor_devices()
    )
    row = RowReduce(proj_grad, proj_part, scratch[:6])
    proj_all = RowGather(proj_part, proj_sum, scratch[6:8])
    gathers = [
        RowGather(up_part, up_sum, scratch[8:10]),
        RowGather(down_part, down_sum, scratch[10:12]),
        RowGather(out_part, out_sum, scratch[12:14]),
    ]
    small = SmallSum(packed, packed_sum, scratch[14:20])
    norms = SmallSum(norm_own, norm_sums, scratch[20:26])
    small.pair()
    length = grad_low.shape[0]
    proj_grad[...] = dot_tn(first[...].reshape(length, first.shape[2]), grad_low[...]).astype(
        jnp.bfloat16
    )
    row.pair()
    small.plane()
    row.plane()
    for gather in gathers:
        gather.plane()
    hat, rate = normalised(tokens[...].astype(jnp.float32))
    small.tensor()
    row.finish()
    proj_all.plane()
    small.finish()
    for gather in gathers:
        gather.pair()
    proj_all.pair()
    grad = grad_first[me].astype(jnp.float32)
    for k, copy in enumerate(blocks):
        copy.wait()
        grad = grad + block_recv[k].astype(jnp.float32)
    norm_own[...] = jnp.zeros_like(norm_own)
    norm_own[0:1] = column_sum(grad * hat)
    norm_own[1:2] = column_sum(grad)
    norms.pair()
    grad_tokens[...] = grad_residual[...] + norm_back(grad, gain[...], hat, rate)
    norms.plane()
    norms.tensor()
    norms.finish()
    for gather in gathers + [proj_all]:
        gather.finish()


def communicate(kernel, shapes, operands, anywhere, scratch, channel, name):
    vmem = pl.BlockSpec(memory_space=pltpu.VMEM)
    free = pl.BlockSpec(memory_space=pl.ANY)
    return pl.pallas_call(
        kernel,
        out_shape=shapes,
        in_specs=[free if i in anywhere[0] else vmem for i in range(len(operands))],
        out_specs=[free if i in anywhere[1] else vmem for i in range(len(shapes))],
        scratch_shapes=scratch,
        compiler_params=pltpu.CompilerParams(
            collective_id=channel, has_side_effects=True, vmem_limit_bytes=60 * 1024 * 1024
        ),
        cost_estimate=pl.CostEstimate(flops=0, bytes_accessed=200_000_000, transcendentals=0),
        name=name,
    )(*operands)


def body(
    tokens,
    segment_ids,
    norm1_gain,
    norm1_bias,
    proj_weight,
    proj_bias,
    short_weight,
    short_bias,
    embed_weight,
    embed_bias,
    sine_freq,
    inner_weight,
    inner_bias,
    filter_weight,
    decay_rate,
    skip_gain,
    out_weight,
    out_bias,
    norm2_gain,
    norm2_bias,
    up_weight,
    up_bias,
    down_weight,
    down_bias,
    cotangent,
):
    row_count, shard_len, model_width = tokens.shape
    groups = lax.axis_size("tensor")
    rows = lax.axis_size("dp")
    place = lax.axis_index("tensor")
    row_place = lax.axis_index("dp")
    length = shard_len * groups
    channels = proj_weight.shape[2]
    units = up_weight.shape[1]
    channel_slice = channels // rows

    out_part = lax.dynamic_slice_in_dim(out_weight, row_place * channel_slice, channel_slice, 0)
    out_rows = -(-channel_slice // 16) * 16
    out_part = jnp.pad(out_part, ((0, out_rows - channel_slice), (0, 0)))

    low = jnp.bfloat16
    region = shard_len
    chips = rows // 2
    proj_columns = 3 * channels
    transforms = transform(length) + transform(region)
    features = features_by_row()
    columns = jnp.stack(
        [*sine_freq, embed_bias, *inner_bias] + [jnp.zeros_like(embed_bias)] * 2, axis=1
    )
    decay = decay_rate[None]
    width = embed_weight.shape[1]
    segment = segment_ids.reshape(length, 1)
    proj = proj_weight.transpose(1, 0, 2)
    cotangent = cotangent[0]
    all_cotangent = lax.all_gather(cotangent, "tensor")
    short_flat = short_weight.reshape(3, proj_columns)
    skip = skip_gain[None]
    filter_parts = [features, embed_weight, inner_weight, columns, filter_weight, decay]
    semaphores = pltpu.SemaphoreType.DMA
    blocked = (groups, shard_len, model_width)
    (
        first_all,
        out_all,
        pre,
        main_re,
        main_im,
        main_top,
        small_re,
        small_im,
        small_top,
        gated_own,
        projected,
        mixed,
        summed,
    ) = communicate(
        front_kernel,
        [
            shaped(blocked, low),
            shaped((groups, chips, 2) + out_part.shape, low),
            shaped((3, width, length)),
            shaped((length, channels)),
            shaped((length, channels)),
            shaped((1, channels)),
            shaped((region, channels)),
            shaped((region, channels)),
            shaped((1, channels)),
            shaped((groups, shard_len, channels), low),
            shaped((length, proj_columns)),
            shaped((length, proj_columns)),
            shaped((length, channels)),
        ],
        [
            tokens[0],
            norm1_gain[None],
            norm1_bias[None],
            out_part,
            segment,
            *filter_parts,
            proj,
            proj_bias.reshape(1, proj_columns),
            short_flat,
            short_bias.reshape(1, proj_columns),
            skip,
            *transforms,
        ],
        ((3,), (1,)),
        [
            pltpu.VMEM((groups, shard_len, channels), low),
            pltpu.VMEM((length, 8), jnp.int32),
            semaphores((1,)),
            semaphores((2, groups)),
            semaphores((groups,)),
            semaphores((2, groups - 1)),
            semaphores((2, chips - 1)),
            semaphores((2, 1)),
            semaphores((2, groups - 1)),
        ],
        0,
        "front",
    )
    taps_bins = (main_re, main_im, main_top, small_re, small_im, small_top)
    out_all = out_all[..., :channel_slice, :].reshape(groups, channels, model_width)
    vectors = jnp.stack([out_bias, norm2_gain, norm2_bias])
    (
        residual,
        grad_residual,
        mlp_partial,
        up_grad,
        down_grad,
        grad_up_bias,
        grad_gated,
        out_grad,
        middle_sums,
    ) = communicate(
        middle_kernel,
        [
            shaped((shard_len, model_width)),
            shaped((shard_len, model_width)),
            shaped(blocked, low),
            shaped((model_width, units), low),
            shaped((units, model_width), low),
            shaped((1, units)),
            shaped((groups, shard_len, channels), low),
            shaped((groups, channels, model_width), low),
            shaped((8, model_width)),
        ],
        [
            gated_own,
            out_all,
            tokens[0],
            vectors,
            all_cotangent,
            up_weight,
            up_bias[None],
            down_weight,
        ],
        ((), ()),
        [
            pltpu.VMEM(blocked, low),
            pltpu.VMEM((groups, shard_len, units), low),
            pltpu.VMEM((groups, shard_len, units), low),
            pltpu.VMEM(blocked, low),
            pltpu.VMEM(blocked, low),
            pltpu.VMEM((shard_len, model_width), jnp.float32),
            semaphores((2, groups)),
            semaphores((groups,)),
            semaphores((groups,)),
            semaphores((groups,)),
        ],
        1,
        "middle",
    )
    fold = max(1, 32 * chips // channels)
    out_grad = out_grad.reshape(groups, channels * fold, model_width // fold)
    (
        grad_first,
        grad_low,
        back_sums,
        skip_sum,
        mlp_out,
        up_part,
        down_part,
        out_part,
        embed_grad,
        grad_inner_weight,
        grad_filter_weight,
        column_grad,
    ) = communicate(
        back_kernel,
        [
            shaped(blocked, low),
            shaped((length, proj_columns), low),
            shaped((8, proj_columns)),
            shaped((1, channels)),
            shaped((shard_len, model_width)),
            shaped((model_width // rows, units), low),
            shaped((units // rows, model_width), low),
            shaped((channels * fold // rows, model_width // fold), low),
            shaped(embed_weight.shape),
            shaped(inner_weight.shape),
            shaped(filter_weight.shape),
            shaped(columns.shape),
        ],
        [
            grad_gated,
            mlp_partial,
            up_grad,
            down_grad,
            out_grad,
            proj,
            short_flat,
            skip,
            segment,
            *filter_parts,
            pre,
            *transforms,
            *taps_bins,
            projected,
            mixed,
            summed,
        ],
        ((0, 1, 2, 3, 4), ()),
        [
            pltpu.VMEM((groups, shard_len, channels), low),
            pltpu.VMEM((length, channels), jnp.float32),
            pltpu.VMEM((length, 8), jnp.int32),
            pltpu.VMEM((shard_len, model_width), low),
            pltpu.VMEM((groups - 1, shard_len, model_width), low),
            semaphores((2,)),
            semaphores((2, groups - 1)),
            semaphores((2, groups - 1)),
        ]
        + row_reduce_scratch(up_grad.shape, chips)
        + row_reduce_scratch(down_grad.shape, chips)
        + row_reduce_scratch(out_grad.shape, chips),
        2,
        "back",
    )
    grad_norm2_gain, grad_norm2_bias, grad_out_bias, grad_down_bias = middle_sums[:4]
    grad_skip_gain = skip_sum[0]
    grad_up_bias = grad_up_bias[0]
    grad_short_weight = back_sums[:3].reshape(short_weight.shape)
    grad_short_bias = back_sums[3].reshape(short_bias.shape)
    grad_proj_bias = back_sums[4].reshape(proj_bias.shape)
    grad_embed_weight = embed_grad
    grad_sine_freq = column_grad[:, :3].T
    grad_embed_bias = column_grad[:, 3]
    grad_inner_bias = column_grad[:, 4:6].T

    everywhere = (
        grad_out_bias,
        grad_norm2_gain,
        grad_norm2_bias,
        grad_down_bias,
        grad_embed_weight,
        grad_embed_bias,
        grad_sine_freq,
        grad_inner_weight,
        grad_inner_bias,
    )
    rows_only = (
        grad_proj_bias,
        grad_short_weight,
        grad_short_bias,
        grad_filter_weight,
        grad_skip_gain,
        grad_up_bias,
    )

    def pack(parts):
        flat = jnp.concatenate([part.reshape(-1) for part in parts])
        return jnp.pad(flat, (0, -flat.size % 1024)).reshape(-1, 128)

    def unpack(packed, parts):
        flat = packed.reshape(-1)
        results = []
        start = 0
        for part in parts:
            results.append(flat[start : start + part.size].reshape(part.shape))
            start += part.size
        return results

    wide = pack(everywhere)
    packed = jnp.concatenate([wide, pack(rows_only)], axis=0)
    part_rows = proj.shape[1] // rows
    grad_tokens, proj_grad, final_sums, packed, up_grad, down_grad, out_grad = communicate(
        final_kernel,
        [
            shaped((shard_len, model_width)),
            shaped((model_width, proj_columns), low),
            shaped((8, model_width)),
            shaped(packed.shape),
            shaped(up_grad.shape, low),
            shaped(down_grad.shape, low),
            shaped(out_grad.shape[1:], low),
        ],
        [
            grad_first,
            first_all,
            grad_low,
            tokens[0],
            norm1_gain[None],
            grad_residual,
            packed,
            up_part,
            down_part,
            out_part,
        ],
        ((), ()),
        [
            pltpu.VMEM((model_width, proj_columns), low),
            pltpu.VMEM((part_rows, proj_columns), low),
            pltpu.VMEM((8, model_width), jnp.float32),
            pltpu.VMEM((groups - 1, shard_len, model_width), low),
            semaphores((2, groups - 1)),
        ]
        + row_reduce_scratch((model_width, proj_columns), chips)
        + row_gather_scratch(chips) * 4
        + small_sum_scratch(packed.shape, wide.shape[0], chips, groups)
        + small_sum_scratch((8, model_width), 8, chips, groups),
        3,
        "final",
    )
    grad_tokens = grad_tokens[None]
    grad_proj_weight = proj_grad.astype(jnp.float32).reshape(model_width, 3, channels)
    grad_out_weight = out_grad.reshape(out_weight.shape).astype(jnp.float32)
    grad_up_weight = up_grad.astype(jnp.float32)
    grad_down_weight = down_grad.astype(jnp.float32)
    layer_out = (residual + mlp_out + down_bias).astype(low)[None]
    grad_norm1_gain, grad_norm1_bias = final_sums[:2]
    wide, narrow = packed[: wide.shape[0]], packed[wide.shape[0] :]
    (
        grad_out_bias,
        grad_norm2_gain,
        grad_norm2_bias,
        grad_down_bias,
        grad_embed_weight,
        grad_embed_bias,
        grad_sine_freq,
        grad_inner_weight,
        grad_inner_bias,
    ) = unpack(wide, everywhere)
    (
        grad_proj_bias,
        grad_short_weight,
        grad_short_bias,
        grad_filter_weight,
        grad_skip_gain,
        grad_up_bias,
    ) = unpack(narrow, rows_only)
    return (
        layer_out,
        grad_tokens,
        grad_norm1_gain,
        grad_norm1_bias,
        grad_proj_weight,
        grad_proj_bias,
        grad_short_weight,
        grad_short_bias,
        grad_embed_weight,
        grad_embed_bias,
        grad_sine_freq,
        grad_inner_weight,
        grad_inner_bias,
        grad_filter_weight,
        grad_skip_gain,
        grad_out_weight,
        grad_out_bias,
        grad_norm2_gain,
        grad_norm2_bias,
        grad_up_weight,
        grad_up_bias,
        grad_down_weight,
        grad_down_bias,
    )


def solution(mesh):
    return jax.shard_map(
        body,
        mesh=mesh,
        in_specs=(
            P("dp", "tensor", None),
            P("dp", None),
            P(),
            P(),
            P(None, None, "tensor"),
            P(None, "tensor"),
            P(None, None, "tensor"),
            P(None, "tensor"),
            P(),
            P(),
            P(),
            P(),
            P(),
            P(None, "tensor"),
            P("tensor"),
            P("tensor"),
            P("tensor", None),
            P(),
            P(),
            P(),
            P(None, "tensor"),
            P("tensor"),
            P("tensor", None),
            P(),
            P("dp", "tensor", None),
        ),
        out_specs=(
            P("dp", "tensor", None),
            P("dp", "tensor", None),
            P(),
            P(),
            P(None, None, "tensor"),
            P(None, "tensor"),
            P(None, None, "tensor"),
            P(None, "tensor"),
            P(),
            P(),
            P(),
            P(),
            P(),
            P(None, "tensor"),
            P("tensor"),
            P("tensor", None),
            P(),
            P(),
            P(),
            P(None, "tensor"),
            P("tensor"),
            P("tensor", None),
            P(),
        ),
        check_vma=False,
    )
```

```python
import functools
import math

import jax
import jax.numpy as jnp
import ml_dtypes
import numpy as np
from jax import lax
from jax.experimental import pallas as pl
from jax.experimental.pallas import tpu as pltpu
from jax.sharding import PartitionSpec as P

FEAT = 33
SEQ = 1024
NDOC = 8


EPS = 1e-05
HIGH = lax.Precision.HIGHEST
SHIFT = 0.1
GELU_RATE = math.sqrt(2.0 / math.pi)
GELU_CUBE = 0.044715


def dot_nn(left, right):
    return jnp.dot(left, right, preferred_element_type=jnp.float32)


def dot_nt(left, right):
    return lax.dot_general(
        left, right, (((1,), (1,)), ((), ())), preferred_element_type=jnp.float32
    )


def dot_tn(left, right):
    return lax.dot_general(
        left, right, (((0,), (0,)), ((), ())), preferred_element_type=jnp.float32
    )


def transform(length):
    places = np.arange(length)
    angles = ((places[:, None] * places[None, :]) % (2 * length)) * (np.pi / length)
    return (
        jnp.asarray(np.cos(angles).astype(ml_dtypes.bfloat16)),
        jnp.asarray((-np.sin(angles)).astype(ml_dtypes.bfloat16)),
    )


def features_by_row():
    places = np.arange(SEQ, dtype=np.float32)
    bands = np.arange(1, (FEAT - 1) // 2 + 1, dtype=np.float32)
    angles = 2.0 * np.pi * np.arange(SEQ)[None, :] * bands[:, None].astype(np.float64) / SEQ
    rows = np.concatenate([(places / (SEQ - 1))[None, :], np.cos(angles), np.sin(angles)], axis=0)
    return jnp.asarray(rows.astype(np.float32))


def exact(left, right, contract):
    return lax.dot_general(
        left, right, (contract, ((), ())), precision=HIGH, preferred_element_type=jnp.float32
    )


def bin_scale(length):
    bins = lax.broadcasted_iota(jnp.int32, (length, 1), 0)
    return jnp.where(bins == 0, 0.5 / length, 1.0 / length)


def signs(length):
    places = lax.broadcasted_iota(jnp.int32, (length, 1), 0)
    return (1 - 2 * lax.rem(places, 2)).astype(jnp.float32)


def modulation(length, decay):
    places = lax.broadcasted_iota(jnp.int32, (length, 1), 0).astype(jnp.float32)
    return jnp.exp(-decay * (places / SEQ)) + SHIFT


def make_taps(
    features, embed, inner, columns, biases, filter_weight, decay, transforms, pre, taps_bins
):
    cos_main, sin_main, cos_small, sin_small = transforms
    main_re, main_im, main_top, small_re, small_im, small_top = taps_bins
    length = features.shape[1]
    region = cos_small.shape[0]
    hidden = None
    for i in range(3):
        if i == 0:
            value = exact(embed[...], features[...], ((0,), (0,)))
        else:
            value = exact(inner[i - 1], hidden, ((0,), (0,)))
        value = value + biases[i]
        pre[i] = value
        hidden = jnp.sin(columns[i] * value)
    taps = exact(hidden, filter_weight[...], ((0,), (0,)))
    taps = (taps * modulation(length, decay[...])).astype(jnp.bfloat16)
    scale = bin_scale(length)
    main_re[...] = dot_nn(cos_main[...], taps) * scale
    main_im[...] = dot_nn(sin_main[...], taps) * scale
    top = jnp.sum(taps.astype(jnp.float32) * signs(length), axis=0, keepdims=True)
    main_top[...] = top * (0.5 / length)
    short = taps[:region]
    scale = bin_scale(region)
    small_re[...] = dot_nn(cos_small[...], short) * scale
    small_im[...] = dot_nn(sin_small[...], short) * scale
    top = jnp.sum(short.astype(jnp.float32) * signs(region), axis=0, keepdims=True)
    small_top[...] = top * (0.5 / region)


def spectra(values, marks, cos_main, sin_main, cos_small, sin_small):
    length = values.shape[0]
    region = cos_small.shape[0]
    main = jnp.where(marks[:, 0:1] > 0, values, 0.0)
    top = jnp.sum(main * signs(length), axis=0, keepdims=True)
    main = main.astype(jnp.bfloat16)
    main_bins = (dot_nn(cos_main[...], main), dot_nn(sin_main[...], main), top)
    head, tail = values[:region], values[length - region :]
    head_slot, tail_slot = marks[:region, 3:4], marks[length - region :, 4:5]
    pieces = [
        jnp.where(head_slot == d, head, 0.0) + jnp.where(tail_slot == d, tail, 0.0)
        for d in range(NDOC)
    ]
    small = jnp.concatenate(pieces, axis=1)
    top = jnp.sum(small * signs(region), axis=0, keepdims=True)
    small = small.astype(jnp.bfloat16)
    small_bins = (dot_nn(cos_small[...], small), dot_nn(sin_small[...], small), top)
    return main_bins, small_bins


def times(left, right, conjugate):
    left_re, left_im, left_top = left
    right_re, right_im, right_top = right
    if conjugate:
        return (
            left_re * right_re + left_im * right_im,
            left_re * right_im - left_im * right_re,
            left_top * right_top,
        )
    return (
        left_re * right_re - left_im * right_im,
        left_re * right_im + left_im * right_re,
        left_top * right_top,
    )


def from_bins(bins, cos_rows, sin_rows):
    real, imag, top = bins
    return (
        dot_nn(cos_rows[...], real.astype(jnp.bfloat16))
        + dot_nn(sin_rows[...], imag.astype(jnp.bfloat16))
        + signs(real.shape[0]) * top
    )


def beside(part):
    return jnp.concatenate([part] * NDOC, axis=1)


def filtered(main_bins, small_bins, taps_main, taps_small, marks, transforms, conjugate):
    cos_main, sin_main, cos_small, sin_small = transforms
    main = from_bins(times(taps_main, main_bins, conjugate), cos_main, sin_main)
    taps_wide = tuple(beside(part) for part in taps_small)
    small = from_bins(times(taps_wide, small_bins, conjugate), cos_small, sin_small)
    length, channels = main.shape
    region = small.shape[0]
    main = jnp.where(marks[:, 0:1] > 0, main, 0.0)
    head, tail = main[:region], main[length - region :]
    head_slot, tail_slot = marks[:region, 3:4], marks[length - region :, 4:5]
    for d in range(NDOC):
        piece = small[:, d * channels : (d + 1) * channels]
        head = head + jnp.where(head_slot == d, piece, 0.0)
        tail = tail + jnp.where(tail_slot == d, piece, 0.0)
    return jnp.concatenate([head, main[region : length - region], tail], axis=0)


def filter_back(
    grad_taps,
    features,
    embed,
    rates,
    inner,
    filter_weight,
    decay,
    pre,
    filter_sums,
    channel_sums,
):
    length = features.shape[1]
    width = filter_weight.shape[0]
    rows = filter_rows(width)
    ones = jnp.ones((8, length), jnp.float32)
    raw = grad_taps[...] * modulation(length, decay[...])
    back = exact(filter_weight[...], raw, ((1,), (1,)))
    for i in (2, 1, 0):
        angle = rates[i] * pre[i]
        if i == 2:
            channel_sums[:width] = exact(jnp.sin(angle), raw, ((1,), (0,)))
        act = back * jnp.cos(angle)
        filter_sums[rows.freq + i : rows.freq + i + 1] = exact(ones, act * pre[i], ((1,), (1,)))[0:1]
        step = act * rates[i]
        bias = exact(ones, step, ((1,), (1,)))[0:1]
        if i == 0:
            filter_sums[rows.embed_bias : rows.embed_bias + 1] = bias
            filter_sums[rows.embed : rows.embed + FEAT] = exact(features[...], step, ((1,), (1,)))
        else:
            filter_sums[rows.inner_bias + i - 1 : rows.inner_bias + i] = bias
            below = jnp.sin(rates[i - 1] * pre[i - 1])
            filter_sums[(i - 1) * width : i * width] = exact(below, step, ((1,), (1,)))
            back = exact(inner[i - 1], step, ((1,), (0,)))


def shaped(shape, dtype=jnp.float32):
    return jax.ShapeDtypeStruct(shape, dtype)


def row_marks(segment, marks, region):
    ids = to_column(segment[...].astype(jnp.float32)).astype(jnp.int32)
    length = ids.shape[0]
    places = lax.broadcasted_iota(jnp.int32, ids.shape, 0)
    inside = ids == ids[region - 1 : region]
    marks[:, 0:1] = inside.astype(jnp.int32)
    for lag in (1, 2):
        same = (ids == pltpu.roll(ids, lag, 0)) & (places >= lag)
        marks[:, lag : lag + 1] = same.astype(jnp.int32)
    marks[:, 3:4] = jnp.where(inside | (places >= region), -1, ids)
    marks[:, 4:5] = jnp.where(inside | (places < length - region), -1, ids)


BY_INDEX = pl.DeviceIdType.MESH


def greet(devices):
    barrier = pltpu.get_barrier_semaphore()
    for device in devices:
        pl.semaphore_signal(barrier, inc=1, device_id=device, device_id_type=BY_INDEX)
    pl.semaphore_wait(barrier, len(devices))


def remote(source, target, send_sem, recv_sem, device):
    return pltpu.make_async_remote_copy(
        src_ref=source,
        dst_ref=target,
        send_sem=send_sem,
        recv_sem=recv_sem,
        device_id=device,
        device_id_type=BY_INDEX,
    )


def tensor_peers():
    count = lax.axis_size("tensor")
    me = lax.axis_index("tensor")
    return [lax.rem(me + k, count) for k in range(1, count)]


def tensor_devices():
    return [{"tensor": peer} for peer in tensor_peers()]


def sibling():
    me = lax.axis_index("dp")
    return {"dp": me + 1 - 2 * lax.rem(me, 2)}


def chip_peers():
    chips = lax.axis_size("dp") // 2
    me = lax.axis_index("dp")
    core = lax.rem(me, 2)
    result = []
    for k in range(1, chips):
        chip = lax.rem(me // 2 + k, chips)
        result.append((chip, 2 * chip + core))
    return result


def chip_devices():
    return [{"dp": mate} for unused_chip, mate in chip_peers()]


def spread(source, target, sems, devices):
    copies = []
    for k, device in enumerate(devices):
        copies.append(
            remote(
                source(k) if callable(source) else source,
                target(k) if callable(target) else target,
                sems.at[0, k],
                sems.at[1, k],
                device,
            )
        )
        copies[-1].start()
    return copies


def wait_all(copies):
    for copy in copies:
        copy.wait()


def span(index, size):
    return pl.ds(pl.multiple_of(index * size, 16), size)


def staged(pairs, sems):
    copies = []
    for i, (source, target) in enumerate(pairs):
        copies.append(pltpu.make_async_copy(source, target, sems.at[i]))
        copies[-1].start()
    return copies


def to_column(row):
    size = row.shape[1]
    piece = min(size, 128)
    shape = (piece, piece)
    same = lax.broadcasted_iota(jnp.int32, shape, 0) == lax.broadcasted_iota(jnp.int32, shape, 1)
    pieces = [
        jnp.sum(jnp.where(same, row[:, i : i + piece], 0.0), axis=1, keepdims=True)
        for i in range(0, size, piece)
    ]
    return jnp.concatenate(pieces, axis=0)


class Chain:
    def __init__(self, slots, send_sems, recv_sems):
        self.slots, self.send_sems, self.recv_sems = slots, send_sems, recv_sems
        self.count = lax.axis_size("tensor")
        self.me = lax.axis_index("tensor")

    def copy(self, block, side):
        step = 1 - 2 * side
        return remote(
            self.slots.at[block],
            self.slots.at[block],
            self.send_sems.at[side, block],
            self.recv_sems.at[block],
            {"tensor": lax.rem(self.me + step + self.count, self.count)},
        )

    def advance(self, step):
        lower, upper = self.me - step, self.me + step

        @pl.when(lower >= 0)
        def _():
            @pl.when(step > 0)
            def _():
                self.copy(lower, 0).wait_recv()

            @pl.when(self.me < self.count - 1)
            def _():
                self.copy(lower, 0).start()

        @pl.when(upper < self.count)
        def _():
            @pl.when(step > 0)
            def _():
                self.copy(upper, 1).wait_recv()

            @pl.when(self.me > 0)
            def _():
                self.copy(upper, 1).start()

    def finish(self):
        for block in range(self.count):

            @pl.when((self.me < self.count - 1) & (block <= self.me))
            def _():
                self.copy(block, 0).wait_send()

            @pl.when((self.me > 0) & (block >= self.me))
            def _():
                self.copy(block, 1).wait_send()


def normalised(values):
    average = jnp.mean(values, axis=-1, keepdims=True)
    centered = values - average
    variance = jnp.mean(centered * centered, axis=-1, keepdims=True)
    rate = lax.rsqrt(variance + EPS)
    return centered * rate, rate


def norm_back(grad, gain, hat, rate):
    e = grad * gain
    return rate * (
        e
        - jnp.mean(e, axis=-1, keepdims=True)
        - hat * jnp.mean(e * hat, axis=-1, keepdims=True)
    )


def column_sum(values):
    return jnp.sum(values, axis=0, keepdims=True)


def front_kernel(
    tokens,
    gain,
    shift,
    part,
    cotangent,
    segment,
    embed,
    embed_bias,
    freq,
    inner,
    inner_bias,
    filter_weight,
    decay,
    proj_bias,
    short,
    short_bias,
    skip,
    features_hbm,
    proj_hbm,
    cos_main_hbm,
    sin_main_hbm,
    cos_small,
    sin_small,
    first_out,
    part_all,
    cotangent_out,
    pre_out,
    main_re_out,
    main_im_out,
    main_top,
    small_re,
    small_im,
    small_top,
    gated_own,
    projected_out,
    mixed_out,
    summed_out,
    features,
    proj,
    cos_main,
    sin_main,
    first_all,
    cotangent_all,
    pre,
    main_re,
    main_im,
    projected,
    mixed,
    summed,
    gated,
    marks,
    load_sems,
    store_sems,
    local_sems,
    first_send,
    first_recv,
    cotangent_send,
    cotangent_recv,
    part_sems,
    chip_sems,
    core_sems,
    gated_sems,
):
    me = lax.axis_index("tensor")
    count = lax.axis_size("tensor")
    place = lax.axis_index("dp")
    core = lax.rem(place, 2)
    chip = place // 2
    peers = tensor_peers()
    shard = tokens.shape[0]
    channels = skip.shape[1]
    taps_bins = (main_re, main_im, main_top, small_re, small_im, small_top)
    transforms = (cos_main, sin_main, cos_small, sin_small)
    loads = staged(
        [
            (proj_hbm, proj),
            (features_hbm, features),
            (cos_main_hbm, cos_main),
            (sin_main_hbm, sin_main),
        ],
        load_sems,
    )
    greet(tensor_devices() + [sibling()] + chip_devices())

    hat, unused_rate = normalised(tokens[...].astype(jnp.float32))
    first_all[me] = (hat * gain[...] + shift[...]).astype(jnp.bfloat16)
    chain = Chain(first_all, first_send, first_recv)
    chain.advance(0)
    cotangent_all[me] = cotangent[...]
    later = Chain(cotangent_all, cotangent_send, cotangent_recv)
    own = pltpu.make_async_copy(part, part_all.at[me, chip, core], local_sems.at[0])
    own.start()
    parts = spread(part, part_all.at[me, chip, core], part_sems, tensor_devices())

    def project(block):
        rows = pl.ds(pl.multiple_of(block * shard, shard), shard)
        for k in range(3):
            lanes = slice(k * channels, (k + 1) * channels)
            projected[rows, lanes] = dot_nn(first_all[block], proj[k]) + proj_bias[k : k + 1]

    wait_all(loads)
    project(me)
    columns = [to_column(freq[i : i + 1]) for i in range(3)]
    biases = [to_column(embed_bias[...])] + [to_column(inner_bias[i : i + 1]) for i in range(2)]
    make_taps(
        features, embed, inner, columns, biases, filter_weight, decay, transforms, pre, taps_bins
    )
    row_marks(segment, marks, cos_small.shape[0])
    stores = [(pre, pre_out), (main_re, main_re_out), (main_im, main_im_out)]
    stored = staged(stores, store_sems)

    def turn(step, carry):
        chain.advance(step)

        def side(index, carry):
            block = me + step * (2 * index - 1)

            @pl.when((block >= 0) & (block < count))
            def _():
                project(block)

            return carry

        return lax.fori_loop(0, 2, side, carry)

    lax.fori_loop(1, 2, turn, 0)
    own.wait()
    wait_all(parts)
    held = part_all.at[:, chip, core]
    parts = spread(held, held, chip_sems, chip_devices())
    lax.fori_loop(2, count, turn, 0)
    later.advance(0)
    more = store_sems.at[pl.ds(len(stores), 5)]
    stored += staged([(first_all, first_out), (projected, projected_out)], more)
    wait_all(parts)
    held = part_all.at[:, :, core]
    parts = spread(held, held, core_sems, [sibling()])

    for k in range(3):
        lanes = slice(k * channels, (k + 1) * channels)
        value = projected[:, lanes]
        running = short_bias[k : k + 1] + short[0, k : k + 1] * value
        for lag in (1, 2):
            moved = jnp.where(marks[:, lag : lag + 1] > 0, pltpu.roll(value, lag, 0), 0.0)
            running = running + short[lag, k : k + 1] * moved
        mixed[:, lanes] = running
    product = mixed[:, 2 * channels :] * mixed[:, channels : 2 * channels]
    more = store_sems.at[pl.ds(len(stores) + 2, 3)]
    stored += staged([(mixed, mixed_out)], more)
    low = product.astype(jnp.bfloat16).astype(jnp.float32)
    main_bins, small_bins = spectra(low, marks, *transforms)
    result = filtered(
        main_bins,
        small_bins,
        (main_re[...], main_im[...], main_top[...]),
        (small_re[...], small_im[...], small_top[...]),
        marks,
        transforms,
        False,
    )
    total = result + skip[...] * product
    summed[...] = total
    gated[...] = (total * mixed[:, :channels]).astype(jnp.bfloat16).reshape(gated.shape)
    swapped = spread(
        lambda k: gated.at[peers[k]], gated_own.at[me], gated_sems, tensor_devices()
    )
    more = store_sems.at[pl.ds(len(stores) + 3, 2)]
    stored += staged([(summed, summed_out)], more)
    gated_own[me] = gated[me]
    for step in range(1, count):
        later.advance(step)
    more = store_sems.at[pl.ds(len(stores) + 4, 1)]
    stored += staged([(cotangent_all, cotangent_out)], more)
    chain.finish()
    later.finish()
    wait_all(parts + swapped + stored)


def middle_kernel(
    gated,
    out,
    tokens,
    out_bias,
    gain,
    shift,
    cotangent_hbm,
    up_hbm,
    bias,
    down_hbm,
    residual_out,
    grad_residual,
    mlp_out,
    up_out,
    down_out,
    bias_grad,
    grad_gated,
    out_grad,
    gain_sum,
    shift_sum,
    out_sum,
    down_sum,
    cotangent,
    up,
    down,
    residual,
    mlp,
    up_grad,
    down_grad,
    second,
    active,
    low,
    parting,
    arriving,
    own_part,
    load_sems,
    store_sems,
    second_send,
    second_recv,
    part_send,
    part_recv,
):
    me = lax.axis_index("tensor")
    count = lax.axis_size("tensor")
    shard, width = tokens.shape
    units = up.shape[1]
    loads = staged([(up_hbm, up), (down_hbm, down), (cotangent_hbm, cotangent)], load_sems)
    greet(tensor_devices())
    base = tokens[...].astype(jnp.float32) + out_bias[...]
    for block in range(count):
        base = base + dot_nn(gated[block], out[block])
    residual[...] = base
    hat, unused_rate = normalised(base)
    second[me] = (hat * gain[...] + shift[...]).astype(jnp.bfloat16)
    chain = Chain(second, second_send, second_recv)
    bias_grad[...] = jnp.zeros_like(bias_grad)

    def sent(block):
        return remote(
            parting.at[block],
            arriving.at[me],
            part_send.at[block],
            part_recv.at[me],
            {"tensor": block},
        )

    def work(block):
        cut = units // 2
        for lanes in (slice(0, cut), slice(cut, units)):
            hidden = dot_nn(second[block], up[:, lanes]) + bias[:, lanes]
            cube = GELU_CUBE * hidden * hidden
            slope = jnp.tanh(GELU_RATE * hidden * (1.0 + cube))
            gate = 0.5 * (1.0 + slope)
            active[block, :, lanes] = (hidden * gate).astype(jnp.bfloat16)
            rate = gate + (0.5 * GELU_RATE) * hidden * (1.0 - slope * slope) * (1.0 + 3.0 * cube)
            grad_hidden = dot_nt(cotangent[block], down[lanes]) * rate
            bias_grad[:, lanes] += column_sum(grad_hidden)
            low[block, :, lanes] = grad_hidden.astype(jnp.bfloat16)
        part = dot_nt(low[block], up[...])

        @pl.when(block == me)
        def _():
            own_part[...] = part

        @pl.when(block != me)
        def _():
            parting[block] = part.astype(jnp.bfloat16)
            sent(block).start()

        mlp[block] = dot_nn(active[block], down[...]).astype(jnp.bfloat16)

    def turn(step, carry):
        chain.advance(step)

        @pl.when(step == 0)
        def _():
            wait_all(loads)

        def side(index, carry):
            block = me + step * (2 * index - 1)

            @pl.when((block >= 0) & (block < count) & ((step > 0) | (index == 0)))
            def _():
                work(block)

            return carry

        return lax.fori_loop(0, 2, side, carry)

    lax.fori_loop(0, count, turn, 0)
    stored = staged([(residual, residual_out), (mlp, mlp_out)], store_sems)
    tokens_all = count * shard
    up_grad[...] = dot_tn(
        second[...].reshape(tokens_all, width), low[...].reshape(tokens_all, units)
    ).astype(jnp.bfloat16)
    down_grad[...] = dot_tn(
        active[...].reshape(tokens_all, units), cotangent[...].reshape(tokens_all, width)
    ).astype(jnp.bfloat16)
    stored += staged([(up_grad, up_out), (down_grad, down_out)], store_sems.at[pl.ds(2, 2)])
    for peer in tensor_peers():
        remote(
            parting.at[peer],
            arriving.at[peer],
            part_send.at[peer],
            part_recv.at[peer],
            {"tensor": peer},
        ).wait_recv()
        own_part[...] += arriving[peer].astype(jnp.float32)
    grad_normed = own_part[...]
    hat, rate = normalised(residual[...])
    grad_out = cotangent[me].astype(jnp.float32)
    grad = grad_out + norm_back(grad_normed, gain[...], hat, rate)
    grad_residual[...] = grad
    gain_sum[...] = column_sum(grad_normed * hat)
    shift_sum[...] = column_sum(grad_normed)
    out_sum[...] = column_sum(grad)
    down_sum[...] = column_sum(grad_out)
    grad_low = grad.astype(jnp.bfloat16)
    for block in range(count):
        grad_gated[block] = dot_nt(grad_low, out[block]).astype(jnp.bfloat16)
        out_grad[block] = dot_tn(gated[block], grad_low).astype(jnp.bfloat16)
    chain.finish()
    for peer in tensor_peers():
        sent(peer).wait_send()
    wait_all(stored)


class RowReduce:
    def __init__(self, source, part, refs):
        half, core_recv, chip_recv, load_sem, core_sems, chip_sems = refs[:6]
        self.source, self.part, self.half = source, part, half
        self.core_recv, self.chip_recv = core_recv, chip_recv
        self.load_sem, self.core_sems, self.chip_sems = load_sem, core_sems, chip_sems
        self.across = tuple(refs[6:])
        place = lax.axis_index("dp")
        self.core, self.chip = lax.rem(place, 2), place // 2
        self.chips = lax.axis_size("dp") // 2
        self.rows = half.shape[-2]
        self.size = self.rows // self.chips

    def pair(self):
        self.load = pltpu.make_async_copy(
            self.source.at[..., span(self.core, self.rows), :], self.half, self.load_sem.at[0]
        )
        self.load.start()
        self.copies = spread(
            self.source.at[..., span(1 - self.core, self.rows), :],
            self.core_recv,
            self.core_sems,
            [sibling()],
        )

    def plane(self):
        self.load.wait()
        wait_all(self.copies)
        self.half[...] = (
            self.half[...].astype(jnp.float32) + self.core_recv[...].astype(jnp.float32)
        ).astype(self.half.dtype)
        mates = chip_peers()
        self.copies = spread(
            lambda k: self.half.at[..., span(mates[k][0], self.size), :],
            lambda k: self.chip_recv.at[k],
            self.chip_sems,
            chip_devices(),
        )

    def gathered(self):
        value = self.half[..., span(self.chip, self.size), :].astype(jnp.float32)
        for k, copy in enumerate(self.copies):
            copy.wait()
            value = value + self.chip_recv[k].astype(jnp.float32)
        return value

    def cross(self):
        held, held_recv, sems = self.across
        held[...] = self.gathered().astype(held.dtype)
        peers = tensor_peers()
        self.copies = spread(
            lambda k: held.at[peers[k]], lambda k: held_recv.at[k], sems, tensor_devices()
        )

    def crossed(self):
        held, held_recv, sems = self.across
        value = held[lax.axis_index("tensor")].astype(jnp.float32)
        for k, copy in enumerate(self.copies):
            copy.wait()
            value = value + held_recv[k].astype(jnp.float32)
        return value

    def finish(self):
        value = self.crossed() if self.across else self.gathered()
        self.part[...] = value.astype(self.part.dtype)


def row_reduce_scratch(shape, chips):
    rows, columns = shape[-2:]
    lead = tuple(shape[:-2])
    size = rows // 2 // chips
    low = jnp.bfloat16
    scratch = [
        pltpu.VMEM(lead + (rows // 2, columns), low),
        pltpu.VMEM(lead + (rows // 2, columns), low),
        pltpu.VMEM((chips - 1,) + lead + (size, columns), low),
        pltpu.SemaphoreType.DMA((1,)),
        pltpu.SemaphoreType.DMA((2, 1)),
        pltpu.SemaphoreType.DMA((2, chips - 1)),
    ]
    if lead:
        scratch += [
            pltpu.VMEM(lead + (size, columns), low),
            pltpu.VMEM((lead[0] - 1, size, columns), low),
            pltpu.SemaphoreType.DMA((2, lead[0] - 1)),
        ]
    return scratch


class RowGather:
    def __init__(self, part, total, refs):
        self.part, self.total = part, total
        self.own_sem, self.chip_sems, self.core_sems = refs
        place = lax.axis_index("dp")
        core, chip = lax.rem(place, 2), place // 2
        chips = lax.axis_size("dp") // 2
        self.mine = span(core * chips + chip, part.shape[0])
        self.half = span(core, part.shape[0] * chips)

    def plane(self):
        own = self.total.at[self.mine]
        self.copies = staged([(self.part, own)], self.own_sem)
        self.copies += spread(self.part, own, self.chip_sems, chip_devices())

    def pair(self):
        wait_all(self.copies)
        own = self.total.at[self.half]
        self.copies = spread(own, own, self.core_sems, [sibling()])

    def finish(self):
        wait_all(self.copies)


def row_gather_scratch(chips):
    return [
        pltpu.SemaphoreType.DMA((1,)),
        pltpu.SemaphoreType.DMA((2, chips - 1)),
        pltpu.SemaphoreType.DMA((2, 1)),
    ]


class SmallSums:
    def __init__(self, sources, results, wide, refs):
        self.sources, self.results, self.wide = sources, results, wide
        count = len(sources)
        self.core_recv = refs[:count]
        self.chip_slots = refs[count : 2 * count]
        self.group_slots = refs[2 * count : 2 * count + wide]
        self.core_sems, self.chip_sems, self.group_sems = refs[2 * count + wide :]
        self.me = lax.axis_index("tensor")
        self.chip = lax.axis_index("dp") // 2

    def pair(self):
        self.copies = []
        for i, source in enumerate(self.sources):
            self.copies += spread(source, self.core_recv[i], self.core_sems.at[i], [sibling()])

    def plane(self):
        wait_all(self.copies)
        self.copies = []
        for i, source in enumerate(self.sources):
            self.chip_slots[i][self.chip] = source[...] + self.core_recv[i][...]
            own = self.chip_slots[i].at[self.chip]
            self.copies += spread(own, own, self.chip_sems.at[i], chip_devices())

    def total(self, slots):
        value = slots[0]
        for i in range(1, slots.shape[0]):
            value = value + slots[i]
        return value

    def tensor(self):
        wait_all(self.copies)
        self.copies = []
        for i in range(len(self.sources)):
            if i >= self.wide:
                self.results[i][...] = self.total(self.chip_slots[i])
                continue
            self.group_slots[i][self.me] = self.total(self.chip_slots[i])
            own = self.group_slots[i].at[self.me]
            self.copies += spread(own, own, self.group_sems.at[i], tensor_devices())

    def finish(self):
        wait_all(self.copies)
        for i in range(self.wide):
            self.results[i][...] = self.total(self.group_slots[i])


def small_sums_scratch(shapes, wide, chips, groups):
    return (
        [pltpu.VMEM(shape, jnp.float32) for shape in shapes]
        + [pltpu.VMEM((chips,) + tuple(shape), jnp.float32) for shape in shapes]
        + [pltpu.VMEM((groups,) + tuple(shape), jnp.float32) for shape in shapes[:wide]]
        + [
            pltpu.SemaphoreType.DMA((len(shapes), 2, 1)),
            pltpu.SemaphoreType.DMA((len(shapes), 2, chips - 1)),
            pltpu.SemaphoreType.DMA((max(wide, 1), 2, groups - 1)),
        ]
    )


class channel_rows:
    def __init__(self, width):
        self.filter = 0
        self.short = width
        self.short_bias = width + 9
        self.proj_bias = width + 12
        self.skip = width + 15
        self.size = width + 16


class filter_rows:
    def __init__(self, width):
        self.inner = 0
        self.embed = 2 * width
        self.embed_bias = self.embed + FEAT + -FEAT % 8
        self.freq = self.embed_bias + 1
        self.inner_bias = self.embed_bias + 4
        self.size = self.embed_bias + 8


def back_kernel(
    grad_blocks,
    mlp,
    up_grad,
    down_grad,
    out_grad,
    short,
    skip,
    segment,
    embed,
    freq,
    inner,
    filter_weight,
    decay,
    main_top,
    small_re,
    small_im,
    small_top,
    cos_small,
    sin_small,
    mixed_hbm,
    cos_main_hbm,
    sin_main_hbm,
    main_re_hbm,
    main_im_hbm,
    summed_hbm,
    projected_hbm,
    proj_hbm,
    features_hbm,
    pre_hbm,
    grad_first,
    grad_low,
    mlp_sum,
    up_part,
    down_part,
    out_part,
    filter_sums,
    channel_sums,
    mixed,
    cos_main,
    sin_main,
    main_re,
    main_im,
    summed,
    projected,
    proj,
    features,
    pre,
    grad_gated,
    grad_taps,
    marks,
    mlp_own,
    mlp_recv,
    load_sems,
    local_sems,
    gated_sems,
    mlp_sems,
    *scratch,
):
    me = lax.axis_index("tensor")
    count = lax.axis_size("tensor")
    peers = tensor_peers()
    channels = skip.shape[1]
    length = projected.shape[0]
    region = cos_small.shape[0]
    shard = length // count
    transforms = (cos_main, sin_main, cos_small, sin_small)
    loads = staged(
        [
            (mixed_hbm, mixed),
            (cos_main_hbm, cos_main),
            (sin_main_hbm, sin_main),
            (main_re_hbm, main_re),
            (main_im_hbm, main_im),
            (summed_hbm, summed),
            (projected_hbm, projected),
            (proj_hbm, proj),
            (features_hbm, features),
            (pre_hbm, pre),
        ],
        load_sems,
    )
    greet(tensor_devices() + [sibling()] + chip_devices())
    up_row = RowReduce(up_grad, up_part, scratch[:6])
    down_row = RowReduce(down_grad, down_part, scratch[6:12])
    out_row = RowReduce(out_grad, out_part, scratch[12:21])
    weights = (out_row, up_row, down_row)
    places = channel_rows(filter_weight.shape[0])
    filter_sums[...] = jnp.zeros_like(filter_sums)
    own = pltpu.make_async_copy(grad_blocks.at[me], grad_gated.at[me], local_sems.at[0])
    own.start()
    arriving = spread(
        lambda k: grad_blocks.at[peers[k]], grad_gated.at[me], gated_sems, tensor_devices()
    )
    for weight in weights:
        weight.pair()
    own_mlp = pltpu.make_async_copy(mlp.at[me], mlp_own, local_sems.at[1])
    own_mlp.start()
    row_marks(segment, marks, region)
    wait_all(loads[:3])
    gate_out = mixed[:, :channels]
    gate_in = mixed[:, channels : 2 * channels]
    values = mixed[:, 2 * channels :]
    product = values * gate_in
    low = product.astype(jnp.bfloat16).astype(jnp.float32)
    value_main, value_small = spectra(low, marks, *transforms)
    for weight in weights:
        weight.plane()
    own.wait()
    wait_all(arriving)
    mlps = spread(
        lambda k: mlp.at[peers[k]], lambda k: mlp_recv.at[k], mlp_sems, tensor_devices()
    )
    grad = grad_gated[...].reshape(length, channels).astype(jnp.float32)
    grad_summed = grad * gate_out
    channel_sums[places.skip : places.skip + 1] = column_sum(grad_summed * product)
    low = grad_summed.astype(jnp.bfloat16).astype(jnp.float32)
    grad_main, grad_small = spectra(low, marks, *transforms)
    real, imag, top = times(value_main, grad_main, True)
    scale = bin_scale(length)
    taps = from_bins((real * scale, imag * scale, top * (0.5 / length)), cos_main, sin_main)
    scale = bin_scale(region)
    real, imag, top = (
        sum(part[:, d * channels : (d + 1) * channels] for d in range(NDOC))
        for part in times(value_small, grad_small, True)
    )
    taps_small = from_bins((real * scale, imag * scale, top * (0.5 / region)), cos_small, sin_small)
    grad_taps[:region] = taps[:region] + taps_small
    grad_taps[region:] = taps[region:]
    wait_all(loads[3:])
    result = filtered(
        grad_main,
        grad_small,
        (main_re[...], main_im[...], main_top[...]),
        (small_re[...], small_im[...], small_top[...]),
        marks,
        transforms,
        True,
    )
    grad_product = result + grad_summed * skip[...]
    parts = (grad * summed[...], grad_product * values, grad_product * gate_in)
    for k, part in enumerate(parts):
        lanes = slice(k * channels, (k + 1) * channels)
        source = projected[:, lanes]
        row = places.short_bias + k
        channel_sums[row : row + 1] = column_sum(part)
        row = places.short + k
        channel_sums[row : row + 1] = column_sum(part * source)
        running = short[0, k : k + 1] * part
        for lag in (1, 2):
            kept = jnp.where(marks[:, lag : lag + 1] > 0, part, 0.0)
            row = places.short + 3 * lag + k
            channel_sums[row : row + 1] = column_sum(kept * pltpu.roll(source, lag, 0))
            running = running + short[lag, k : k + 1] * pltpu.roll(kept, length - lag, 0)
        row = places.proj_bias + k
        channel_sums[row : row + 1] = column_sum(running)
        grad_low[:, lanes] = running.astype(jnp.bfloat16)
    out_row.cross()
    for block in range(count):
        rows = slice(block * shard, (block + 1) * shard)
        total = dot_nt(grad_low[rows, :channels], proj[0])
        for k in (1, 2):
            total = total + dot_nt(grad_low[rows, k * channels : (k + 1) * channels], proj[k])
        grad_first[block] = total.astype(jnp.bfloat16)
    filter_back(
        grad_taps,
        features,
        embed,
        [to_column(freq[i : i + 1]) for i in range(3)],
        inner,
        filter_weight,
        decay,
        pre,
        filter_sums,
        channel_sums,
    )
    for weight in weights:
        weight.finish()
    own_mlp.wait()
    total = mlp_own[...].astype(jnp.float32)
    for k, copy in enumerate(mlps):
        copy.wait()
        total = total + mlp_recv[k].astype(jnp.float32)
    mlp_sum[...] = total


def final_kernel(
    grad_first,
    tokens,
    gain,
    shift,
    out_bias_sum,
    gain_sum,
    shift_sum,
    down_bias_sum,
    filter_sums,
    channel_sums,
    up_bias_sum,
    up_part,
    down_part,
    out_part,
    first_hbm,
    grad_low_hbm,
    grad_tokens,
    proj_sum,
    up_sum,
    down_sum,
    out_sum,
    line_all,
    filter_all,
    channel_all,
    up_bias_all,
    first,
    grad_low,
    proj_grad,
    proj_part,
    lines,
    load_sems,
    block_recv,
    block_sems,
    *scratch,
):
    me = lax.axis_index("tensor")
    count = lax.axis_size("tensor")
    peers = tensor_peers()
    loads = staged([(first_hbm, first), (grad_low_hbm, grad_low)], load_sems)
    greet(tensor_devices() + [sibling()] + chip_devices())
    blocks = spread(
        lambda k: grad_first.at[peers[k]], lambda k: block_recv.at[k], block_sems, tensor_devices()
    )
    row = RowReduce(proj_grad, proj_part, scratch[:6])
    proj_all = RowGather(proj_part, proj_sum, scratch[6:9])
    gathers = (
        RowGather(up_part, up_sum, scratch[9:12]),
        RowGather(down_part, down_sum, scratch[12:15]),
        RowGather(out_part, out_sum, scratch[15:18]),
    )
    small = SmallSums(
        (lines, filter_sums, channel_sums, up_bias_sum),
        (line_all, filter_all, channel_all, up_bias_all),
        2,
        scratch[18:],
    )
    length, columns = grad_low.shape
    channels = columns // 3
    width = tokens.shape[1]
    wait_all(loads)
    for k in range(3):
        proj_grad[k * width : (k + 1) * width] = dot_tn(
            first[...].reshape(length, width), grad_low[:, k * channels : (k + 1) * channels]
        ).astype(jnp.bfloat16)
    row.pair()
    plain = jnp.zeros_like(gain[...])
    scaled = jnp.zeros_like(gain[...])
    for block in range(count):
        grad = grad_first[block].astype(jnp.float32)
        plain = plain + column_sum(grad)
        scaled = scaled + column_sum(grad * first[block].astype(jnp.float32))
    lines[0:1] = out_bias_sum[...]
    lines[1:2] = gain_sum[...]
    lines[2:3] = shift_sum[...]
    lines[3:4] = down_bias_sum[...]
    lines[4:5] = (scaled - shift[...] * plain) / gain[...]
    lines[5:6] = plain
    lines[6:8] = jnp.zeros_like(lines[6:8])
    small.pair()
    row.plane()
    for gather in gathers:
        gather.plane()
    small.plane()
    hat, rate = normalised(tokens[...].astype(jnp.float32))
    row.finish()
    proj_all.plane()
    small.tensor()
    for gather in gathers:
        gather.pair()
    proj_all.pair()
    small.finish()
    grad = grad_first[me].astype(jnp.float32)
    for k, copy in enumerate(blocks):
        copy.wait()
        grad = grad + block_recv[k].astype(jnp.float32)
    grad_tokens[...] = norm_back(grad, gain[...], hat, rate)
    for gather in gathers + (proj_all,):
        gather.finish()


def finish_kernel(
    residual,
    mlp_sum,
    down_bias,
    grad_tokens,
    grad_residual,
    proj_sum,
    up_sum,
    down_sum,
    out_sum,
    line_all,
    filter_all,
    channel_all,
    up_bias_all,
    layer_out,
    tokens_out,
    proj_out,
    up_out,
    down_out,
    out_out,
    out_bias_out,
    gain2_out,
    shift2_out,
    down_bias_out,
    gain1_out,
    shift1_out,
    embed_out,
    embed_bias_out,
    freq_out,
    inner_out,
    inner_bias_out,
    filter_out,
    short_out,
    short_bias_out,
    proj_bias_out,
    skip_out,
    up_bias_out,
):
    layer_out[...] = (residual[...] + mlp_sum[...] + down_bias[...]).astype(layer_out.dtype)
    tokens_out[...] = grad_tokens[...] + grad_residual[...]
    for source, target in (
        (proj_sum, proj_out),
        (up_sum, up_out),
        (down_sum, down_out),
        (out_sum, out_out),
    ):
        target[...] = source[...].astype(jnp.float32)

    @pl.when(pl.program_id(0) == 0)
    def _():
        lines = (out_bias_out, gain2_out, shift2_out, down_bias_out, gain1_out, shift1_out)
        for i, line in enumerate(lines):
            line[...] = line_all[i : i + 1]
        width = filter_out.shape[0]
        rows = filter_rows(width)
        for i in range(2):
            inner_out[i] = filter_all[i * width : (i + 1) * width]
        embed_out[...] = filter_all[rows.embed : rows.embed + FEAT]
        embed_bias_out[...] = filter_all[rows.embed_bias : rows.embed_bias + 1]
        freq_out[...] = filter_all[rows.freq : rows.freq + 3]
        inner_bias_out[...] = filter_all[rows.inner_bias : rows.inner_bias + 2]
        rows = channel_rows(width)
        filter_out[...] = channel_all[:width]
        for lag in range(3):
            row = rows.short + 3 * lag
            short_out[lag] = channel_all[row : row + 3]
        short_bias_out[...] = channel_all[rows.short_bias : rows.short_bias + 3]
        proj_bias_out[...] = channel_all[rows.proj_bias : rows.proj_bias + 3]
        skip_out[...] = channel_all[rows.skip : rows.skip + 1]
        up_bias_out[...] = up_bias_all[...]


def finish(big, shapes):
    steps = 8

    def rows(shape):
        return pl.BlockSpec((shape[0] // steps, shape[1]), lambda i: (i, 0))

    def whole(shape):
        return pl.BlockSpec(tuple(shape), lambda i: (0,) * len(shape))

    in_specs = [
        whole(array.shape) if i == 2 or i > 8 else rows(array.shape) for i, array in enumerate(big)
    ]
    out_specs = [rows(shape.shape) if i < 6 else whole(shape.shape) for i, shape in enumerate(shapes)]
    return pl.pallas_call(
        finish_kernel,
        grid=(steps,),
        in_specs=in_specs,
        out_specs=out_specs,
        out_shape=shapes,
        compiler_params=pltpu.CompilerParams(
            dimension_semantics=("arbitrary",), vmem_limit_bytes=48 * 1024 * 1024
        ),
        name="finish",
    )(*big)


def communicate(kernel, shapes, operands, anywhere, scratch, channel, name):
    vmem = pl.BlockSpec(memory_space=pltpu.VMEM)
    free = pl.BlockSpec(memory_space=pl.ANY)
    return pl.pallas_call(
        kernel,
        out_shape=shapes,
        in_specs=[free if i in anywhere[0] else vmem for i in range(len(operands))],
        out_specs=[free if i in anywhere[1] else vmem for i in range(len(shapes))],
        scratch_shapes=scratch,
        compiler_params=pltpu.CompilerParams(
            collective_id=channel, has_side_effects=True, vmem_limit_bytes=60 * 1024 * 1024
        ),
        cost_estimate=pl.CostEstimate(flops=0, bytes_accessed=200_000_000, transcendentals=0),
        name=name,
    )(*operands)


def body(
    tokens,
    segment_ids,
    norm1_gain,
    norm1_bias,
    proj_weight,
    proj_bias,
    short_weight,
    short_bias,
    embed_weight,
    embed_bias,
    sine_freq,
    inner_weight,
    inner_bias,
    filter_weight,
    decay_rate,
    skip_gain,
    out_weight,
    out_bias,
    norm2_gain,
    norm2_bias,
    up_weight,
    up_bias,
    down_weight,
    down_bias,
    cotangent,
):
    row_count, shard_len, model_width = tokens.shape
    groups = lax.axis_size("tensor")
    rows = lax.axis_size("dp")
    place = lax.axis_index("tensor")
    row_place = lax.axis_index("dp")
    length = shard_len * groups
    channels = proj_weight.shape[2]
    units = up_weight.shape[1]
    channel_slice = channels // rows

    out_part = lax.dynamic_slice_in_dim(out_weight, row_place * channel_slice, channel_slice, 0)
    out_rows = -(-channel_slice // 16) * 16
    out_part = jnp.pad(out_part, ((0, out_rows - channel_slice), (0, 0)))

    low = jnp.bfloat16
    region = shard_len
    chips = rows // 2
    proj_columns = 3 * channels
    cos_main, sin_main = transform(length)
    cos_small, sin_small = transform(region)
    features = features_by_row()
    decay = decay_rate[None]
    width = embed_weight.shape[1]
    embed_bias = embed_bias[None]
    proj = proj_weight.transpose(1, 0, 2)
    skip = skip_gain[None]
    semaphores = pltpu.SemaphoreType.DMA
    vmem = pltpu.VMEM
    single = jnp.float32
    blocked = (groups, shard_len, model_width)
    swapped = (groups, shard_len, channels)
    line = (1, model_width)
    (
        first_all,
        out_all,
        all_cotangent,
        pre,
        main_re,
        main_im,
        main_top,
        small_re,
        small_im,
        small_top,
        gated_own,
        projected,
        mixed,
        summed,
    ) = communicate(
        front_kernel,
        [
            shaped(blocked, low),
            shaped((groups, chips, 2) + out_part.shape, low),
            shaped(blocked, low),
            shaped((3, width, length)),
            shaped((length, channels)),
            shaped((length, channels)),
            shaped((1, channels)),
            shaped((region, channels)),
            shaped((region, channels)),
            shaped((1, channels)),
            shaped(swapped, low),
            shaped((length, proj_columns)),
            shaped((length, proj_columns)),
            shaped((length, channels)),
        ],
        [
            tokens[0],
            norm1_gain[None],
            norm1_bias[None],
            out_part,
            cotangent[0],
            segment_ids,
            embed_weight,
            embed_bias,
            sine_freq,
            inner_weight,
            inner_bias,
            filter_weight,
            decay,
            proj_bias,
            short_weight,
            short_bias,
            skip,
            features,
            proj,
            cos_main,
            sin_main,
            cos_small,
            sin_small,
        ],
        ((3, 17, 18, 19, 20), (0, 1, 2, 3, 4, 5, 11, 12, 13)),
        [
            vmem(features.shape, single),
            vmem(proj.shape, low),
            vmem(cos_main.shape, low),
            vmem(sin_main.shape, low),
            vmem(blocked, low),
            vmem(blocked, low),
            vmem((3, width, length), single),
            vmem((length, channels), single),
            vmem((length, channels), single),
            vmem((length, proj_columns), single),
            vmem((length, proj_columns), single),
            vmem((length, channels), single),
            vmem(swapped, low),
            vmem((length, 8), jnp.int32),
            semaphores((4,)),
            semaphores((8,)),
            semaphores((1,)),
            semaphores((2, groups)),
            semaphores((groups,)),
            semaphores((2, groups)),
            semaphores((groups,)),
            semaphores((2, groups - 1)),
            semaphores((2, chips - 1)),
            semaphores((2, 1)),
            semaphores((2, groups - 1)),
        ],
        0,
        "front",
    )
    out_all = out_all[..., :channel_slice, :].reshape(groups, channels, model_width)
    (
        residual,
        grad_residual,
        mlp_partial,
        up_grad,
        down_grad,
        grad_up_bias,
        grad_gated,
        out_grad,
        grad_norm2_gain,
        grad_norm2_bias,
        grad_out_bias,
        grad_down_bias,
    ) = communicate(
        middle_kernel,
        [
            shaped((shard_len, model_width)),
            shaped((shard_len, model_width)),
            shaped(blocked, low),
            shaped((model_width, units), low),
            shaped((units, model_width), low),
            shaped((1, units)),
            shaped(swapped, low),
            shaped((groups, channels, model_width), low),
            shaped(line),
            shaped(line),
            shaped(line),
            shaped(line),
        ],
        [
            gated_own,
            out_all,
            tokens[0],
            out_bias[None],
            norm2_gain[None],
            norm2_bias[None],
            all_cotangent,
            up_weight,
            up_bias[None],
            down_weight,
        ],
        ((6, 7, 9), (0, 2, 3, 4)),
        [
            vmem(blocked, low),
            vmem((model_width, units), low),
            vmem((units, model_width), low),
            vmem((shard_len, model_width), single),
            vmem(blocked, low),
            vmem((model_width, units), low),
            vmem((units, model_width), low),
            vmem(blocked, low),
            vmem((groups, shard_len, units), low),
            vmem((groups, shard_len, units), low),
            vmem(blocked, low),
            vmem(blocked, low),
            vmem((shard_len, model_width), single),
            semaphores((3,)),
            semaphores((4,)),
            semaphores((2, groups)),
            semaphores((groups,)),
            semaphores((groups,)),
            semaphores((groups,)),
        ],
        1,
        "middle",
    )
    fold = max(1, 32 * chips // channels)
    out_grad = out_grad.reshape(groups, channels * fold, model_width // fold)
    out_size = (channels * fold // rows, model_width // fold)
    filter_shape = (filter_rows(width).size, width)
    channel_shape = (channel_rows(width).size, channels)
    (
        grad_first,
        grad_low,
        mlp_out,
        up_part,
        down_part,
        out_part,
        filter_sums,
        channel_sums,
    ) = communicate(
        back_kernel,
        [
            shaped(blocked, low),
            shaped((length, proj_columns), low),
            shaped((shard_len, model_width)),
            shaped((model_width // rows, units), low),
            shaped((units // rows, model_width), low),
            shaped(out_size, low),
            shaped(filter_shape),
            shaped(channel_shape),
        ],
        [
            grad_gated,
            mlp_partial,
            up_grad,
            down_grad,
            out_grad,
            short_weight,
            skip,
            segment_ids,
            embed_weight,
            sine_freq,
            inner_weight,
            filter_weight,
            decay,
            main_top,
            small_re,
            small_im,
            small_top,
            cos_small,
            sin_small,
            mixed,
            cos_main,
            sin_main,
            main_re,
            main_im,
            summed,
            projected,
            proj,
            features,
            pre,
        ],
        ((0, 1, 2, 3, 4, 19, 20, 21, 22, 23, 24, 25, 26, 27, 28), ()),
        [
            vmem((length, proj_columns), single),
            vmem(cos_main.shape, low),
            vmem(sin_main.shape, low),
            vmem((length, channels), single),
            vmem((length, channels), single),
            vmem((length, channels), single),
            vmem((length, proj_columns), single),
            vmem(proj.shape, low),
            vmem(features.shape, single),
            vmem(pre.shape, single),
            vmem(swapped, low),
            vmem((length, channels), single),
            vmem((length, 8), jnp.int32),
            vmem((shard_len, model_width), low),
            vmem((groups - 1, shard_len, model_width), low),
            semaphores((10,)),
            semaphores((2,)),
            semaphores((2, groups - 1)),
            semaphores((2, groups - 1)),
        ]
        + row_reduce_scratch(up_grad.shape, chips)
        + row_reduce_scratch(down_grad.shape, chips)
        + row_reduce_scratch(out_grad.shape, chips),
        2,
        "back",
    )
    (
        grad_tokens,
        proj_sum,
        up_sum,
        down_sum,
        out_sum,
        line_all,
        filter_all,
        channel_all,
        up_bias_all,
    ) = communicate(
        final_kernel,
        [
            shaped((shard_len, model_width)),
            shaped((3 * model_width, channels), low),
            shaped(up_grad.shape, low),
            shaped(down_grad.shape, low),
            shaped(out_grad.shape[1:], low),
            shaped((8, model_width)),
            shaped(filter_shape),
            shaped(channel_shape),
            shaped(grad_up_bias.shape),
        ],
        [
            grad_first,
            tokens[0],
            norm1_gain[None],
            norm1_bias[None],
            grad_out_bias,
            grad_norm2_gain,
            grad_norm2_bias,
            grad_down_bias,
            filter_sums,
            channel_sums,
            grad_up_bias,
            up_part,
            down_part,
            out_part,
            first_all,
            grad_low,
        ],
        ((14, 15), (1, 2, 3, 4)),
        [
            vmem(blocked, low),
            vmem((length, proj_columns), low),
            vmem((3 * model_width, channels), low),
            vmem((3 * model_width // rows, channels), low),
            vmem((8, model_width), single),
            semaphores((2,)),
            vmem((groups - 1, shard_len, model_width), low),
            semaphores((2, groups - 1)),
        ]
        + row_reduce_scratch((3 * model_width, channels), chips)
        + row_gather_scratch(chips) * 4
        + small_sums_scratch(
            [(8, model_width), filter_shape, channel_shape, grad_up_bias.shape], 2, chips, groups
        ),
        3,
        "final",
    )
    (
        layer_out,
        grad_tokens,
        grad_proj_weight,
        grad_up_weight,
        grad_down_weight,
        grad_out_weight,
        grad_out_bias,
        grad_norm2_gain,
        grad_norm2_bias,
        grad_down_bias,
        grad_norm1_gain,
        grad_norm1_bias,
        grad_embed_weight,
        grad_embed_bias,
        grad_sine_freq,
        grad_inner_weight,
        grad_inner_bias,
        grad_filter_weight,
        grad_short_weight,
        grad_short_bias,
        grad_proj_bias,
        grad_skip_gain,
        grad_up_bias,
    ) = finish(
        [
            residual,
            mlp_out,
            down_bias[None],
            grad_tokens,
            grad_residual,
            proj_sum,
            up_sum,
            down_sum,
            out_sum.reshape(out_weight.shape),
            line_all,
            filter_all,
            channel_all,
            up_bias_all,
        ],
        [
            shaped((shard_len, model_width), low),
            shaped((shard_len, model_width)),
            shaped((3 * model_width, channels)),
            shaped(up_weight.shape),
            shaped(down_weight.shape),
            shaped(out_weight.shape),
            shaped(line),
            shaped(line),
            shaped(line),
            shaped(line),
            shaped(line),
            shaped(line),
            shaped(embed_weight.shape),
            shaped(embed_bias.shape),
            shaped(sine_freq.shape),
            shaped(inner_weight.shape),
            shaped(inner_bias.shape),
            shaped(filter_weight.shape),
            shaped(short_weight.shape),
            shaped(short_bias.shape),
            shaped(proj_bias.shape),
            shaped(skip.shape),
            shaped(up_bias_all.shape),
        ],
    )
    grad_proj_weight = grad_proj_weight.reshape(3, model_width, channels).transpose(1, 0, 2)
    return (
        layer_out[None],
        grad_tokens[None],
        grad_norm1_gain[0],
        grad_norm1_bias[0],
        grad_proj_weight,
        grad_proj_bias,
        grad_short_weight,
        grad_short_bias,
        grad_embed_weight,
        grad_embed_bias[0],
        grad_sine_freq,
        grad_inner_weight,
        grad_inner_bias,
        grad_filter_weight,
        grad_skip_gain[0],
        grad_out_weight,
        grad_out_bias[0],
        grad_norm2_gain[0],
        grad_norm2_bias[0],
        grad_up_weight,
        grad_up_bias[0],
        grad_down_weight,
        grad_down_bias[0],
    )


def solution(mesh):
    return jax.shard_map(
        body,
        mesh=mesh,
        in_specs=(
            P("dp", "tensor", None),
            P("dp", None),
            P(),
            P(),
            P(None, None, "tensor"),
            P(None, "tensor"),
            P(None, None, "tensor"),
            P(None, "tensor"),
            P(),
            P(),
            P(),
            P(),
            P(),
            P(None, "tensor"),
            P("tensor"),
            P("tensor"),
            P("tensor", None),
            P(),
            P(),
            P(),
            P(None, "tensor"),
            P("tensor"),
            P("tensor", None),
            P(),
            P("dp", "tensor", None),
        ),
        out_specs=(
            P("dp", "tensor", None),
            P("dp", "tensor", None),
            P(),
            P(),
            P(None, None, "tensor"),
            P(None, "tensor"),
            P(None, None, "tensor"),
            P(None, "tensor"),
            P(),
            P(),
            P(),
            P(),
            P(),
            P(None, "tensor"),
            P("tensor"),
            P("tensor", None),
            P(),
            P(),
            P(),
            P(None, "tensor"),
            P("tensor"),
            P("tensor", None),
            P(),
        ),
        check_vma=False,
    )
```

```python
import functools
import math

import jax
import jax.numpy as jnp
import ml_dtypes
import numpy as np
from jax import lax
from jax.experimental import pallas as pl
from jax.experimental.pallas import tpu as pltpu
from jax.sharding import PartitionSpec as P

FEAT = 33
SEQ = 1024
NDOC = 8


EPS = 1e-05
HIGH = lax.Precision.HIGHEST
SHIFT = 0.1
GELU_RATE = math.sqrt(2.0 / math.pi)
GELU_CUBE = 0.044715


def dot_nn(left, right):
    return jnp.dot(left, right, preferred_element_type=jnp.float32)


def dot_nt(left, right):
    return lax.dot_general(
        left, right, (((1,), (1,)), ((), ())), preferred_element_type=jnp.float32
    )


def dot_tn(left, right):
    return lax.dot_general(
        left, right, (((0,), (0,)), ((), ())), preferred_element_type=jnp.float32
    )


def transform(length):
    places = np.arange(length)
    angles = ((places[:, None] * places[None, :]) % (2 * length)) * (np.pi / length)
    return (
        jnp.asarray(np.cos(angles).astype(ml_dtypes.bfloat16)),
        jnp.asarray((-np.sin(angles)).astype(ml_dtypes.bfloat16)),
    )


def features_by_row():
    places = np.arange(SEQ, dtype=np.float32)
    bands = np.arange(1, (FEAT - 1) // 2 + 1, dtype=np.float32)
    angles = 2.0 * np.pi * np.arange(SEQ)[None, :] * bands[:, None].astype(np.float64) / SEQ
    rows = np.concatenate([(places / (SEQ - 1))[None, :], np.cos(angles), np.sin(angles)], axis=0)
    return jnp.asarray(rows.astype(np.float32))


def exact(left, right, contract):
    return lax.dot_general(
        left, right, (contract, ((), ())), precision=HIGH, preferred_element_type=jnp.float32
    )


def bin_scale(length):
    bins = lax.broadcasted_iota(jnp.int32, (length, 1), 0)
    return jnp.where(bins == 0, 0.5 / length, 1.0 / length)


def signs(length):
    places = lax.broadcasted_iota(jnp.int32, (length, 1), 0)
    return (1 - 2 * lax.rem(places, 2)).astype(jnp.float32)


def modulation(length, decay):
    places = lax.broadcasted_iota(jnp.int32, (length, 1), 0).astype(jnp.float32)
    return jnp.exp(-decay * (places / SEQ)) + SHIFT


def make_taps(
    features, embed, inner, columns, biases, filter_weight, decay, transforms, pre, taps_bins
):
    cos_main, sin_main, cos_small, sin_small = transforms
    main_re, main_im, main_top, small_re, small_im, small_top = taps_bins
    length = features.shape[1]
    region = cos_small.shape[0]
    hidden = None
    for i in range(3):
        if i == 0:
            value = exact(embed[...], features[...], ((0,), (0,)))
        else:
            value = exact(inner[i - 1], hidden, ((0,), (0,)))
        value = value + biases[i]
        pre[i] = value
        hidden = jnp.sin(columns[i] * value)
    taps = exact(hidden, filter_weight[...], ((0,), (0,)))
    taps = (taps * modulation(length, decay[...])).astype(jnp.bfloat16)
    scale = bin_scale(length)
    main_re[...] = dot_nn(cos_main[...], taps) * scale
    main_im[...] = dot_nn(sin_main[...], taps) * scale
    top = jnp.sum(taps.astype(jnp.float32) * signs(length), axis=0, keepdims=True)
    main_top[...] = top * (0.5 / length)
    short = taps[:region]
    scale = bin_scale(region)
    small_re[...] = dot_nn(cos_small[...], short) * scale
    small_im[...] = dot_nn(sin_small[...], short) * scale
    top = jnp.sum(short.astype(jnp.float32) * signs(region), axis=0, keepdims=True)
    small_top[...] = top * (0.5 / region)


def spectra(values, marks, cos_main, sin_main, cos_small, sin_small):
    length = values.shape[0]
    region = cos_small.shape[0]
    main = jnp.where(marks[:, 0:1] > 0, values, 0.0)
    top = jnp.sum(main * signs(length), axis=0, keepdims=True)
    main = main.astype(jnp.bfloat16)
    main_bins = (dot_nn(cos_main[...], main), dot_nn(sin_main[...], main), top)
    head, tail = values[:region], values[length - region :]
    head_slot, tail_slot = marks[:region, 3:4], marks[length - region :, 4:5]
    pieces = [
        jnp.where(head_slot == d, head, 0.0) + jnp.where(tail_slot == d, tail, 0.0)
        for d in range(NDOC)
    ]
    small = jnp.concatenate(pieces, axis=1)
    top = jnp.sum(small * signs(region), axis=0, keepdims=True)
    small = small.astype(jnp.bfloat16)
    small_bins = (dot_nn(cos_small[...], small), dot_nn(sin_small[...], small), top)
    return main_bins, small_bins


def times(left, right, conjugate):
    left_re, left_im, left_top = left
    right_re, right_im, right_top = right
    if conjugate:
        return (
            left_re * right_re + left_im * right_im,
            left_re * right_im - left_im * right_re,
            left_top * right_top,
        )
    return (
        left_re * right_re - left_im * right_im,
        left_re * right_im + left_im * right_re,
        left_top * right_top,
    )


def from_bins(bins, cos_rows, sin_rows):
    real, imag, top = bins
    return (
        dot_nn(cos_rows[...], real.astype(jnp.bfloat16))
        + dot_nn(sin_rows[...], imag.astype(jnp.bfloat16))
        + signs(real.shape[0]) * top
    )


def beside(part):
    return jnp.concatenate([part] * NDOC, axis=1)


def filtered(main_bins, small_bins, taps_main, taps_small, marks, transforms, conjugate):
    cos_main, sin_main, cos_small, sin_small = transforms
    main = from_bins(times(taps_main, main_bins, conjugate), cos_main, sin_main)
    taps_wide = tuple(beside(part) for part in taps_small)
    small = from_bins(times(taps_wide, small_bins, conjugate), cos_small, sin_small)
    length, channels = main.shape
    region = small.shape[0]
    main = jnp.where(marks[:, 0:1] > 0, main, 0.0)
    head, tail = main[:region], main[length - region :]
    head_slot, tail_slot = marks[:region, 3:4], marks[length - region :, 4:5]
    for d in range(NDOC):
        piece = small[:, d * channels : (d + 1) * channels]
        head = head + jnp.where(head_slot == d, piece, 0.0)
        tail = tail + jnp.where(tail_slot == d, piece, 0.0)
    return jnp.concatenate([head, main[region : length - region], tail], axis=0)


def filter_back(
    grad_taps,
    features,
    embed,
    rates,
    inner,
    filter_weight,
    decay,
    pre,
    filter_sums,
    channel_sums,
):
    length = features.shape[1]
    width = filter_weight.shape[0]
    rows = filter_rows(width)
    ones = jnp.ones((8, length), jnp.float32)
    raw = grad_taps[...] * modulation(length, decay[...])
    back = exact(filter_weight[...], raw, ((1,), (1,)))
    for i in (2, 1, 0):
        angle = rates[i] * pre[i]
        if i == 2:
            channel_sums[:width] = exact(jnp.sin(angle), raw, ((1,), (0,)))
        act = back * jnp.cos(angle)
        filter_sums[rows.freq + i : rows.freq + i + 1, :width] = exact(ones, act * pre[i], ((1,), (1,)))[0:1]
        step = act * rates[i]
        bias = exact(ones, step, ((1,), (1,)))[0:1]
        if i == 0:
            filter_sums[rows.embed_bias : rows.embed_bias + 1, :width] = bias
            filter_sums[rows.embed : rows.embed + FEAT, :width] = exact(
                features[...], step, ((1,), (1,))
            )
        else:
            filter_sums[rows.inner_bias + i - 1 : rows.inner_bias + i, :width] = bias
            below = jnp.sin(rates[i - 1] * pre[i - 1])
            filter_sums[:width, (i - 1) * width : i * width] = exact(below, step, ((1,), (1,)))
            back = exact(inner[i - 1], step, ((1,), (0,)))


def shaped(shape, dtype=jnp.float32):
    return jax.ShapeDtypeStruct(shape, dtype)


def row_marks(segment, marks, region):
    ids = to_column(segment[...].astype(jnp.float32)).astype(jnp.int32)
    length = ids.shape[0]
    places = lax.broadcasted_iota(jnp.int32, ids.shape, 0)
    inside = ids == ids[region - 1 : region]
    marks[:, 0:1] = inside.astype(jnp.int32)
    for lag in (1, 2):
        same = (ids == pltpu.roll(ids, lag, 0)) & (places >= lag)
        marks[:, lag : lag + 1] = same.astype(jnp.int32)
    marks[:, 3:4] = jnp.where(inside | (places >= region), -1, ids)
    marks[:, 4:5] = jnp.where(inside | (places < length - region), -1, ids)


BY_INDEX = pl.DeviceIdType.MESH


def greet(devices):
    barrier = pltpu.get_barrier_semaphore()
    for device in devices:
        pl.semaphore_signal(barrier, inc=1, device_id=device, device_id_type=BY_INDEX)
    pl.semaphore_wait(barrier, len(devices))


def remote(source, target, send_sem, recv_sem, device):
    return pltpu.make_async_remote_copy(
        src_ref=source,
        dst_ref=target,
        send_sem=send_sem,
        recv_sem=recv_sem,
        device_id=device,
        device_id_type=BY_INDEX,
    )


def tensor_peers():
    count = lax.axis_size("tensor")
    me = lax.axis_index("tensor")
    return [lax.rem(me + k, count) for k in range(1, count)]


def tensor_devices():
    return [{"tensor": peer} for peer in tensor_peers()]


def sibling():
    me = lax.axis_index("dp")
    return {"dp": me + 1 - 2 * lax.rem(me, 2)}


def chip_peers():
    chips = lax.axis_size("dp") // 2
    me = lax.axis_index("dp")
    core = lax.rem(me, 2)
    result = []
    for k in range(1, chips):
        chip = lax.rem(me // 2 + k, chips)
        result.append((chip, 2 * chip + core))
    return result


def chip_devices():
    return [{"dp": mate} for unused_chip, mate in chip_peers()]


def spread(source, target, sems, devices):
    copies = []
    for k, device in enumerate(devices):
        copies.append(
            remote(
                source(k) if callable(source) else source,
                target(k) if callable(target) else target,
                sems.at[0, k],
                sems.at[1, k],
                device,
            )
        )
        copies[-1].start()
    return copies


def wait_all(copies):
    for copy in copies:
        copy.wait()


def span(index, size):
    return pl.ds(pl.multiple_of(index * size, 16), size)


def staged(pairs, sems):
    copies = []
    for i, (source, target) in enumerate(pairs):
        copies.append(pltpu.make_async_copy(source, target, sems.at[i]))
        copies[-1].start()
    return copies


def to_column(row):
    size = row.shape[1]
    piece = min(size, 128)
    shape = (piece, piece)
    same = lax.broadcasted_iota(jnp.int32, shape, 0) == lax.broadcasted_iota(jnp.int32, shape, 1)
    pieces = [
        jnp.sum(jnp.where(same, row[:, i : i + piece], 0.0), axis=1, keepdims=True)
        for i in range(0, size, piece)
    ]
    return jnp.concatenate(pieces, axis=0)


class Chain:
    def __init__(self, slots, send_sems, recv_sems):
        self.slots, self.send_sems, self.recv_sems = slots, send_sems, recv_sems
        self.count = lax.axis_size("tensor")
        self.me = lax.axis_index("tensor")
        self.rows = slots.shape[1] // 2

    def copy(self, block, half, side):
        step = 1 - 2 * side
        piece = self.slots.at[block, pl.ds(half * self.rows, self.rows)]
        return remote(
            piece,
            piece,
            self.send_sems.at[side, half, block],
            self.recv_sems.at[half, block],
            {"tensor": lax.rem(self.me + step + self.count, self.count)},
        )

    def pass_on(self, step, half, side):
        block = self.me - step * (1 - 2 * side)

        @pl.when((block >= 0) & (block < self.count))
        def _():
            @pl.when(step > 0)
            def _():
                self.copy(block, half, side).wait_recv()

            @pl.when((self.me < self.count - 1) if side == 0 else (self.me > 0))
            def _():
                self.copy(block, half, side).start()

    def advance(self, step):
        for half in range(2):
            for side in range(2):
                self.pass_on(step, half, side)

    def finish(self):
        for block in range(self.count):
            for half in range(2):

                @pl.when((self.me < self.count - 1) & (block <= self.me))
                def _():
                    self.copy(block, half, 0).wait_send()

                @pl.when((self.me > 0) & (block >= self.me))
                def _():
                    self.copy(block, half, 1).wait_send()


def chain_scratch(count):
    return [pltpu.SemaphoreType.DMA((2, 2, count)), pltpu.SemaphoreType.DMA((2, count))]


def normalised(values):
    average = jnp.mean(values, axis=-1, keepdims=True)
    centered = values - average
    variance = jnp.mean(centered * centered, axis=-1, keepdims=True)
    rate = lax.rsqrt(variance + EPS)
    return centered * rate, rate


def norm_back(grad, gain, hat, rate):
    e = grad * gain
    return rate * (
        e
        - jnp.mean(e, axis=-1, keepdims=True)
        - hat * jnp.mean(e * hat, axis=-1, keepdims=True)
    )


def column_sum(values):
    return jnp.sum(values, axis=0, keepdims=True)


def front_kernel(
    tokens,
    gain,
    shift,
    part,
    cotangent,
    segment,
    embed,
    embed_bias,
    freq,
    inner,
    inner_bias,
    filter_weight,
    decay,
    proj_bias,
    short,
    short_bias,
    skip,
    features_hbm,
    proj_hbm,
    cos_main_hbm,
    sin_main_hbm,
    cos_small,
    sin_small,
    out_bias,
    second_gain,
    second_shift,
    first_out,
    part_all,
    cotangent_out,
    pre_out,
    main_re_out,
    main_im_out,
    main_top,
    small_re,
    small_im,
    small_top,
    gated_own,
    projected_out,
    mixed_out,
    summed_out,
    out,
    residual,
    second,
    features,
    proj,
    cos_main,
    sin_main,
    first_all,
    cotangent_all,
    pre,
    main_re,
    main_im,
    projected,
    mixed,
    summed,
    gated,
    held_parts,
    marks,
    load_sems,
    store_sems,
    local_sems,
    first_send,
    first_recv,
    cotangent_send,
    cotangent_recv,
    part_sems,
    chip_sems,
    core_sems,
    gated_sems,
):
    me = lax.axis_index("tensor")
    count = lax.axis_size("tensor")
    place = lax.axis_index("dp")
    core = lax.rem(place, 2)
    chip = place // 2
    peers = tensor_peers()
    shard = tokens.shape[0]
    channels = skip.shape[1]
    taps_bins = (main_re, main_im, main_top, small_re, small_im, small_top)
    transforms = (cos_main, sin_main, cos_small, sin_small)
    loads = staged(
        [
            (proj_hbm, proj),
            (features_hbm, features),
            (cos_main_hbm, cos_main),
            (sin_main_hbm, sin_main),
        ],
        load_sems,
    )
    greet(tensor_devices() + [sibling()] + chip_devices())

    hat, unused_rate = normalised(tokens[...].astype(jnp.float32))
    first_all[me] = (hat * gain[...] + shift[...]).astype(jnp.bfloat16)
    chain = Chain(first_all, first_send, first_recv)
    chain.advance(0)
    cotangent_all[me] = cotangent[...]
    later = Chain(cotangent_all, cotangent_send, cotangent_recv)
    own = pltpu.make_async_copy(part, part_all.at[me, chip, core], local_sems.at[0])
    own.start()
    parts = spread(part, part_all.at[me, chip, core], part_sems, tensor_devices())

    def project(block):
        rows = pl.ds(pl.multiple_of(block * shard, shard), shard)
        for k in range(3):
            lanes = slice(k * channels, (k + 1) * channels)
            projected[rows, lanes] = dot_nn(first_all[block], proj[k]) + proj_bias[k : k + 1]

    wait_all(loads)
    project(me)
    columns = [to_column(freq[i : i + 1]) for i in range(3)]
    biases = [to_column(embed_bias[...])] + [to_column(inner_bias[i : i + 1]) for i in range(2)]
    make_taps(
        features, embed, inner, columns, biases, filter_weight, decay, transforms, pre, taps_bins
    )
    row_marks(segment, marks, cos_small.shape[0])
    stores = [(pre, pre_out), (main_re, main_re_out), (main_im, main_im_out)]
    stored = staged(stores, store_sems)

    def turn(step, carry):
        chain.advance(step)

        def side(index, carry):
            block = me + step * (2 * index - 1)

            @pl.when((block >= 0) & (block < count))
            def _():
                project(block)

            return carry

        return lax.fori_loop(0, 2, side, carry)

    lax.fori_loop(1, 2, turn, 0)
    own.wait()
    wait_all(parts)
    held = part_all.at[:, chip, core]
    parts = spread(held, held, chip_sems, chip_devices())
    lax.fori_loop(2, count, turn, 0)
    later.advance(0)
    more = store_sems.at[pl.ds(len(stores), 5)]
    stored += staged([(first_all, first_out), (projected, projected_out)], more)
    wait_all(parts)
    held = part_all.at[:, :, core]
    parts = spread(held, held, core_sems, [sibling()])

    for k in range(3):
        lanes = slice(k * channels, (k + 1) * channels)
        value = projected[:, lanes]
        running = short_bias[k : k + 1] + short[0, k : k + 1] * value
        for lag in (1, 2):
            moved = jnp.where(marks[:, lag : lag + 1] > 0, pltpu.roll(value, lag, 0), 0.0)
            running = running + short[lag, k : k + 1] * moved
        mixed[:, lanes] = running
    product = mixed[:, 2 * channels :] * mixed[:, channels : 2 * channels]
    more = store_sems.at[pl.ds(len(stores) + 2, 3)]
    stored += staged([(mixed, mixed_out)], more)
    low = product.astype(jnp.bfloat16).astype(jnp.float32)
    main_bins, small_bins = spectra(low, marks, *transforms)
    result = filtered(
        main_bins,
        small_bins,
        (main_re[...], main_im[...], main_top[...]),
        (small_re[...], small_im[...], small_top[...]),
        marks,
        transforms,
        False,
    )
    total = result + skip[...] * product
    summed[...] = total
    gated[...] = (total * mixed[:, :channels]).astype(jnp.bfloat16).reshape(gated.shape)
    swapped = spread(
        lambda k: gated.at[peers[k]], gated_own.at[me], gated_sems, tensor_devices()
    )
    more = store_sems.at[pl.ds(len(stores) + 3, 2)]
    stored += staged([(summed, summed_out)], more)
    gated_own[me] = gated[me]
    wait_all(parts)
    load = pltpu.make_async_copy(part_all, held_parts, local_sems.at[0])
    load.start()
    later.advance(1)
    load.wait()
    wait_all(swapped)
    size = channels // (held_parts.shape[1] * 2)
    base = tokens[...].astype(jnp.float32) + out_bias[...]
    for block in range(count):
        if held_parts.shape[3] == size:
            out[block] = held_parts[block].reshape(out.shape[1:])
        else:
            wide = held_parts[block].astype(jnp.float32)[:, :, :size]
            out[block] = wide.reshape(out.shape[1:]).astype(out.dtype)
        base = base + dot_nn(gated_own[block], out[block])
    residual[...] = base
    hat, unused_rate = normalised(base)
    second[...] = (hat * second_gain[...] + second_shift[...]).astype(jnp.bfloat16)
    for step in range(2, count):
        later.advance(step)
    more = store_sems.at[pl.ds(len(stores) + 4, 1)]
    stored += staged([(cotangent_all, cotangent_out)], more)
    chain.finish()
    later.finish()
    wait_all(stored)


def middle_kernel(
    second_own,
    gain,
    bias,
    cotangent_hbm,
    up_hbm,
    down_hbm,
    residual_hbm,
    gated_hbm,
    out_hbm,
    grad_residual,
    mlp_out,
    up_out,
    down_out,
    bias_grad,
    grad_gated,
    out_grad,
    gain_sum,
    shift_sum,
    out_sum,
    down_sum,
    cotangent,
    up,
    down,
    residual,
    gated,
    out,
    mlp,
    up_grad,
    down_grad,
    second,
    active,
    low,
    parting,
    arriving,
    own_part,
    load_sems,
    store_sems,
    second_send,
    second_recv,
    part_send,
    part_recv,
):
    me = lax.axis_index("tensor")
    count = lax.axis_size("tensor")
    shard, width = second_own.shape
    units = up.shape[1]
    loads = staged(
        [
            (up_hbm, up),
            (down_hbm, down),
            (cotangent_hbm, cotangent),
            (residual_hbm, residual),
            (gated_hbm, gated),
            (out_hbm, out),
        ],
        load_sems,
    )
    greet(tensor_devices())
    second[me] = second_own[...]
    chain = Chain(second, second_send, second_recv)
    bias_grad[...] = jnp.zeros_like(bias_grad)

    def sent(block):
        return remote(
            parting.at[block],
            arriving.at[me],
            part_send.at[block],
            part_recv.at[me],
            {"tensor": block},
        )

    def work(block):
        cut = units // 2
        for lanes in (slice(0, cut), slice(cut, units)):
            hidden = dot_nn(second[block], up[:, lanes]) + bias[:, lanes]
            cube = GELU_CUBE * hidden * hidden
            slope = jnp.tanh(GELU_RATE * hidden * (1.0 + cube))
            gate = 0.5 * (1.0 + slope)
            active[block, :, lanes] = (hidden * gate).astype(jnp.bfloat16)
            rate = gate + (0.5 * GELU_RATE) * hidden * (1.0 - slope * slope) * (1.0 + 3.0 * cube)
            grad_hidden = dot_nt(cotangent[block], down[lanes]) * rate
            bias_grad[:, lanes] += column_sum(grad_hidden)
            low[block, :, lanes] = grad_hidden.astype(jnp.bfloat16)
        part = dot_nt(low[block], up[...])

        @pl.when(block == me)
        def _():
            own_part[...] = part

        @pl.when(block != me)
        def _():
            parting[block] = part.astype(jnp.bfloat16)
            sent(block).start()

        mlp[block] = dot_nn(active[block], down[...]).astype(jnp.bfloat16)

    def turn(step, carry):
        chain.advance(step)

        @pl.when(step == 0)
        def _():
            wait_all(loads[:3])

        def side(index, carry):
            block = me + step * (2 * index - 1)

            @pl.when((block >= 0) & (block < count) & ((step > 0) | (index == 0)))
            def _():
                work(block)

            return carry

        return lax.fori_loop(0, 2, side, carry)

    lax.fori_loop(0, count, turn, 0)
    stored = staged([(mlp, mlp_out)], store_sems)
    tokens_all = count * shard
    up_grad[...] = dot_tn(
        second[...].reshape(tokens_all, width), low[...].reshape(tokens_all, units)
    ).astype(jnp.bfloat16)
    down_grad[...] = dot_tn(
        active[...].reshape(tokens_all, units), cotangent[...].reshape(tokens_all, width)
    ).astype(jnp.bfloat16)
    stored += staged([(up_grad, up_out), (down_grad, down_out)], store_sems.at[pl.ds(1, 2)])
    wait_all(loads[3:])
    for peer in tensor_peers():
        remote(
            parting.at[peer],
            arriving.at[peer],
            part_send.at[peer],
            part_recv.at[peer],
            {"tensor": peer},
        ).wait_recv()
        own_part[...] += arriving[peer].astype(jnp.float32)
    grad_normed = own_part[...]
    hat, rate = normalised(residual[...])
    grad_out = cotangent[me].astype(jnp.float32)
    grad = grad_out + norm_back(grad_normed, gain[...], hat, rate)
    grad_residual[...] = grad
    gain_sum[...] = column_sum(grad_normed * hat)
    shift_sum[...] = column_sum(grad_normed)
    out_sum[...] = column_sum(grad)
    down_sum[...] = column_sum(grad_out)
    grad_low = grad.astype(jnp.bfloat16)
    for block in range(count):
        grad_gated[block] = dot_nt(grad_low, out[block]).astype(jnp.bfloat16)
        out_grad[block] = dot_tn(gated[block], grad_low).astype(jnp.bfloat16)
    chain.finish()
    for peer in tensor_peers():
        sent(peer).wait_send()
    wait_all(stored)


class RowReduce:
    def __init__(self, source, part, refs):
        half, core_recv, chip_recv, load_sem, core_sems, chip_sems = refs[:6]
        self.source, self.part, self.half = source, part, half
        self.core_recv, self.chip_recv = core_recv, chip_recv
        self.load_sem, self.core_sems, self.chip_sems = load_sem, core_sems, chip_sems
        self.across = tuple(refs[6:])
        place = lax.axis_index("dp")
        self.core, self.chip = lax.rem(place, 2), place // 2
        self.chips = lax.axis_size("dp") // 2
        self.rows = half.shape[-2]
        self.size = self.rows // self.chips

    def pair(self):
        self.load = pltpu.make_async_copy(
            self.source.at[..., span(self.core, self.rows), :], self.half, self.load_sem.at[0]
        )
        self.load.start()
        self.copies = spread(
            self.source.at[..., span(1 - self.core, self.rows), :],
            self.core_recv,
            self.core_sems,
            [sibling()],
        )

    def plane(self):
        self.load.wait()
        wait_all(self.copies)
        self.half[...] = (
            self.half[...].astype(jnp.float32) + self.core_recv[...].astype(jnp.float32)
        ).astype(self.half.dtype)
        mates = chip_peers()
        self.copies = spread(
            lambda k: self.half.at[..., span(mates[k][0], self.size), :],
            lambda k: self.chip_recv.at[k],
            self.chip_sems,
            chip_devices(),
        )

    def gathered(self):
        value = self.half[..., span(self.chip, self.size), :].astype(jnp.float32)
        for k, copy in enumerate(self.copies):
            copy.wait()
            value = value + self.chip_recv[k].astype(jnp.float32)
        return value

    def cross(self):
        held, held_recv, sems = self.across
        held[...] = self.gathered().astype(held.dtype)
        peers = tensor_peers()
        self.copies = spread(
            lambda k: held.at[peers[k]], lambda k: held_recv.at[k], sems, tensor_devices()
        )

    def crossed(self):
        held, held_recv, sems = self.across
        value = held[lax.axis_index("tensor")].astype(jnp.float32)
        for k, copy in enumerate(self.copies):
            copy.wait()
            value = value + held_recv[k].astype(jnp.float32)
        return value

    def finish(self):
        value = self.crossed() if self.across else self.gathered()
        self.part[...] = value.astype(self.part.dtype)


def row_reduce_scratch(shape, chips):
    rows, columns = shape[-2:]
    lead = tuple(shape[:-2])
    size = rows // 2 // chips
    low = jnp.bfloat16
    scratch = [
        pltpu.VMEM(lead + (rows // 2, columns), low),
        pltpu.VMEM(lead + (rows // 2, columns), low),
        pltpu.VMEM((chips - 1,) + lead + (size, columns), low),
        pltpu.SemaphoreType.DMA((1,)),
        pltpu.SemaphoreType.DMA((2, 1)),
        pltpu.SemaphoreType.DMA((2, chips - 1)),
    ]
    if lead:
        scratch += [
            pltpu.VMEM(lead + (size, columns), low),
            pltpu.VMEM((lead[0] - 1, size, columns), low),
            pltpu.SemaphoreType.DMA((2, lead[0] - 1)),
        ]
    return scratch


class RowGather:
    def __init__(self, part, total, refs):
        self.part, self.total = part, total
        self.own_sem, self.chip_sems, self.core_sems = refs
        place = lax.axis_index("dp")
        core, chip = lax.rem(place, 2), place // 2
        chips = lax.axis_size("dp") // 2
        self.mine = span(core * chips + chip, part.shape[0])
        self.half = span(core, part.shape[0] * chips)

    def plane(self):
        own = self.total.at[self.mine]
        self.copies = staged([(self.part, own)], self.own_sem)
        self.copies += spread(self.part, own, self.chip_sems, chip_devices())

    def pair(self):
        wait_all(self.copies)
        own = self.total.at[self.half]
        self.copies = spread(own, own, self.core_sems, [sibling()])

    def finish(self):
        wait_all(self.copies)


def row_gather_scratch(chips):
    return [
        pltpu.SemaphoreType.DMA((1,)),
        pltpu.SemaphoreType.DMA((2, chips - 1)),
        pltpu.SemaphoreType.DMA((2, 1)),
    ]


class SmallSums:
    def __init__(self, sources, results, wide, refs):
        self.sources, self.results, self.wide = sources, results, wide
        count = len(sources)
        self.core_recv = refs[:count]
        self.chip_slots = refs[count : 2 * count]
        self.group_slots = refs[2 * count : 2 * count + wide]
        self.core_sems, self.chip_sems, self.group_sems = refs[2 * count + wide :]
        self.me = lax.axis_index("tensor")
        self.chip = lax.axis_index("dp") // 2

    def pair(self):
        self.copies = []
        for i, source in enumerate(self.sources):
            self.copies += spread(source, self.core_recv[i], self.core_sems.at[i], [sibling()])

    def plane(self):
        wait_all(self.copies)
        self.copies = []
        for i, source in enumerate(self.sources):
            self.chip_slots[i][self.chip] = source[...] + self.core_recv[i][...]
            own = self.chip_slots[i].at[self.chip]
            self.copies += spread(own, own, self.chip_sems.at[i], chip_devices())

    def total(self, slots):
        value = slots[0]
        for i in range(1, slots.shape[0]):
            value = value + slots[i]
        return value

    def tensor(self):
        wait_all(self.copies)
        self.copies = []
        for i in range(len(self.sources)):
            if i >= self.wide:
                self.results[i][...] = self.total(self.chip_slots[i])
                continue
            self.group_slots[i][self.me] = self.total(self.chip_slots[i])
            own = self.group_slots[i].at[self.me]
            self.copies += spread(own, own, self.group_sems.at[i], tensor_devices())

    def finish(self):
        wait_all(self.copies)
        for i in range(self.wide):
            self.results[i][...] = self.total(self.group_slots[i])


def small_sums_scratch(shapes, wide, chips, groups):
    return (
        [pltpu.VMEM(shape, jnp.float32) for shape in shapes]
        + [pltpu.VMEM((chips,) + tuple(shape), jnp.float32) for shape in shapes]
        + [pltpu.VMEM((groups,) + tuple(shape), jnp.float32) for shape in shapes[:wide]]
        + [
            pltpu.SemaphoreType.DMA((len(shapes), 2, 1)),
            pltpu.SemaphoreType.DMA((len(shapes), 2, chips - 1)),
            pltpu.SemaphoreType.DMA((max(wide, 1), 2, groups - 1)),
        ]
    )


class channel_rows:
    def __init__(self, width):
        self.filter = 0
        self.short = width
        self.short_bias = width + 9
        self.proj_bias = width + 12
        self.skip = width + 15
        self.size = width + 16


class filter_rows:
    def __init__(self, width):
        self.embed = width
        self.embed_bias = self.embed + FEAT + -FEAT % 8
        self.freq = self.embed_bias + 1
        self.inner_bias = self.embed_bias + 4
        self.size = self.embed_bias + 8


def back_kernel(
    grad_blocks,
    mlp,
    up_grad,
    down_grad,
    out_grad,
    short,
    skip,
    segment,
    embed,
    freq,
    inner,
    filter_weight,
    decay,
    main_top,
    small_re,
    small_im,
    small_top,
    cos_small,
    sin_small,
    mixed_hbm,
    cos_main_hbm,
    sin_main_hbm,
    main_re_hbm,
    main_im_hbm,
    summed_hbm,
    projected_hbm,
    proj_hbm,
    features_hbm,
    pre_hbm,
    grad_first,
    grad_low,
    mlp_sum,
    up_sum,
    down_part,
    out_part,
    filter_sums,
    channel_sums,
    mixed,
    cos_main,
    sin_main,
    main_re,
    main_im,
    summed,
    projected,
    proj,
    features,
    pre,
    grad_gated,
    grad_taps,
    marks,
    mlp_own,
    mlp_recv,
    up_part,
    load_sems,
    local_sems,
    gated_sems,
    mlp_sems,
    *scratch,
):
    me = lax.axis_index("tensor")
    count = lax.axis_size("tensor")
    peers = tensor_peers()
    channels = skip.shape[1]
    length = projected.shape[0]
    region = cos_small.shape[0]
    shard = length // count
    transforms = (cos_main, sin_main, cos_small, sin_small)
    loads = staged(
        [
            (mixed_hbm, mixed),
            (cos_main_hbm, cos_main),
            (sin_main_hbm, sin_main),
            (main_re_hbm, main_re),
            (main_im_hbm, main_im),
            (summed_hbm, summed),
            (projected_hbm, projected),
            (proj_hbm, proj),
            (features_hbm, features),
            (pre_hbm, pre),
        ],
        load_sems,
    )
    greet(tensor_devices() + [sibling()] + chip_devices())
    up_row = RowReduce(up_grad, up_part, scratch[:6])
    down_row = RowReduce(down_grad, down_part, scratch[6:12])
    out_row = RowReduce(out_grad, out_part, scratch[12:21])
    weights = (up_row, down_row, out_row)
    up_all = RowGather(up_part, up_sum, scratch[21:24])
    places = channel_rows(filter_weight.shape[0])
    filter_sums[...] = jnp.zeros_like(filter_sums)
    own = pltpu.make_async_copy(grad_blocks.at[me], grad_gated.at[me], local_sems.at[0])
    own.start()
    arriving = spread(
        lambda k: grad_blocks.at[peers[k]], grad_gated.at[me], gated_sems, tensor_devices()
    )
    for weight in weights:
        weight.pair()
    own_mlp = pltpu.make_async_copy(mlp.at[me], mlp_own, local_sems.at[1])
    own_mlp.start()
    row_marks(segment, marks, region)
    wait_all(loads[:3])
    gate_out = mixed[:, :channels]
    gate_in = mixed[:, channels : 2 * channels]
    values = mixed[:, 2 * channels :]
    product = values * gate_in
    low = product.astype(jnp.bfloat16).astype(jnp.float32)
    value_main, value_small = spectra(low, marks, *transforms)
    up_row.plane()
    out_row.plane()
    own.wait()
    wait_all(arriving)
    mlps = spread(
        lambda k: mlp.at[peers[k]], lambda k: mlp_recv.at[k], mlp_sems, tensor_devices()
    )
    grad = grad_gated[...].reshape(length, channels).astype(jnp.float32)
    grad_summed = grad * gate_out
    channel_sums[places.skip : places.skip + 1] = column_sum(grad_summed * product)
    low = grad_summed.astype(jnp.bfloat16).astype(jnp.float32)
    grad_main, grad_small = spectra(low, marks, *transforms)
    real, imag, top = times(value_main, grad_main, True)
    scale = bin_scale(length)
    taps = from_bins((real * scale, imag * scale, top * (0.5 / length)), cos_main, sin_main)
    scale = bin_scale(region)
    real, imag, top = (
        sum(part[:, d * channels : (d + 1) * channels] for d in range(NDOC))
        for part in times(value_small, grad_small, True)
    )
    taps_small = from_bins((real * scale, imag * scale, top * (0.5 / region)), cos_small, sin_small)
    grad_taps[:region] = taps[:region] + taps_small
    grad_taps[region:] = taps[region:]
    down_row.plane()
    wait_all(loads[3:])
    result = filtered(
        grad_main,
        grad_small,
        (main_re[...], main_im[...], main_top[...]),
        (small_re[...], small_im[...], small_top[...]),
        marks,
        transforms,
        True,
    )
    grad_product = result + grad_summed * skip[...]
    parts = (grad * summed[...], grad_product * values, grad_product * gate_in)
    for k, part in enumerate(parts):
        lanes = slice(k * channels, (k + 1) * channels)
        source = projected[:, lanes]
        row = places.short_bias + k
        channel_sums[row : row + 1] = column_sum(part)
        row = places.short + k
        channel_sums[row : row + 1] = column_sum(part * source)
        running = short[0, k : k + 1] * part
        for lag in (1, 2):
            kept = jnp.where(marks[:, lag : lag + 1] > 0, part, 0.0)
            row = places.short + 3 * lag + k
            channel_sums[row : row + 1] = column_sum(kept * pltpu.roll(source, lag, 0))
            running = running + short[lag, k : k + 1] * pltpu.roll(kept, length - lag, 0)
        row = places.proj_bias + k
        channel_sums[row : row + 1] = column_sum(running)
        grad_low[:, lanes] = running.astype(jnp.bfloat16)
    out_row.cross()
    for block in range(count):
        rows = slice(block * shard, (block + 1) * shard)
        total = dot_nt(grad_low[rows, :channels], proj[0])
        for k in (1, 2):
            total = total + dot_nt(grad_low[rows, k * channels : (k + 1) * channels], proj[k])
        grad_first[block] = total.astype(jnp.bfloat16)
    up_row.finish()
    up_all.plane()
    filter_back(
        grad_taps,
        features,
        embed,
        [to_column(freq[i : i + 1]) for i in range(3)],
        inner,
        filter_weight,
        decay,
        pre,
        filter_sums,
        channel_sums,
    )
    up_all.pair()
    for weight in (down_row, out_row):
        weight.finish()
    own_mlp.wait()
    total = mlp_own[...].astype(jnp.float32)
    for k, copy in enumerate(mlps):
        copy.wait()
        total = total + mlp_recv[k].astype(jnp.float32)
    mlp_sum[...] = total
    up_all.finish()


def final_kernel(
    grad_first,
    tokens,
    gain,
    shift,
    out_bias_sum,
    gain_sum,
    shift_sum,
    down_bias_sum,
    filter_sums,
    channel_sums,
    up_bias_sum,
    down_part,
    out_part,
    first_hbm,
    grad_low_hbm,
    grad_tokens,
    proj_sum,
    down_sum,
    out_sum,
    line_all,
    filter_all,
    channel_all,
    up_bias_all,
    first,
    grad_low,
    proj_grad,
    proj_part,
    lines,
    load_sems,
    block_recv,
    block_sems,
    *scratch,
):
    me = lax.axis_index("tensor")
    count = lax.axis_size("tensor")
    peers = tensor_peers()
    loads = staged([(first_hbm, first), (grad_low_hbm, grad_low)], load_sems)
    greet(tensor_devices() + [sibling()] + chip_devices())
    blocks = spread(
        lambda k: grad_first.at[peers[k]], lambda k: block_recv.at[k], block_sems, tensor_devices()
    )
    row = RowReduce(proj_grad, proj_part, scratch[:6])
    proj_all = RowGather(proj_part, proj_sum, scratch[6:9])
    gathers = (
        RowGather(down_part, down_sum, scratch[9:12]),
        RowGather(out_part, out_sum, scratch[12:15]),
    )
    small = SmallSums(
        (lines, filter_sums, channel_sums, up_bias_sum),
        (line_all, filter_all, channel_all, up_bias_all),
        2,
        scratch[15:],
    )
    length, columns = grad_low.shape
    channels = columns // 3
    width = tokens.shape[1]
    wait_all(loads)
    for k in range(3):
        proj_grad[k * width : (k + 1) * width] = dot_tn(
            first[...].reshape(length, width), grad_low[:, k * channels : (k + 1) * channels]
        ).astype(jnp.bfloat16)
    row.pair()
    row.plane()
    plain = jnp.zeros_like(gain[...])
    scaled = jnp.zeros_like(gain[...])
    for block in range(count):
        grad = grad_first[block].astype(jnp.float32)
        plain = plain + column_sum(grad)
        scaled = scaled + column_sum(grad * first[block].astype(jnp.float32))
    lines[0:1] = out_bias_sum[...]
    lines[1:2] = gain_sum[...]
    lines[2:3] = shift_sum[...]
    lines[3:4] = down_bias_sum[...]
    lines[4:5] = (scaled - shift[...] * plain) / gain[...]
    lines[5:6] = plain
    lines[6:8] = jnp.zeros_like(lines[6:8])
    small.pair()
    hat, rate = normalised(tokens[...].astype(jnp.float32))
    small.plane()
    row.finish()
    proj_all.plane()
    for gather in gathers:
        gather.plane()
    small.tensor()
    proj_all.pair()
    for gather in gathers:
        gather.pair()
    small.finish()
    grad = grad_first[me].astype(jnp.float32)
    for k, copy in enumerate(blocks):
        copy.wait()
        grad = grad + block_recv[k].astype(jnp.float32)
    grad_tokens[...] = norm_back(grad, gain[...], hat, rate)
    for gather in gathers + (proj_all,):
        gather.finish()


def finish_kernel(
    residual,
    mlp_sum,
    down_bias,
    grad_tokens,
    grad_residual,
    proj_sum,
    up_sum,
    down_sum,
    out_sum,
    line_all,
    filter_all,
    channel_all,
    up_bias_all,
    layer_out,
    tokens_out,
    proj_out,
    up_out,
    down_out,
    out_out,
    out_bias_out,
    gain2_out,
    shift2_out,
    down_bias_out,
    gain1_out,
    shift1_out,
    embed_out,
    embed_bias_out,
    freq_out,
    inner_out,
    inner_bias_out,
    filter_out,
    short_out,
    short_bias_out,
    proj_bias_out,
    skip_out,
    up_bias_out,
):
    layer_out[...] = (residual[...] + mlp_sum[...] + down_bias[...]).astype(layer_out.dtype)
    tokens_out[...] = grad_tokens[...] + grad_residual[...]
    for source, target in (
        (proj_sum, proj_out),
        (up_sum, up_out),
        (down_sum, down_out),
        (out_sum, out_out),
    ):
        target[...] = source[...].astype(jnp.float32)

    @pl.when(pl.program_id(0) == 0)
    def _():
        lines = (out_bias_out, gain2_out, shift2_out, down_bias_out, gain1_out, shift1_out)
        for i, line in enumerate(lines):
            line[...] = line_all[i : i + 1]
        width = filter_out.shape[0]
        rows = filter_rows(width)
        for i in range(2):
            inner_out[i] = filter_all[:width, i * width : (i + 1) * width]
        embed_out[...] = filter_all[rows.embed : rows.embed + FEAT, :width]
        embed_bias_out[...] = filter_all[rows.embed_bias : rows.embed_bias + 1, :width]
        freq_out[...] = filter_all[rows.freq : rows.freq + 3, :width]
        inner_bias_out[...] = filter_all[rows.inner_bias : rows.inner_bias + 2, :width]
        rows = channel_rows(width)
        filter_out[...] = channel_all[:width]
        for lag in range(3):
            row = rows.short + 3 * lag
            short_out[lag] = channel_all[row : row + 3]
        short_bias_out[...] = channel_all[rows.short_bias : rows.short_bias + 3]
        proj_bias_out[...] = channel_all[rows.proj_bias : rows.proj_bias + 3]
        skip_out[...] = channel_all[rows.skip : rows.skip + 1]
        up_bias_out[...] = up_bias_all[...]


def finish(big, shapes):
    steps = 4

    def rows(shape):
        return pl.BlockSpec((shape[0] // steps, shape[1]), lambda i: (i, 0))

    def whole(shape):
        return pl.BlockSpec(tuple(shape), lambda i: (0,) * len(shape))

    in_specs = [
        whole(array.shape) if i == 2 or i > 8 else rows(array.shape) for i, array in enumerate(big)
    ]
    out_specs = [rows(shape.shape) if i < 6 else whole(shape.shape) for i, shape in enumerate(shapes)]
    return pl.pallas_call(
        finish_kernel,
        grid=(steps,),
        in_specs=in_specs,
        out_specs=out_specs,
        out_shape=shapes,
        compiler_params=pltpu.CompilerParams(
            dimension_semantics=("arbitrary",), vmem_limit_bytes=60 * 1024 * 1024
        ),
        name="finish",
    )(*big)


def communicate(kernel, shapes, operands, anywhere, scratch, channel, name):
    vmem = pl.BlockSpec(memory_space=pltpu.VMEM)
    free = pl.BlockSpec(memory_space=pl.ANY)
    return pl.pallas_call(
        kernel,
        out_shape=shapes,
        in_specs=[free if i in anywhere[0] else vmem for i in range(len(operands))],
        out_specs=[free if i in anywhere[1] else vmem for i in range(len(shapes))],
        scratch_shapes=scratch,
        compiler_params=pltpu.CompilerParams(
            collective_id=channel, has_side_effects=True, vmem_limit_bytes=60 * 1024 * 1024
        ),
        cost_estimate=pl.CostEstimate(flops=0, bytes_accessed=200_000_000, transcendentals=0),
        name=name,
    )(*operands)


def body(
    tokens,
    segment_ids,
    norm1_gain,
    norm1_bias,
    proj_weight,
    proj_bias,
    short_weight,
    short_bias,
    embed_weight,
    embed_bias,
    sine_freq,
    inner_weight,
    inner_bias,
    filter_weight,
    decay_rate,
    skip_gain,
    out_weight,
    out_bias,
    norm2_gain,
    norm2_bias,
    up_weight,
    up_bias,
    down_weight,
    down_bias,
    cotangent,
):
    row_count, shard_len, model_width = tokens.shape
    groups = lax.axis_size("tensor")
    rows = lax.axis_size("dp")
    place = lax.axis_index("tensor")
    row_place = lax.axis_index("dp")
    length = shard_len * groups
    channels = proj_weight.shape[2]
    units = up_weight.shape[1]
    channel_slice = channels // rows

    out_part = lax.dynamic_slice_in_dim(out_weight, row_place * channel_slice, channel_slice, 0)
    out_rows = -(-channel_slice // 16) * 16
    out_part = jnp.pad(out_part, ((0, out_rows - channel_slice), (0, 0)))

    low = jnp.bfloat16
    region = shard_len
    chips = rows // 2
    proj_columns = 3 * channels
    cos_main, sin_main = transform(length)
    cos_small, sin_small = transform(region)
    features = features_by_row()
    decay = decay_rate[None]
    width = embed_weight.shape[1]
    embed_bias = embed_bias[None]
    proj = proj_weight.transpose(1, 0, 2)
    skip = skip_gain[None]
    semaphores = pltpu.SemaphoreType.DMA
    vmem = pltpu.VMEM
    single = jnp.float32
    blocked = (groups, shard_len, model_width)
    swapped = (groups, shard_len, channels)
    line = (1, model_width)
    (
        first_all,
        unused_parts,
        all_cotangent,
        pre,
        main_re,
        main_im,
        main_top,
        small_re,
        small_im,
        small_top,
        gated_own,
        projected,
        mixed,
        summed,
        out_all,
        residual,
        second,
    ) = communicate(
        front_kernel,
        [
            shaped(blocked, low),
            shaped((groups, chips, 2) + out_part.shape, low),
            shaped(blocked, low),
            shaped((3, width, length)),
            shaped((length, channels)),
            shaped((length, channels)),
            shaped((1, channels)),
            shaped((region, channels)),
            shaped((region, channels)),
            shaped((1, channels)),
            shaped(swapped, low),
            shaped((length, proj_columns)),
            shaped((length, proj_columns)),
            shaped((length, channels)),
            shaped((groups, channels, model_width), low),
            shaped((shard_len, model_width)),
            shaped((shard_len, model_width), low),
        ],
        [
            tokens[0],
            norm1_gain[None],
            norm1_bias[None],
            out_part,
            cotangent[0],
            segment_ids,
            embed_weight,
            embed_bias,
            sine_freq,
            inner_weight,
            inner_bias,
            filter_weight,
            decay,
            proj_bias,
            short_weight,
            short_bias,
            skip,
            features,
            proj,
            cos_main,
            sin_main,
            cos_small,
            sin_small,
            out_bias[None],
            norm2_gain[None],
            norm2_bias[None],
        ],
        ((3, 17, 18, 19, 20), (0, 1, 2, 3, 4, 5, 11, 12, 13)),
        [
            vmem(features.shape, single),
            vmem(proj.shape, low),
            vmem(cos_main.shape, low),
            vmem(sin_main.shape, low),
            vmem(blocked, low),
            vmem(blocked, low),
            vmem((3, width, length), single),
            vmem((length, channels), single),
            vmem((length, channels), single),
            vmem((length, proj_columns), single),
            vmem((length, proj_columns), single),
            vmem((length, channels), single),
            vmem(swapped, low),
            vmem((groups, chips, 2) + out_part.shape, low),
            vmem((length, 8), jnp.int32),
            semaphores((4,)),
            semaphores((8,)),
            semaphores((1,)),
            *chain_scratch(groups),
            *chain_scratch(groups),
            semaphores((2, groups - 1)),
            semaphores((2, chips - 1)),
            semaphores((2, 1)),
            semaphores((2, groups - 1)),
        ],
        0,
        "front",
    )
    (
        grad_residual,
        mlp_partial,
        up_grad,
        down_grad,
        grad_up_bias,
        grad_gated,
        out_grad,
        grad_norm2_gain,
        grad_norm2_bias,
        grad_out_bias,
        grad_down_bias,
    ) = communicate(
        middle_kernel,
        [
            shaped((shard_len, model_width)),
            shaped(blocked, low),
            shaped((model_width, units), low),
            shaped((units, model_width), low),
            shaped((1, units)),
            shaped(swapped, low),
            shaped((groups, channels, model_width), low),
            shaped(line),
            shaped(line),
            shaped(line),
            shaped(line),
        ],
        [
            second,
            norm2_gain[None],
            up_bias[None],
            all_cotangent,
            up_weight,
            down_weight,
            residual,
            gated_own,
            out_all,
        ],
        ((3, 4, 5, 6, 7, 8), (1, 2, 3)),
        [
            vmem(blocked, low),
            vmem((model_width, units), low),
            vmem((units, model_width), low),
            vmem((shard_len, model_width), single),
            vmem(swapped, low),
            vmem((groups, channels, model_width), low),
            vmem(blocked, low),
            vmem((model_width, units), low),
            vmem((units, model_width), low),
            vmem(blocked, low),
            vmem((groups, shard_len, units), low),
            vmem((groups, shard_len, units), low),
            vmem(blocked, low),
            vmem(blocked, low),
            vmem((shard_len, model_width), single),
            semaphores((6,)),
            semaphores((3,)),
            *chain_scratch(groups),
            semaphores((groups,)),
            semaphores((groups,)),
        ],
        1,
        "middle",
    )
    fold = max(1, 32 * chips // channels)
    out_grad = out_grad.reshape(groups, channels * fold, model_width // fold)
    out_size = (channels * fold // rows, model_width // fold)
    filter_shape = (filter_rows(width).size, 2 * width)
    channel_shape = (channel_rows(width).size, channels)
    (
        grad_first,
        grad_low,
        mlp_out,
        up_sum,
        down_part,
        out_part,
        filter_sums,
        channel_sums,
    ) = communicate(
        back_kernel,
        [
            shaped(blocked, low),
            shaped((length, proj_columns), low),
            shaped((shard_len, model_width)),
            shaped(up_grad.shape, low),
            shaped((units // rows, model_width), low),
            shaped(out_size, low),
            shaped(filter_shape),
            shaped(channel_shape),
        ],
        [
            grad_gated,
            mlp_partial,
            up_grad,
            down_grad,
            out_grad,
            short_weight,
            skip,
            segment_ids,
            embed_weight,
            sine_freq,
            inner_weight,
            filter_weight,
            decay,
            main_top,
            small_re,
            small_im,
            small_top,
            cos_small,
            sin_small,
            mixed,
            cos_main,
            sin_main,
            main_re,
            main_im,
            summed,
            projected,
            proj,
            features,
            pre,
        ],
        ((0, 1, 2, 3, 4, 19, 20, 21, 22, 23, 24, 25, 26, 27, 28), (3,)),
        [
            vmem((length, proj_columns), single),
            vmem(cos_main.shape, low),
            vmem(sin_main.shape, low),
            vmem((length, channels), single),
            vmem((length, channels), single),
            vmem((length, channels), single),
            vmem((length, proj_columns), single),
            vmem(proj.shape, low),
            vmem(features.shape, single),
            vmem(pre.shape, single),
            vmem(swapped, low),
            vmem((length, channels), single),
            vmem((length, 8), jnp.int32),
            vmem((shard_len, model_width), low),
            vmem((groups - 1, shard_len, model_width), low),
            vmem((model_width // rows, units), low),
            semaphores((10,)),
            semaphores((2,)),
            semaphores((2, groups - 1)),
            semaphores((2, groups - 1)),
        ]
        + row_reduce_scratch(up_grad.shape, chips)
        + row_reduce_scratch(down_grad.shape, chips)
        + row_reduce_scratch(out_grad.shape, chips)
        + row_gather_scratch(chips),
        2,
        "back",
    )
    (
        grad_tokens,
        proj_sum,
        down_sum,
        out_sum,
        line_all,
        filter_all,
        channel_all,
        up_bias_all,
    ) = communicate(
        final_kernel,
        [
            shaped((shard_len, model_width)),
            shaped((3 * model_width, channels), low),
            shaped(down_grad.shape, low),
            shaped(out_grad.shape[1:], low),
            shaped((8, model_width)),
            shaped(filter_shape),
            shaped(channel_shape),
            shaped(grad_up_bias.shape),
        ],
        [
            grad_first,
            tokens[0],
            norm1_gain[None],
            norm1_bias[None],
            grad_out_bias,
            grad_norm2_gain,
            grad_norm2_bias,
            grad_down_bias,
            filter_sums,
            channel_sums,
            grad_up_bias,
            down_part,
            out_part,
            first_all,
            grad_low,
        ],
        ((13, 14), (1, 2, 3)),
        [
            vmem(blocked, low),
            vmem((length, proj_columns), low),
            vmem((3 * model_width, channels), low),
            vmem((3 * model_width // rows, channels), low),
            vmem((8, model_width), single),
            semaphores((2,)),
            vmem((groups - 1, shard_len, model_width), low),
            semaphores((2, groups - 1)),
        ]
        + row_reduce_scratch((3 * model_width, channels), chips)
        + row_gather_scratch(chips) * 3
        + small_sums_scratch(
            [(8, model_width), filter_shape, channel_shape, grad_up_bias.shape], 2, chips, groups
        ),
        3,
        "final",
    )
    (
        layer_out,
        grad_tokens,
        grad_proj_weight,
        grad_up_weight,
        grad_down_weight,
        grad_out_weight,
        grad_out_bias,
        grad_norm2_gain,
        grad_norm2_bias,
        grad_down_bias,
        grad_norm1_gain,
        grad_norm1_bias,
        grad_embed_weight,
        grad_embed_bias,
        grad_sine_freq,
        grad_inner_weight,
        grad_inner_bias,
        grad_filter_weight,
        grad_short_weight,
        grad_short_bias,
        grad_proj_bias,
        grad_skip_gain,
        grad_up_bias,
    ) = finish(
        [
            residual,
            mlp_out,
            down_bias[None],
            grad_tokens,
            grad_residual,
            proj_sum,
            up_sum,
            down_sum,
            out_sum.reshape(out_weight.shape),
            line_all,
            filter_all,
            channel_all,
            up_bias_all,
        ],
        [
            shaped((shard_len, model_width), low),
            shaped((shard_len, model_width)),
            shaped((3 * model_width, channels)),
            shaped(up_weight.shape),
            shaped(down_weight.shape),
            shaped(out_weight.shape),
            shaped(line),
            shaped(line),
            shaped(line),
            shaped(line),
            shaped(line),
            shaped(line),
            shaped(embed_weight.shape),
            shaped(embed_bias.shape),
            shaped(sine_freq.shape),
            shaped(inner_weight.shape),
            shaped(inner_bias.shape),
            shaped(filter_weight.shape),
            shaped(short_weight.shape),
            shaped(short_bias.shape),
            shaped(proj_bias.shape),
            shaped(skip.shape),
            shaped(up_bias_all.shape),
        ],
    )
    grad_proj_weight = grad_proj_weight.reshape(3, model_width, channels).transpose(1, 0, 2)
    return (
        layer_out[None],
        grad_tokens[None],
        grad_norm1_gain[0],
        grad_norm1_bias[0],
        grad_proj_weight,
        grad_proj_bias,
        grad_short_weight,
        grad_short_bias,
        grad_embed_weight,
        grad_embed_bias[0],
        grad_sine_freq,
        grad_inner_weight,
        grad_inner_bias,
        grad_filter_weight,
        grad_skip_gain[0],
        grad_out_weight,
        grad_out_bias[0],
        grad_norm2_gain[0],
        grad_norm2_bias[0],
        grad_up_weight,
        grad_up_bias[0],
        grad_down_weight,
        grad_down_bias[0],
    )


def solution(mesh):
    return jax.shard_map(
        body,
        mesh=mesh,
        in_specs=(
            P("dp", "tensor", None),
            P("dp", None),
            P(),
            P(),
            P(None, None, "tensor"),
            P(None, "tensor"),
            P(None, None, "tensor"),
            P(None, "tensor"),
            P(),
            P(),
            P(),
            P(),
            P(),
            P(None, "tensor"),
            P("tensor"),
            P("tensor"),
            P("tensor", None),
            P(),
            P(),
            P(),
            P(None, "tensor"),
            P("tensor"),
            P("tensor", None),
            P(),
            P("dp", "tensor", None),
        ),
        out_specs=(
            P("dp", "tensor", None),
            P("dp", "tensor", None),
            P(),
            P(),
            P(None, None, "tensor"),
            P(None, "tensor"),
            P(None, None, "tensor"),
            P(None, "tensor"),
            P(),
            P(),
            P(),
            P(),
            P(),
            P(None, "tensor"),
            P("tensor"),
            P("tensor", None),
            P(),
            P(),
            P(),
            P(None, "tensor"),
            P("tensor"),
            P("tensor", None),
            P(),
        ),
        check_vma=False,
    )
```

```python
import functools
import math

import jax
import jax.numpy as jnp
import ml_dtypes
import numpy as np
from jax import lax
from jax.experimental import pallas as pl
from jax.experimental.pallas import tpu as pltpu
from jax.sharding import PartitionSpec as P

FEAT = 33
SEQ = 1024
NDOC = 8
SLOTS = NDOC - 1


EPS = 1e-05
HIGH = lax.Precision.HIGHEST
SHIFT = 0.1
GELU_RATE = math.sqrt(2.0 / math.pi)
GELU_CUBE = 0.044715


def dot_nn(left, right):
    return jnp.dot(left, right, preferred_element_type=jnp.float32)


def dot_nt(left, right):
    return lax.dot_general(
        left, right, (((1,), (1,)), ((), ())), preferred_element_type=jnp.float32
    )


def dot_tn(left, right):
    return lax.dot_general(
        left, right, (((0,), (0,)), ((), ())), preferred_element_type=jnp.float32
    )


def transform(length):
    places = np.arange(length)
    angles = ((places[:, None] * places[None, :]) % (2 * length)) * (np.pi / length)
    return (
        jnp.asarray(np.cos(angles).astype(ml_dtypes.bfloat16)),
        jnp.asarray((-np.sin(angles)).astype(ml_dtypes.bfloat16)),
    )


def features_by_row():
    places = np.arange(SEQ, dtype=np.float32)
    bands = np.arange(1, (FEAT - 1) // 2 + 1, dtype=np.float32)
    angles = 2.0 * np.pi * np.arange(SEQ)[None, :] * bands[:, None].astype(np.float64) / SEQ
    rows = np.concatenate([(places / (SEQ - 1))[None, :], np.cos(angles), np.sin(angles)], axis=0)
    return jnp.asarray(rows.astype(np.float32))


def exact(left, right, contract):
    return lax.dot_general(
        left, right, (contract, ((), ())), precision=HIGH, preferred_element_type=jnp.float32
    )


def bin_scale(length):
    bins = lax.broadcasted_iota(jnp.int32, (length, 1), 0)
    return jnp.where(bins == 0, 0.5 / length, 1.0 / length)


def signs(length):
    places = lax.broadcasted_iota(jnp.int32, (length, 1), 0)
    return (1 - 2 * lax.rem(places, 2)).astype(jnp.float32)


def modulation(length, decay):
    places = lax.broadcasted_iota(jnp.int32, (length, 1), 0).astype(jnp.float32)
    return jnp.exp(-decay * (places / SEQ)) + SHIFT


def make_taps(
    features, embed, inner, columns, biases, filter_weight, decay, transforms, pre, taps_bins
):
    cos_main, sin_main, cos_small, sin_small = transforms
    main_re, main_im, main_top, small_re, small_im, small_top = taps_bins
    length = features.shape[1]
    region = cos_small.shape[0]
    hidden = None
    for i in range(3):
        if i == 0:
            value = exact(embed[...], features[...], ((0,), (0,)))
        else:
            value = exact(inner[i - 1], hidden, ((0,), (0,)))
        value = value + biases[i]
        pre[i] = value
        hidden = jnp.sin(columns[i] * value)
    taps = exact(hidden, filter_weight[...], ((0,), (0,)))
    taps = (taps * modulation(length, decay[...])).astype(jnp.bfloat16)
    scale = bin_scale(length)
    main_re[...] = dot_nn(cos_main[...], taps) * scale
    main_im[...] = dot_nn(sin_main[...], taps) * scale
    top = jnp.sum(taps.astype(jnp.float32) * signs(length), axis=0, keepdims=True)
    main_top[...] = top * (0.5 / length)
    short = taps[:region]
    scale = bin_scale(region)
    small_re[...] = dot_nn(cos_small[...], short) * scale
    small_im[...] = dot_nn(sin_small[...], short) * scale
    top = jnp.sum(short.astype(jnp.float32) * signs(region), axis=0, keepdims=True)
    small_top[...] = top * (0.5 / region)


def spectra(values, marks, cos_main, sin_main, cos_small, sin_small):
    length = values.shape[0]
    region = cos_small.shape[0]
    main = jnp.where(marks[:, 0:1] > 0, values, 0.0)
    top = jnp.sum(main * signs(length), axis=0, keepdims=True)
    main = main.astype(jnp.bfloat16)
    main_bins = (dot_nn(cos_main[...], main), dot_nn(sin_main[...], main), top)
    head, tail = values[:region], values[length - region :]
    head_slot, tail_slot = marks[:region, 3:4], marks[length - region :, 4:5]
    pieces = [
        jnp.where(head_slot == d, head, 0.0) + jnp.where(tail_slot == d, tail, 0.0)
        for d in range(SLOTS)
    ]
    small = jnp.concatenate(pieces, axis=1)
    top = jnp.sum(small * signs(region), axis=0, keepdims=True)
    small = small.astype(jnp.bfloat16)
    small_bins = (dot_nn(cos_small[...], small), dot_nn(sin_small[...], small), top)
    return main_bins, small_bins


def times(left, right, conjugate):
    left_re, left_im, left_top = left
    right_re, right_im, right_top = right
    if conjugate:
        return (
            left_re * right_re + left_im * right_im,
            left_re * right_im - left_im * right_re,
            left_top * right_top,
        )
    return (
        left_re * right_re - left_im * right_im,
        left_re * right_im + left_im * right_re,
        left_top * right_top,
    )


def from_bins(bins, cos_rows, sin_rows):
    real, imag, top = bins
    return (
        dot_nn(cos_rows[...], real.astype(jnp.bfloat16))
        + dot_nn(sin_rows[...], imag.astype(jnp.bfloat16))
        + signs(real.shape[0]) * top
    )


def beside(part):
    return jnp.concatenate([part] * SLOTS, axis=1)


def filtered(main_bins, small_bins, taps_main, taps_small, marks, transforms, conjugate):
    cos_main, sin_main, cos_small, sin_small = transforms
    main = from_bins(times(taps_main, main_bins, conjugate), cos_main, sin_main)
    taps_wide = tuple(beside(part) for part in taps_small)
    small = from_bins(times(taps_wide, small_bins, conjugate), cos_small, sin_small)
    length, channels = main.shape
    region = small.shape[0]
    main = jnp.where(marks[:, 0:1] > 0, main, 0.0)
    head, tail = main[:region], main[length - region :]
    head_slot, tail_slot = marks[:region, 3:4], marks[length - region :, 4:5]
    for d in range(SLOTS):
        piece = small[:, d * channels : (d + 1) * channels]
        head = head + jnp.where(head_slot == d, piece, 0.0)
        tail = tail + jnp.where(tail_slot == d, piece, 0.0)
    return jnp.concatenate([head, main[region : length - region], tail], axis=0)


def filter_back(
    grad_taps,
    features,
    embed,
    rates,
    inner,
    filter_weight,
    decay,
    pre,
    filter_sums,
    channel_sums,
):
    length = features.shape[1]
    width = filter_weight.shape[0]
    rows = filter_rows(width)
    ones = jnp.ones((8, length), jnp.float32)
    raw = grad_taps[...] * modulation(length, decay[...])
    back = exact(filter_weight[...], raw, ((1,), (1,)))
    for i in (2, 1, 0):
        angle = rates[i] * pre[i]
        if i == 2:
            channel_sums[:width] = exact(jnp.sin(angle), raw, ((1,), (0,)))
        act = back * jnp.cos(angle)
        filter_sums[rows.freq + i : rows.freq + i + 1, :width] = exact(ones, act * pre[i], ((1,), (1,)))[0:1]
        step = act * rates[i]
        bias = exact(ones, step, ((1,), (1,)))[0:1]
        if i == 0:
            filter_sums[rows.embed_bias : rows.embed_bias + 1, :width] = bias
            filter_sums[rows.embed : rows.embed + FEAT, :width] = exact(
                features[...], step, ((1,), (1,))
            )
        else:
            filter_sums[rows.inner_bias + i - 1 : rows.inner_bias + i, :width] = bias
            below = jnp.sin(rates[i - 1] * pre[i - 1])
            filter_sums[:width, (i - 1) * width : i * width] = exact(below, step, ((1,), (1,)))
            back = exact(inner[i - 1], step, ((1,), (0,)))


def shaped(shape, dtype=jnp.float32):
    return jax.ShapeDtypeStruct(shape, dtype)


def row_marks(segment, marks, region):
    ids = to_column(segment[...].astype(jnp.float32)).astype(jnp.int32)
    length = ids.shape[0]
    places = lax.broadcasted_iota(jnp.int32, ids.shape, 0)
    inside = ids == ids[region - 1 : region]
    marks[:, 0:1] = inside.astype(jnp.int32)
    for lag in (1, 2):
        same = (ids == pltpu.roll(ids, lag, 0)) & (places >= lag)
        marks[:, lag : lag + 1] = same.astype(jnp.int32)
    marks[:, 3:4] = jnp.where(inside | (places >= region), -1, ids)
    marks[:, 4:5] = jnp.where(inside | (places < length - region), -1, ids - 1)


BY_INDEX = pl.DeviceIdType.MESH


def greet(devices):
    barrier = pltpu.get_barrier_semaphore()
    for device in devices:
        pl.semaphore_signal(barrier, inc=1, device_id=device, device_id_type=BY_INDEX)
    pl.semaphore_wait(barrier, len(devices))


def remote(source, target, send_sem, recv_sem, device):
    return pltpu.make_async_remote_copy(
        src_ref=source,
        dst_ref=target,
        send_sem=send_sem,
        recv_sem=recv_sem,
        device_id=device,
        device_id_type=BY_INDEX,
    )


def tensor_peers():
    count = lax.axis_size("tensor")
    me = lax.axis_index("tensor")
    return [lax.rem(me + k, count) for k in range(1, count)]


def tensor_devices():
    return [{"tensor": peer} for peer in tensor_peers()]


def sibling():
    me = lax.axis_index("dp")
    return {"dp": me + 1 - 2 * lax.rem(me, 2)}


def chip_peers():
    chips = lax.axis_size("dp") // 2
    me = lax.axis_index("dp")
    core = lax.rem(me, 2)
    result = []
    for k in range(1, chips):
        chip = lax.rem(me // 2 + k, chips)
        result.append((chip, 2 * chip + core))
    return result


def chip_devices():
    return [{"dp": mate} for unused_chip, mate in chip_peers()]


def spread(source, target, sems, devices):
    copies = []
    for k, device in enumerate(devices):
        copies.append(
            remote(
                source(k) if callable(source) else source,
                target(k) if callable(target) else target,
                sems.at[0, k],
                sems.at[1, k],
                device,
            )
        )
        copies[-1].start()
    return copies


def wait_all(copies):
    for copy in copies:
        copy.wait()


def span(index, size):
    return pl.ds(pl.multiple_of(index * size, 16), size)


def staged(pairs, sems):
    copies = []
    for i, (source, target) in enumerate(pairs):
        copies.append(pltpu.make_async_copy(source, target, sems.at[i]))
        copies[-1].start()
    return copies


def to_column(row):
    size = row.shape[1]
    piece = min(size, 128)
    shape = (piece, piece)
    same = lax.broadcasted_iota(jnp.int32, shape, 0) == lax.broadcasted_iota(jnp.int32, shape, 1)
    pieces = [
        jnp.sum(jnp.where(same, row[:, i : i + piece], 0.0), axis=1, keepdims=True)
        for i in range(0, size, piece)
    ]
    return jnp.concatenate(pieces, axis=0)


class Chain:
    def __init__(self, slots, send_sems, recv_sems):
        self.slots, self.send_sems, self.recv_sems = slots, send_sems, recv_sems
        self.count = lax.axis_size("tensor")
        self.me = lax.axis_index("tensor")
        self.rows = slots.shape[1] // 2

    def copy(self, block, half, side):
        step = 1 - 2 * side
        piece = self.slots.at[block, pl.ds(half * self.rows, self.rows)]
        return remote(
            piece,
            piece,
            self.send_sems.at[side, half, block],
            self.recv_sems.at[half, block],
            {"tensor": lax.rem(self.me + step + self.count, self.count)},
        )

    def pass_on(self, step, half, side):
        block = self.me - step * (1 - 2 * side)

        @pl.when((block >= 0) & (block < self.count))
        def _():
            @pl.when(step > 0)
            def _():
                self.copy(block, half, side).wait_recv()

            @pl.when((self.me < self.count - 1) if side == 0 else (self.me > 0))
            def _():
                self.copy(block, half, side).start()

    def advance(self, step):
        for half in range(2):
            for side in range(2):
                self.pass_on(step, half, side)

    def finish(self):
        for block in range(self.count):
            for half in range(2):

                @pl.when((self.me < self.count - 1) & (block <= self.me))
                def _():
                    self.copy(block, half, 0).wait_send()

                @pl.when((self.me > 0) & (block >= self.me))
                def _():
                    self.copy(block, half, 1).wait_send()


def chain_scratch(count):
    return [pltpu.SemaphoreType.DMA((2, 2, count)), pltpu.SemaphoreType.DMA((2, count))]


def normalised(values):
    average = jnp.mean(values, axis=-1, keepdims=True)
    centered = values - average
    variance = jnp.mean(centered * centered, axis=-1, keepdims=True)
    rate = lax.rsqrt(variance + EPS)
    return centered * rate, rate


def norm_back(grad, gain, hat, rate):
    e = grad * gain
    return rate * (
        e
        - jnp.mean(e, axis=-1, keepdims=True)
        - hat * jnp.mean(e * hat, axis=-1, keepdims=True)
    )


def column_sum(values):
    return jnp.sum(values, axis=0, keepdims=True)


def front_kernel(
    tokens,
    gain,
    shift,
    part,
    cotangent,
    segment,
    embed,
    embed_bias,
    freq,
    inner,
    inner_bias,
    filter_weight,
    decay,
    proj_bias,
    short,
    short_bias,
    skip,
    features_hbm,
    proj_hbm,
    cos_main_hbm,
    sin_main_hbm,
    cos_small,
    sin_small,
    out_bias,
    second_gain,
    second_shift,
    first_out,
    part_all,
    cotangent_out,
    pre_out,
    main_re_out,
    main_im_out,
    main_top,
    small_re,
    small_im,
    small_top,
    gated_own,
    projected_out,
    mixed_out,
    summed_out,
    out,
    residual,
    second,
    features,
    proj,
    cos_main,
    sin_main,
    first_all,
    cotangent_all,
    pre,
    main_re,
    main_im,
    projected,
    mixed,
    summed,
    gated,
    held_parts,
    marks,
    load_sems,
    store_sems,
    local_sems,
    first_send,
    first_recv,
    cotangent_send,
    cotangent_recv,
    part_sems,
    chip_sems,
    core_sems,
    gated_sems,
):
    me = lax.axis_index("tensor")
    count = lax.axis_size("tensor")
    place = lax.axis_index("dp")
    core = lax.rem(place, 2)
    chip = place // 2
    peers = tensor_peers()
    shard = tokens.shape[0]
    channels = skip.shape[1]
    taps_bins = (main_re, main_im, main_top, small_re, small_im, small_top)
    transforms = (cos_main, sin_main, cos_small, sin_small)
    loads = staged(
        [
            (proj_hbm, proj),
            (features_hbm, features),
            (cos_main_hbm, cos_main),
            (sin_main_hbm, sin_main),
        ],
        load_sems,
    )
    greet(tensor_devices() + [sibling()] + chip_devices())

    cotangent_all[me] = cotangent[...]
    later = Chain(cotangent_all, cotangent_send, cotangent_recv)
    hat, unused_rate = normalised(tokens[...].astype(jnp.float32))
    first_all[me] = (hat * gain[...] + shift[...]).astype(jnp.bfloat16)
    chain = Chain(first_all, first_send, first_recv)
    chain.advance(0)
    own = pltpu.make_async_copy(part, part_all.at[me, chip, core], local_sems.at[0])
    own.start()
    parts = spread(part, part_all.at[me, chip, core], part_sems, tensor_devices())

    def project(block):
        rows = pl.ds(pl.multiple_of(block * shard, shard), shard)
        for k in range(3):
            lanes = slice(k * channels, (k + 1) * channels)
            projected[rows, lanes] = dot_nn(first_all[block], proj[k]) + proj_bias[k : k + 1]

    wait_all(loads)
    project(me)
    columns = [to_column(freq[i : i + 1]) for i in range(3)]
    biases = [to_column(embed_bias[...])] + [to_column(inner_bias[i : i + 1]) for i in range(2)]
    make_taps(
        features, embed, inner, columns, biases, filter_weight, decay, transforms, pre, taps_bins
    )
    stores = [(pre, pre_out), (main_re, main_re_out), (main_im, main_im_out)]
    stored = staged(stores, store_sems)

    def turn(step, carry):
        chain.advance(step)

        def side(index, carry):
            block = me + step * (2 * index - 1)

            @pl.when((block >= 0) & (block < count))
            def _():
                project(block)

            return carry

        return lax.fori_loop(0, 2, side, carry)

    lax.fori_loop(1, 2, turn, 0)
    own.wait()
    wait_all(parts)
    held = part_all.at[:, chip, core]
    parts = spread(held, held, chip_sems, chip_devices())
    lax.fori_loop(2, count, turn, 0)
    later.advance(0)
    row_marks(segment, marks, cos_small.shape[0])
    more = store_sems.at[pl.ds(len(stores), 5)]
    stored += staged([(first_all, first_out), (projected, projected_out)], more)
    wait_all(parts)
    held = part_all.at[:, :, core]
    parts = spread(held, held, core_sems, [sibling()])

    for k in range(3):
        lanes = slice(k * channels, (k + 1) * channels)
        value = projected[:, lanes]
        running = short_bias[k : k + 1] + short[0, k : k + 1] * value
        for lag in (1, 2):
            moved = jnp.where(marks[:, lag : lag + 1] > 0, pltpu.roll(value, lag, 0), 0.0)
            running = running + short[lag, k : k + 1] * moved
        mixed[:, lanes] = running
    product = mixed[:, 2 * channels :] * mixed[:, channels : 2 * channels]
    more = store_sems.at[pl.ds(len(stores) + 2, 3)]
    stored += staged([(mixed, mixed_out)], more)
    low = product.astype(jnp.bfloat16).astype(jnp.float32)
    main_bins, small_bins = spectra(low, marks, *transforms)
    later.advance(1)
    result = filtered(
        main_bins,
        small_bins,
        (main_re[...], main_im[...], main_top[...]),
        (small_re[...], small_im[...], small_top[...]),
        marks,
        transforms,
        False,
    )
    total = result + skip[...] * product
    summed[...] = total
    gated[...] = (total * mixed[:, :channels]).astype(jnp.bfloat16).reshape(gated.shape)
    swapped = spread(
        lambda k: gated.at[peers[k]], gated_own.at[me], gated_sems, tensor_devices()
    )
    later.advance(2)
    more = store_sems.at[pl.ds(len(stores) + 3, 2)]
    stored += staged([(summed, summed_out)], more)
    gated_own[me] = gated[me]
    wait_all(parts)
    load = pltpu.make_async_copy(part_all, held_parts, local_sems.at[0])
    load.start()
    load.wait()
    wait_all(swapped)
    size = channels // (held_parts.shape[1] * 2)
    base = tokens[...].astype(jnp.float32) + out_bias[...]
    for block in range(count):
        if held_parts.shape[3] == size:
            out[block] = held_parts[block].reshape(out.shape[1:])
        else:
            wide = held_parts[block].astype(jnp.float32)[:, :, :size]
            out[block] = wide.reshape(out.shape[1:]).astype(out.dtype)
        base = base + dot_nn(gated_own[block], out[block])
    residual[...] = base
    hat, unused_rate = normalised(base)
    second[...] = (hat * second_gain[...] + second_shift[...]).astype(jnp.bfloat16)
    for step in range(3, count):
        later.advance(step)
    more = store_sems.at[pl.ds(len(stores) + 4, 1)]
    stored += staged([(cotangent_all, cotangent_out)], more)
    chain.finish()
    later.finish()
    wait_all(stored)


def middle_kernel(
    second_own,
    gain,
    bias,
    cotangent_hbm,
    up_hbm,
    down_hbm,
    residual_hbm,
    gated_hbm,
    out_hbm,
    grad_residual,
    mlp_out,
    up_out,
    down_out,
    bias_grad,
    grad_gated,
    out_grad,
    gain_sum,
    shift_sum,
    out_sum,
    down_sum,
    cotangent,
    up,
    down,
    residual,
    gated,
    out,
    mlp,
    up_grad,
    down_grad,
    second,
    active,
    low,
    parting,
    arriving,
    own_part,
    load_sems,
    store_sems,
    second_send,
    second_recv,
    part_send,
    part_recv,
):
    me = lax.axis_index("tensor")
    count = lax.axis_size("tensor")
    shard, width = second_own.shape
    units = up.shape[1]
    loads = staged(
        [
            (up_hbm, up),
            (down_hbm, down),
            (cotangent_hbm, cotangent),
            (residual_hbm, residual),
            (gated_hbm, gated),
            (out_hbm, out),
        ],
        load_sems,
    )
    greet(tensor_devices())
    second[me] = second_own[...]
    chain = Chain(second, second_send, second_recv)
    bias_grad[...] = jnp.zeros_like(bias_grad)

    def sent(block):
        return remote(
            parting.at[block],
            arriving.at[me],
            part_send.at[block],
            part_recv.at[me],
            {"tensor": block},
        )

    def work(block):
        cut = units // 2
        for lanes in (slice(0, cut), slice(cut, units)):
            hidden = dot_nn(second[block], up[:, lanes]) + bias[:, lanes]
            cube = GELU_CUBE * hidden * hidden
            slope = jnp.tanh(GELU_RATE * hidden * (1.0 + cube))
            gate = 0.5 * (1.0 + slope)
            active[block, :, lanes] = (hidden * gate).astype(jnp.bfloat16)
            rate = gate + (0.5 * GELU_RATE) * hidden * (1.0 - slope * slope) * (1.0 + 3.0 * cube)
            grad_hidden = dot_nt(cotangent[block], down[lanes]) * rate
            bias_grad[:, lanes] += column_sum(grad_hidden)
            low[block, :, lanes] = grad_hidden.astype(jnp.bfloat16)
        part = dot_nt(low[block], up[...])

        @pl.when(block == me)
        def _():
            own_part[...] = part

        @pl.when(block != me)
        def _():
            parting[block] = part.astype(jnp.bfloat16)
            sent(block).start()

        mlp[block] = dot_nn(active[block], down[...]).astype(jnp.bfloat16)

    def turn(step, carry):
        chain.advance(step)

        @pl.when(step == 0)
        def _():
            wait_all(loads[:3])

        def side(index, carry):
            block = me + step * (2 * index - 1)

            @pl.when((block >= 0) & (block < count) & ((step > 0) | (index == 0)))
            def _():
                work(block)

            return carry

        return lax.fori_loop(0, 2, side, carry)

    lax.fori_loop(0, count, turn, 0)
    stored = staged([(mlp, mlp_out)], store_sems)
    tokens_all = count * shard
    up_grad[...] = dot_tn(
        second[...].reshape(tokens_all, width), low[...].reshape(tokens_all, units)
    ).astype(jnp.bfloat16)
    down_grad[...] = dot_tn(
        active[...].reshape(tokens_all, units), cotangent[...].reshape(tokens_all, width)
    ).astype(jnp.bfloat16)
    stored += staged([(up_grad, up_out), (down_grad, down_out)], store_sems.at[pl.ds(1, 2)])
    wait_all(loads[3:])
    for peer in tensor_peers():
        remote(
            parting.at[peer],
            arriving.at[peer],
            part_send.at[peer],
            part_recv.at[peer],
            {"tensor": peer},
        ).wait_recv()
        own_part[...] += arriving[peer].astype(jnp.float32)
    grad_normed = own_part[...]
    hat, rate = normalised(residual[...])
    grad_out = cotangent[me].astype(jnp.float32)
    grad = grad_out + norm_back(grad_normed, gain[...], hat, rate)
    grad_residual[...] = grad
    gain_sum[...] = column_sum(grad_normed * hat)
    shift_sum[...] = column_sum(grad_normed)
    out_sum[...] = column_sum(grad)
    down_sum[...] = column_sum(grad_out)
    grad_low = grad.astype(jnp.bfloat16)
    for block in range(count):
        grad_gated[block] = dot_nt(grad_low, out[block]).astype(jnp.bfloat16)
        out_grad[block] = dot_tn(gated[block], grad_low).astype(jnp.bfloat16)
    chain.finish()
    for peer in tensor_peers():
        sent(peer).wait_send()
    wait_all(stored)


class RowReduce:
    def __init__(self, source, part, refs):
        half, core_recv, chip_recv, load_sem, core_sems, chip_sems = refs[:6]
        self.source, self.part, self.half = source, part, half
        self.core_recv, self.chip_recv = core_recv, chip_recv
        self.load_sem, self.core_sems, self.chip_sems = load_sem, core_sems, chip_sems
        self.across = tuple(refs[6:])
        place = lax.axis_index("dp")
        self.core, self.chip = lax.rem(place, 2), place // 2
        self.chips = lax.axis_size("dp") // 2
        self.rows = half.shape[-2]
        self.size = self.rows // self.chips

    def pair(self):
        self.load = pltpu.make_async_copy(
            self.source.at[..., span(self.core, self.rows), :], self.half, self.load_sem.at[0]
        )
        self.load.start()
        self.copies = spread(
            self.source.at[..., span(1 - self.core, self.rows), :],
            self.core_recv,
            self.core_sems,
            [sibling()],
        )

    def plane(self):
        self.load.wait()
        wait_all(self.copies)
        self.half[...] = (
            self.half[...].astype(jnp.float32) + self.core_recv[...].astype(jnp.float32)
        ).astype(self.half.dtype)
        mates = chip_peers()
        self.copies = spread(
            lambda k: self.half.at[..., span(mates[k][0], self.size), :],
            lambda k: self.chip_recv.at[k],
            self.chip_sems,
            chip_devices(),
        )

    def gathered(self):
        value = self.half[..., span(self.chip, self.size), :].astype(jnp.float32)
        for k, copy in enumerate(self.copies):
            copy.wait()
            value = value + self.chip_recv[k].astype(jnp.float32)
        return value

    def cross(self):
        held, held_recv, sems = self.across
        held[...] = self.gathered().astype(held.dtype)
        peers = tensor_peers()
        self.copies = spread(
            lambda k: held.at[peers[k]], lambda k: held_recv.at[k], sems, tensor_devices()
        )

    def crossed(self):
        held, held_recv, sems = self.across
        value = held[lax.axis_index("tensor")].astype(jnp.float32)
        for k, copy in enumerate(self.copies):
            copy.wait()
            value = value + held_recv[k].astype(jnp.float32)
        return value

    def finish(self):
        value = self.crossed() if self.across else self.gathered()
        self.part[...] = value.astype(self.part.dtype)


def row_reduce_scratch(shape, chips):
    rows, columns = shape[-2:]
    lead = tuple(shape[:-2])
    size = rows // 2 // chips
    low = jnp.bfloat16
    scratch = [
        pltpu.VMEM(lead + (rows // 2, columns), low),
        pltpu.VMEM(lead + (rows // 2, columns), low),
        pltpu.VMEM((chips - 1,) + lead + (size, columns), low),
        pltpu.SemaphoreType.DMA((1,)),
        pltpu.SemaphoreType.DMA((2, 1)),
        pltpu.SemaphoreType.DMA((2, chips - 1)),
    ]
    if lead:
        scratch += [
            pltpu.VMEM(lead + (size, columns), low),
            pltpu.VMEM((lead[0] - 1, size, columns), low),
            pltpu.SemaphoreType.DMA((2, lead[0] - 1)),
        ]
    return scratch


class RowGather:
    def __init__(self, part, total, refs):
        self.part, self.total = part, total
        self.own_sem, self.chip_sems, self.core_sems = refs
        place = lax.axis_index("dp")
        core, chip = lax.rem(place, 2), place // 2
        chips = lax.axis_size("dp") // 2
        self.mine = span(core * chips + chip, part.shape[0])
        self.half = span(core, part.shape[0] * chips)

    def plane(self):
        own = self.total.at[self.mine]
        self.copies = staged([(self.part, own)], self.own_sem)
        self.copies += spread(self.part, own, self.chip_sems, chip_devices())

    def pair(self):
        wait_all(self.copies)
        own = self.total.at[self.half]
        self.copies = spread(own, own, self.core_sems, [sibling()])

    def finish(self):
        wait_all(self.copies)


def row_gather_scratch(chips):
    return [
        pltpu.SemaphoreType.DMA((1,)),
        pltpu.SemaphoreType.DMA((2, chips - 1)),
        pltpu.SemaphoreType.DMA((2, 1)),
    ]


class Scatter:
    def __init__(self, blocks, refs):
        self.blocks = blocks
        self.relayed, self.arrived = refs[:2]
        self.send_sems, self.recv_sems, self.relay_sems = refs[2:]
        self.me = lax.axis_index("tensor")
        self.count = lax.axis_size("tensor")

    def far(self, block):
        distance = jnp.abs(block - self.me)
        return (distance > 2) & (lax.rem(distance, 2) == 1)

    def joined(self, block):
        distance = jnp.abs(block - self.me)
        outer = self.me + jnp.where(block > self.me, -1, 1)
        inside = (outer >= 0) & (outer < self.count)
        return (distance > 1) & (lax.rem(distance, 2) == 0) & inside

    def plain(self, block):
        return jnp.logical_not(self.far(block) | self.joined(block))

    def by_neighbour(self, block):
        step = jnp.where(block > self.me, 1, -1)
        return remote(
            self.blocks.at[block],
            self.relayed.at[lax.div(block, 2)],
            self.send_sems.at[block],
            self.relay_sems.at[block],
            {"tensor": lax.rem(self.me + step + self.count, self.count)},
        )

    def direct(self, block, source):
        return remote(
            source,
            self.arrived.at[lax.rem(self.me - block + self.count, self.count) - 1],
            self.send_sems.at[block],
            self.recv_sems.at[self.me],
            {"tensor": block},
        )

    def start(self):
        any_far = (self.me >= 3) | (self.me + 3 < self.count)
        for peer in tensor_peers():

            @pl.when(self.far(peer))
            def _():
                self.by_neighbour(peer).start()

        for peer in tensor_peers():

            @pl.when(self.plain(peer) & jnp.logical_not(any_far))
            def _():
                self.direct(peer, self.blocks.at[peer]).start()

    def follow(self):
        any_far = (self.me >= 3) | (self.me + 3 < self.count)
        for peer in tensor_peers():

            @pl.when(self.far(peer))
            def _():
                self.by_neighbour(peer).wait_send()

        for peer in tensor_peers():

            @pl.when(self.plain(peer) & any_far)
            def _():
                self.direct(peer, self.blocks.at[peer]).start()

        for peer in tensor_peers():

            @pl.when(self.joined(peer))
            def _():
                self.by_neighbour(peer).wait_recv()
                held = self.relayed.at[lax.div(peer, 2)]
                held[...] = (
                    self.blocks[peer].astype(jnp.float32) + held[...].astype(jnp.float32)
                ).astype(held.dtype)
                self.direct(peer, held).start()

    def finish(self, total):
        total[...] = self.blocks[self.me].astype(jnp.float32)
        for k, peer in enumerate(tensor_peers()):

            @pl.when(self.joined(peer))
            def _():
                self.direct(peer, self.relayed.at[lax.div(peer, 2)]).wait_send()

            @pl.when(self.plain(peer))
            def _():
                self.direct(peer, self.blocks.at[peer]).wait_send()

            @pl.when(jnp.logical_not(self.far(peer)))
            def _():
                remote(
                    self.blocks.at[peer],
                    self.arrived.at[k],
                    self.send_sems.at[peer],
                    self.recv_sems.at[peer],
                    {"tensor": peer},
                ).wait_recv()
                total[...] += self.arrived[k].astype(jnp.float32)


def scatter_scratch(shape):
    half = (shape[0] // 2,) + tuple(shape[1:])
    rest = (shape[0] - 1,) + tuple(shape[1:])
    return [pltpu.VMEM(half, jnp.bfloat16), pltpu.VMEM(rest, jnp.bfloat16)] + [pltpu.SemaphoreType.DMA((shape[0],))] * 3


class SmallSums:
    def __init__(self, sources, results, wide, refs):
        self.sources, self.results, self.wide = sources, results, wide
        count = len(sources)
        self.core_recv = refs[:count]
        self.chip_slots = refs[count : 2 * count]
        self.group_slots = refs[2 * count : 2 * count + wide]
        self.core_sems, self.chip_sems, self.group_sems = refs[2 * count + wide :]
        self.me = lax.axis_index("tensor")
        self.chip = lax.axis_index("dp") // 2

    def pair(self):
        self.copies = []
        for i, source in enumerate(self.sources):
            self.copies += spread(source, self.core_recv[i], self.core_sems.at[i], [sibling()])

    def plane(self):
        wait_all(self.copies)
        self.copies = []
        for i, source in enumerate(self.sources):
            self.chip_slots[i][self.chip] = source[...] + self.core_recv[i][...]
            own = self.chip_slots[i].at[self.chip]
            self.copies += spread(own, own, self.chip_sems.at[i], chip_devices())

    def total(self, slots):
        value = slots[0]
        for i in range(1, slots.shape[0]):
            value = value + slots[i]
        return value

    def tensor(self):
        wait_all(self.copies)
        self.copies = []
        for i in range(len(self.sources)):
            if i >= self.wide:
                self.results[i][...] = self.total(self.chip_slots[i])
                continue
            self.group_slots[i][self.me] = self.total(self.chip_slots[i])
            own = self.group_slots[i].at[self.me]
            self.copies += spread(own, own, self.group_sems.at[i], tensor_devices())

    def finish(self):
        wait_all(self.copies)
        for i in range(self.wide):
            self.results[i][...] = self.total(self.group_slots[i])


def small_sums_scratch(shapes, wide, chips, groups):
    return (
        [pltpu.VMEM(shape, jnp.float32) for shape in shapes]
        + [pltpu.VMEM((chips,) + tuple(shape), jnp.float32) for shape in shapes]
        + [pltpu.VMEM((groups,) + tuple(shape), jnp.float32) for shape in shapes[:wide]]
        + [
            pltpu.SemaphoreType.DMA((len(shapes), 2, 1)),
            pltpu.SemaphoreType.DMA((len(shapes), 2, chips - 1)),
            pltpu.SemaphoreType.DMA((max(wide, 1), 2, groups - 1)),
        ]
    )


class channel_rows:
    def __init__(self, width):
        self.filter = 0
        self.short = width
        self.short_bias = width + 9
        self.proj_bias = width + 12
        self.skip = width + 15
        self.size = width + 16


class filter_rows:
    def __init__(self, width):
        self.embed = width
        self.embed_bias = self.embed + FEAT + -FEAT % 8
        self.freq = self.embed_bias + 1
        self.inner_bias = self.embed_bias + 4
        self.size = self.embed_bias + 8


def back_kernel(
    grad_blocks,
    mlp_hbm,
    up_grad,
    down_grad,
    out_grad,
    short,
    skip,
    segment,
    embed,
    freq,
    inner,
    filter_weight,
    decay,
    main_top,
    small_re,
    small_im,
    small_top,
    cos_small,
    sin_small,
    mixed_hbm,
    cos_main_hbm,
    sin_main_hbm,
    main_re_hbm,
    main_im_hbm,
    summed_hbm,
    projected_hbm,
    proj_hbm,
    features_hbm,
    pre_hbm,
    grad_first,
    grad_low,
    mlp_sum,
    up_sum,
    down_part,
    out_part,
    filter_sums,
    channel_sums,
    mixed,
    cos_main,
    sin_main,
    main_re,
    main_im,
    summed,
    projected,
    proj,
    features,
    pre,
    grad_gated,
    grad_taps,
    marks,
    mlp,
    up_part,
    load_sems,
    local_sems,
    gated_sems,
    *scratch,
):
    me = lax.axis_index("tensor")
    count = lax.axis_size("tensor")
    peers = tensor_peers()
    channels = skip.shape[1]
    length = projected.shape[0]
    region = cos_small.shape[0]
    shard = length // count
    transforms = (cos_main, sin_main, cos_small, sin_small)
    loads = staged(
        [
            (mixed_hbm, mixed),
            (cos_main_hbm, cos_main),
            (sin_main_hbm, sin_main),
            (main_re_hbm, main_re),
            (main_im_hbm, main_im),
            (summed_hbm, summed),
            (projected_hbm, projected),
            (proj_hbm, proj),
            (features_hbm, features),
            (pre_hbm, pre),
        ],
        load_sems,
    )
    greet(tensor_devices() + [sibling()] + chip_devices())
    up_row = RowReduce(up_grad, up_part, scratch[:6])
    down_row = RowReduce(down_grad, down_part, scratch[6:12])
    out_row = RowReduce(out_grad, out_part, scratch[12:21])
    weights = (up_row, down_row, out_row)
    up_all = RowGather(up_part, up_sum, scratch[21:24])
    scatter = Scatter(mlp, scratch[24:])
    places = channel_rows(filter_weight.shape[0])
    filter_sums[...] = jnp.zeros_like(filter_sums)
    own = pltpu.make_async_copy(grad_blocks.at[me], grad_gated.at[me], local_sems.at[0])
    own.start()
    arriving = spread(
        lambda k: grad_blocks.at[peers[k]], grad_gated.at[me], gated_sems, tensor_devices()
    )
    for weight in weights:
        weight.pair()
    mlp_load = pltpu.make_async_copy(mlp_hbm, mlp, local_sems.at[1])
    mlp_load.start()
    row_marks(segment, marks, region)
    wait_all(loads[:3])
    gate_out = mixed[:, :channels]
    gate_in = mixed[:, channels : 2 * channels]
    values = mixed[:, 2 * channels :]
    product = values * gate_in
    low = product.astype(jnp.bfloat16).astype(jnp.float32)
    value_main, value_small = spectra(low, marks, *transforms)
    up_row.plane()
    out_row.plane()
    own.wait()
    wait_all(arriving)
    mlp_load.wait()
    scatter.start()
    grad = grad_gated[...].reshape(length, channels).astype(jnp.float32)
    grad_summed = grad * gate_out
    channel_sums[places.skip : places.skip + 1] = column_sum(grad_summed * product)
    low = grad_summed.astype(jnp.bfloat16).astype(jnp.float32)
    grad_main, grad_small = spectra(low, marks, *transforms)
    real, imag, top = times(value_main, grad_main, True)
    scale = bin_scale(length)
    taps = from_bins((real * scale, imag * scale, top * (0.5 / length)), cos_main, sin_main)
    scale = bin_scale(region)
    real, imag, top = (
        sum(part[:, d * channels : (d + 1) * channels] for d in range(SLOTS))
        for part in times(value_small, grad_small, True)
    )
    taps_small = from_bins((real * scale, imag * scale, top * (0.5 / region)), cos_small, sin_small)
    grad_taps[:region] = taps[:region] + taps_small
    grad_taps[region:] = taps[region:]
    scatter.follow()
    down_row.plane()
    wait_all(loads[3:])
    result = filtered(
        grad_main,
        grad_small,
        (main_re[...], main_im[...], main_top[...]),
        (small_re[...], small_im[...], small_top[...]),
        marks,
        transforms,
        True,
    )
    grad_product = result + grad_summed * skip[...]
    parts = (grad * summed[...], grad_product * values, grad_product * gate_in)
    for k, part in enumerate(parts):
        lanes = slice(k * channels, (k + 1) * channels)
        source = projected[:, lanes]
        row = places.short_bias + k
        channel_sums[row : row + 1] = column_sum(part)
        row = places.short + k
        channel_sums[row : row + 1] = column_sum(part * source)
        running = short[0, k : k + 1] * part
        for lag in (1, 2):
            kept = jnp.where(marks[:, lag : lag + 1] > 0, part, 0.0)
            row = places.short + 3 * lag + k
            channel_sums[row : row + 1] = column_sum(kept * pltpu.roll(source, lag, 0))
            running = running + short[lag, k : k + 1] * pltpu.roll(kept, length - lag, 0)
        row = places.proj_bias + k
        channel_sums[row : row + 1] = column_sum(running)
        grad_low[:, lanes] = running.astype(jnp.bfloat16)
    up_row.finish()
    up_all.plane()
    out_row.cross()
    for block in range(count):
        rows = slice(block * shard, (block + 1) * shard)
        total = dot_nt(grad_low[rows, :channels], proj[0])
        for k in (1, 2):
            total = total + dot_nt(grad_low[rows, k * channels : (k + 1) * channels], proj[k])
        grad_first[block] = total.astype(jnp.bfloat16)
    filter_back(
        grad_taps,
        features,
        embed,
        [to_column(freq[i : i + 1]) for i in range(3)],
        inner,
        filter_weight,
        decay,
        pre,
        filter_sums,
        channel_sums,
    )
    up_all.pair()
    for weight in (down_row, out_row):
        weight.finish()
    scatter.finish(mlp_sum)
    up_all.finish()


def final_kernel(
    grad_first,
    tokens,
    gain,
    shift,
    out_bias_sum,
    gain_sum,
    shift_sum,
    down_bias_sum,
    filter_sums,
    channel_sums,
    up_bias_sum,
    down_part,
    out_part,
    first_hbm,
    grad_low_hbm,
    grad_tokens,
    proj_sum,
    down_sum,
    out_sum,
    line_all,
    filter_all,
    channel_all,
    up_bias_all,
    first,
    grad_low,
    proj_grad,
    proj_part,
    lines,
    load_sems,
    grad_own,
    *scratch,
):
    count = lax.axis_size("tensor")
    loads = staged([(first_hbm, first), (grad_low_hbm, grad_low)], load_sems)
    greet(tensor_devices() + [sibling()] + chip_devices())
    scatter = Scatter(grad_first, scratch[:5])
    scatter.start()
    scratch = scratch[5:]
    row = RowReduce(proj_grad, proj_part, scratch[:6])
    proj_all = RowGather(proj_part, proj_sum, scratch[6:9])
    gathers = (
        RowGather(down_part, down_sum, scratch[9:12]),
        RowGather(out_part, out_sum, scratch[12:15]),
    )
    small = SmallSums(
        (lines, filter_sums, channel_sums, up_bias_sum),
        (line_all, filter_all, channel_all, up_bias_all),
        2,
        scratch[15:],
    )
    length, columns = grad_low.shape
    channels = columns // 3
    width = tokens.shape[1]
    wait_all(loads)
    for k in range(3):
        proj_grad[k * width : (k + 1) * width] = dot_tn(
            first[...].reshape(length, width), grad_low[:, k * channels : (k + 1) * channels]
        ).astype(jnp.bfloat16)
    row.pair()
    row.plane()
    scatter.follow()
    plain = jnp.zeros_like(gain[...])
    scaled = jnp.zeros_like(gain[...])
    for block in range(count):
        grad = grad_first[block].astype(jnp.float32)
        plain = plain + column_sum(grad)
        scaled = scaled + column_sum(grad * first[block].astype(jnp.float32))
    lines[0:1] = out_bias_sum[...]
    lines[1:2] = gain_sum[...]
    lines[2:3] = shift_sum[...]
    lines[3:4] = down_bias_sum[...]
    lines[4:5] = (scaled - shift[...] * plain) / gain[...]
    lines[5:6] = plain
    lines[6:8] = jnp.zeros_like(lines[6:8])
    small.pair()
    hat, rate = normalised(tokens[...].astype(jnp.float32))
    small.plane()
    row.finish()
    proj_all.plane()
    for gather in gathers:
        gather.plane()
    small.tensor()
    proj_all.pair()
    for gather in gathers:
        gather.pair()
    small.finish()
    scatter.finish(grad_own)
    grad_tokens[...] = norm_back(grad_own[...], gain[...], hat, rate)
    for gather in gathers + (proj_all,):
        gather.finish()


def finish_kernel(
    residual,
    mlp_sum,
    down_bias,
    grad_tokens,
    grad_residual,
    proj_sum,
    up_sum,
    down_sum,
    out_sum,
    line_all,
    filter_all,
    channel_all,
    up_bias_all,
    layer_out,
    tokens_out,
    proj_out,
    up_out,
    down_out,
    out_out,
    out_bias_out,
    gain2_out,
    shift2_out,
    down_bias_out,
    gain1_out,
    shift1_out,
    embed_out,
    embed_bias_out,
    freq_out,
    inner_out,
    inner_bias_out,
    filter_out,
    short_out,
    short_bias_out,
    proj_bias_out,
    skip_out,
    up_bias_out,
):
    layer_out[...] = (residual[...] + mlp_sum[...] + down_bias[...]).astype(layer_out.dtype)
    tokens_out[...] = grad_tokens[...] + grad_residual[...]
    for source, target in (
        (proj_sum, proj_out),
        (up_sum, up_out),
        (down_sum, down_out),
        (out_sum, out_out),
    ):
        target[...] = source[...].astype(jnp.float32)

    @pl.when(pl.program_id(0) == 0)
    def _():
        lines = (out_bias_out, gain2_out, shift2_out, down_bias_out, gain1_out, shift1_out)
        for i, line in enumerate(lines):
            line[...] = line_all[i : i + 1]
        width = filter_out.shape[0]
        rows = filter_rows(width)
        for i in range(2):
            inner_out[i] = filter_all[:width, i * width : (i + 1) * width]
        embed_out[...] = filter_all[rows.embed : rows.embed + FEAT, :width]
        embed_bias_out[...] = filter_all[rows.embed_bias : rows.embed_bias + 1, :width]
        freq_out[...] = filter_all[rows.freq : rows.freq + 3, :width]
        inner_bias_out[...] = filter_all[rows.inner_bias : rows.inner_bias + 2, :width]
        rows = channel_rows(width)
        filter_out[...] = channel_all[:width]
        for lag in range(3):
            row = rows.short + 3 * lag
            short_out[lag] = channel_all[row : row + 3]
        short_bias_out[...] = channel_all[rows.short_bias : rows.short_bias + 3]
        proj_bias_out[...] = channel_all[rows.proj_bias : rows.proj_bias + 3]
        skip_out[...] = channel_all[rows.skip : rows.skip + 1]
        up_bias_out[...] = up_bias_all[...]


def finish(big, shapes):
    steps = 4

    def rows(shape):
        return pl.BlockSpec((shape[0] // steps, shape[1]), lambda i: (i, 0))

    def whole(shape):
        return pl.BlockSpec(tuple(shape), lambda i: (0,) * len(shape))

    in_specs = [
        whole(array.shape) if i == 2 or i > 8 else rows(array.shape) for i, array in enumerate(big)
    ]
    out_specs = [rows(shape.shape) if i < 6 else whole(shape.shape) for i, shape in enumerate(shapes)]
    return pl.pallas_call(
        finish_kernel,
        grid=(steps,),
        in_specs=in_specs,
        out_specs=out_specs,
        out_shape=shapes,
        compiler_params=pltpu.CompilerParams(
            dimension_semantics=("arbitrary",), vmem_limit_bytes=60 * 1024 * 1024
        ),
        name="finish",
    )(*big)


def communicate(kernel, shapes, operands, anywhere, scratch, channel, name, limit=60):
    vmem = pl.BlockSpec(memory_space=pltpu.VMEM)
    free = pl.BlockSpec(memory_space=pl.ANY)
    return pl.pallas_call(
        kernel,
        out_shape=shapes,
        in_specs=[free if i in anywhere[0] else vmem for i in range(len(operands))],
        out_specs=[free if i in anywhere[1] else vmem for i in range(len(shapes))],
        scratch_shapes=scratch,
        compiler_params=pltpu.CompilerParams(
            collective_id=channel, has_side_effects=True, vmem_limit_bytes=limit * 1024 * 1024
        ),
        cost_estimate=pl.CostEstimate(flops=0, bytes_accessed=200_000_000, transcendentals=0),
        name=name,
    )(*operands)


def body(
    tokens,
    segment_ids,
    norm1_gain,
    norm1_bias,
    proj_weight,
    proj_bias,
    short_weight,
    short_bias,
    embed_weight,
    embed_bias,
    sine_freq,
    inner_weight,
    inner_bias,
    filter_weight,
    decay_rate,
    skip_gain,
    out_weight,
    out_bias,
    norm2_gain,
    norm2_bias,
    up_weight,
    up_bias,
    down_weight,
    down_bias,
    cotangent,
):
    row_count, shard_len, model_width = tokens.shape
    groups = lax.axis_size("tensor")
    rows = lax.axis_size("dp")
    place = lax.axis_index("tensor")
    row_place = lax.axis_index("dp")
    length = shard_len * groups
    channels = proj_weight.shape[2]
    units = up_weight.shape[1]
    channel_slice = channels // rows

    out_part = lax.dynamic_slice_in_dim(out_weight, row_place * channel_slice, channel_slice, 0)
    out_rows = -(-channel_slice // 16) * 16
    out_part = jnp.pad(out_part, ((0, out_rows - channel_slice), (0, 0)))

    low = jnp.bfloat16
    region = shard_len
    chips = rows // 2
    proj_columns = 3 * channels
    cos_main, sin_main = transform(length)
    cos_small, sin_small = transform(region)
    features = features_by_row()
    decay = decay_rate[None]
    width = embed_weight.shape[1]
    embed_bias = embed_bias[None]
    proj = proj_weight.transpose(1, 0, 2)
    skip = skip_gain[None]
    semaphores = pltpu.SemaphoreType.DMA
    vmem = pltpu.VMEM
    single = jnp.float32
    blocked = (groups, shard_len, model_width)
    swapped = (groups, shard_len, channels)
    line = (1, model_width)
    (
        first_all,
        unused_parts,
        all_cotangent,
        pre,
        main_re,
        main_im,
        main_top,
        small_re,
        small_im,
        small_top,
        gated_own,
        projected,
        mixed,
        summed,
        out_all,
        residual,
        second,
    ) = communicate(
        front_kernel,
        [
            shaped(blocked, low),
            shaped((groups, chips, 2) + out_part.shape, low),
            shaped(blocked, low),
            shaped((3, width, length)),
            shaped((length, channels)),
            shaped((length, channels)),
            shaped((1, channels)),
            shaped((region, channels)),
            shaped((region, channels)),
            shaped((1, channels)),
            shaped(swapped, low),
            shaped((length, proj_columns)),
            shaped((length, proj_columns)),
            shaped((length, channels)),
            shaped((groups, channels, model_width), low),
            shaped((shard_len, model_width)),
            shaped((shard_len, model_width), low),
        ],
        [
            tokens[0],
            norm1_gain[None],
            norm1_bias[None],
            out_part,
            cotangent[0],
            segment_ids,
            embed_weight,
            embed_bias,
            sine_freq,
            inner_weight,
            inner_bias,
            filter_weight,
            decay,
            proj_bias,
            short_weight,
            short_bias,
            skip,
            features,
            proj,
            cos_main,
            sin_main,
            cos_small,
            sin_small,
            out_bias[None],
            norm2_gain[None],
            norm2_bias[None],
        ],
        ((3, 17, 18, 19, 20), (0, 1, 2, 3, 4, 5, 11, 12, 13)),
        [
            vmem(features.shape, single),
            vmem(proj.shape, low),
            vmem(cos_main.shape, low),
            vmem(sin_main.shape, low),
            vmem(blocked, low),
            vmem(blocked, low),
            vmem((3, width, length), single),
            vmem((length, channels), single),
            vmem((length, channels), single),
            vmem((length, proj_columns), single),
            vmem((length, proj_columns), single),
            vmem((length, channels), single),
            vmem(swapped, low),
            vmem((groups, chips, 2) + out_part.shape, low),
            vmem((length, 8), jnp.int32),
            semaphores((4,)),
            semaphores((8,)),
            semaphores((1,)),
            *chain_scratch(groups),
            *chain_scratch(groups),
            semaphores((2, groups - 1)),
            semaphores((2, chips - 1)),
            semaphores((2, 1)),
            semaphores((2, groups - 1)),
        ],
        0,
        "front",
    )
    (
        grad_residual,
        mlp_partial,
        up_grad,
        down_grad,
        grad_up_bias,
        grad_gated,
        out_grad,
        grad_norm2_gain,
        grad_norm2_bias,
        grad_out_bias,
        grad_down_bias,
    ) = communicate(
        middle_kernel,
        [
            shaped((shard_len, model_width)),
            shaped(blocked, low),
            shaped((model_width, units), low),
            shaped((units, model_width), low),
            shaped((1, units)),
            shaped(swapped, low),
            shaped((groups, channels, model_width), low),
            shaped(line),
            shaped(line),
            shaped(line),
            shaped(line),
        ],
        [
            second,
            norm2_gain[None],
            up_bias[None],
            all_cotangent,
            up_weight,
            down_weight,
            residual,
            gated_own,
            out_all,
        ],
        ((3, 4, 5, 6, 7, 8), (1, 2, 3)),
        [
            vmem(blocked, low),
            vmem((model_width, units), low),
            vmem((units, model_width), low),
            vmem((shard_len, model_width), single),
            vmem(swapped, low),
            vmem((groups, channels, model_width), low),
            vmem(blocked, low),
            vmem((model_width, units), low),
            vmem((units, model_width), low),
            vmem(blocked, low),
            vmem((groups, shard_len, units), low),
            vmem((groups, shard_len, units), low),
            vmem(blocked, low),
            vmem(blocked, low),
            vmem((shard_len, model_width), single),
            semaphores((6,)),
            semaphores((3,)),
            *chain_scratch(groups),
            semaphores((groups,)),
            semaphores((groups,)),
        ],
        1,
        "middle",
    )
    fold = max(1, 32 * chips // channels)
    out_grad = out_grad.reshape(groups, channels * fold, model_width // fold)
    out_size = (channels * fold // rows, model_width // fold)
    filter_shape = (filter_rows(width).size, 2 * width)
    channel_shape = (channel_rows(width).size, channels)
    (
        grad_first,
        grad_low,
        mlp_out,
        up_sum,
        down_part,
        out_part,
        filter_sums,
        channel_sums,
    ) = communicate(
        back_kernel,
        [
            shaped(blocked, low),
            shaped((length, proj_columns), low),
            shaped((shard_len, model_width)),
            shaped(up_grad.shape, low),
            shaped((units // rows, model_width), low),
            shaped(out_size, low),
            shaped(filter_shape),
            shaped(channel_shape),
        ],
        [
            grad_gated,
            mlp_partial,
            up_grad,
            down_grad,
            out_grad,
            short_weight,
            skip,
            segment_ids,
            embed_weight,
            sine_freq,
            inner_weight,
            filter_weight,
            decay,
            main_top,
            small_re,
            small_im,
            small_top,
            cos_small,
            sin_small,
            mixed,
            cos_main,
            sin_main,
            main_re,
            main_im,
            summed,
            projected,
            proj,
            features,
            pre,
        ],
        ((0, 1, 2, 3, 4, 19, 20, 21, 22, 23, 24, 25, 26, 27, 28), (3,)),
        [
            vmem((length, proj_columns), single),
            vmem(cos_main.shape, low),
            vmem(sin_main.shape, low),
            vmem((length, channels), single),
            vmem((length, channels), single),
            vmem((length, channels), single),
            vmem((length, proj_columns), single),
            vmem(proj.shape, low),
            vmem(features.shape, single),
            vmem(pre.shape, single),
            vmem(swapped, low),
            vmem((length, channels), single),
            vmem((length, 8), jnp.int32),
            vmem(blocked, low),
            vmem((model_width // rows, units), low),
            semaphores((10,)),
            semaphores((2,)),
            semaphores((2, groups - 1)),
        ]
        + row_reduce_scratch(up_grad.shape, chips)
        + row_reduce_scratch(down_grad.shape, chips)
        + row_reduce_scratch(out_grad.shape, chips)
        + row_gather_scratch(chips)
        + scatter_scratch(blocked),
        2,
        "back",
        63,
    )
    (
        grad_tokens,
        proj_sum,
        down_sum,
        out_sum,
        line_all,
        filter_all,
        channel_all,
        up_bias_all,
    ) = communicate(
        final_kernel,
        [
            shaped((shard_len, model_width)),
            shaped((3 * model_width, channels), low),
            shaped(down_grad.shape, low),
            shaped(out_grad.shape[1:], low),
            shaped((8, model_width)),
            shaped(filter_shape),
            shaped(channel_shape),
            shaped(grad_up_bias.shape),
        ],
        [
            grad_first,
            tokens[0],
            norm1_gain[None],
            norm1_bias[None],
            grad_out_bias,
            grad_norm2_gain,
            grad_norm2_bias,
            grad_down_bias,
            filter_sums,
            channel_sums,
            grad_up_bias,
            down_part,
            out_part,
            first_all,
            grad_low,
        ],
        ((13, 14), (1, 2, 3)),
        [
            vmem(blocked, low),
            vmem((length, proj_columns), low),
            vmem((3 * model_width, channels), low),
            vmem((3 * model_width // rows, channels), low),
            vmem((8, model_width), single),
            semaphores((2,)),
            vmem((shard_len, model_width), single),
        ]
        + scatter_scratch(blocked)
        + row_reduce_scratch((3 * model_width, channels), chips)
        + row_gather_scratch(chips) * 3
        + small_sums_scratch(
            [(8, model_width), filter_shape, channel_shape, grad_up_bias.shape], 2, chips, groups
        ),
        3,
        "final",
    )
    (
        layer_out,
        grad_tokens,
        grad_proj_weight,
        grad_up_weight,
        grad_down_weight,
        grad_out_weight,
        grad_out_bias,
        grad_norm2_gain,
        grad_norm2_bias,
        grad_down_bias,
        grad_norm1_gain,
        grad_norm1_bias,
        grad_embed_weight,
        grad_embed_bias,
        grad_sine_freq,
        grad_inner_weight,
        grad_inner_bias,
        grad_filter_weight,
        grad_short_weight,
        grad_short_bias,
        grad_proj_bias,
        grad_skip_gain,
        grad_up_bias,
    ) = finish(
        [
            residual,
            mlp_out,
            down_bias[None],
            grad_tokens,
            grad_residual,
            proj_sum,
            up_sum,
            down_sum,
            out_sum.reshape(out_weight.shape),
            line_all,
            filter_all,
            channel_all,
            up_bias_all,
        ],
        [
            shaped((shard_len, model_width), low),
            shaped((shard_len, model_width)),
            shaped((3 * model_width, channels)),
            shaped(up_weight.shape),
            shaped(down_weight.shape),
            shaped(out_weight.shape),
            shaped(line),
            shaped(line),
            shaped(line),
            shaped(line),
            shaped(line),
            shaped(line),
            shaped(embed_weight.shape),
            shaped(embed_bias.shape),
            shaped(sine_freq.shape),
            shaped(inner_weight.shape),
            shaped(inner_bias.shape),
            shaped(filter_weight.shape),
            shaped(short_weight.shape),
            shaped(short_bias.shape),
            shaped(proj_bias.shape),
            shaped(skip.shape),
            shaped(up_bias_all.shape),
        ],
    )
    grad_proj_weight = grad_proj_weight.reshape(3, model_width, channels).transpose(1, 0, 2)
    return (
        layer_out[None],
        grad_tokens[None],
        grad_norm1_gain[0],
        grad_norm1_bias[0],
        grad_proj_weight,
        grad_proj_bias,
        grad_short_weight,
        grad_short_bias,
        grad_embed_weight,
        grad_embed_bias[0],
        grad_sine_freq,
        grad_inner_weight,
        grad_inner_bias,
        grad_filter_weight,
        grad_skip_gain[0],
        grad_out_weight,
        grad_out_bias[0],
        grad_norm2_gain[0],
        grad_norm2_bias[0],
        grad_up_weight,
        grad_up_bias[0],
        grad_down_weight,
        grad_down_bias[0],
    )


def solution(mesh):
    return jax.shard_map(
        body,
        mesh=mesh,
        in_specs=(
            P("dp", "tensor", None),
            P("dp", None),
            P(),
            P(),
            P(None, None, "tensor"),
            P(None, "tensor"),
            P(None, None, "tensor"),
            P(None, "tensor"),
            P(),
            P(),
            P(),
            P(),
            P(),
            P(None, "tensor"),
            P("tensor"),
            P("tensor"),
            P("tensor", None),
            P(),
            P(),
            P(),
            P(None, "tensor"),
            P("tensor"),
            P("tensor", None),
            P(),
            P("dp", "tensor", None),
        ),
        out_specs=(
            P("dp", "tensor", None),
            P("dp", "tensor", None),
            P(),
            P(),
            P(None, None, "tensor"),
            P(None, "tensor"),
            P(None, None, "tensor"),
            P(None, "tensor"),
            P(),
            P(),
            P(),
            P(),
            P(),
            P(None, "tensor"),
            P("tensor"),
            P("tensor", None),
            P(),
            P(),
            P(),
            P(None, "tensor"),
            P("tensor"),
            P("tensor", None),
            P(),
        ),
        check_vma=False,
    )
```
